128 devices in a mesh: dp: 16 (over x, z), mp: 8 (over y, core).
Axes of the slice: x: 4, y: 4, z: 4, core: 2. Of those that a mesh axis runs over, the one named last changes fastest.
Arguments:
- tokens: bfloat16 [16, 512, 1536], P('dp'), may hold values from -6 to 6
- lengths: int32 [16], P('dp'), may hold values from 1 to 512, as said below
- cotangent: bfloat16 [16, 512, 1536], P('dp'), may hold values from -6 to 6
- joint_weight: float32 [1536, 2048], P('dp', 'mp'), may hold values from -0.15625 to 0.15625
- joint_moment: float32 [1536, 2048], P('dp', 'mp')
- joint_square: float32 [1536, 2048], P('dp', 'mp')
- mixer_weight: float32 [1536, 1536], P('dp', 'mp'), may hold values from -0.875 to 0.875
- mixer_moment: float32 [1536, 1536], P('dp', 'mp')
- mixer_square: float32 [1536, 1536], P('dp', 'mp')
- expand_weight: float32 [2, 1536, 8960], P(None, 'dp', 'mp')
- expand_moment: float32 [2, 1536, 8960], P(None, 'dp', 'mp')
- expand_square: float32 [2, 1536, 8960], P(None, 'dp', 'mp')
- shrink_weight: float32 [8960, 1536], P('mp', 'dp')
- shrink_moment: float32 [8960, 1536], P('mp', 'dp')
- shrink_square: float32 [8960, 1536], P('mp', 'dp')
- vector_params: float32 [5120], P(('dp', 'mp'))
- vector_moment: float32 [5120], P(('dp', 'mp'))
- vector_square: float32 [5120], P(('dp', 'mp'))
Outputs:
- output: float32 [16, 512, 1536], P('dp')
- input_grad: float32 [16, 512, 1536], P('dp')
- grad_norm: float32 [], replicated
- joint_next: float32 [1536, 2048], P('dp', 'mp')
- joint_moment_next: float32 [1536, 2048], P('dp', 'mp')
- joint_square_next: float32 [1536, 2048], P('dp', 'mp')
- mixer_next: float32 [1536, 1536], P('dp', 'mp')
- mixer_moment_next: float32 [1536, 1536], P('dp', 'mp')
- mixer_square_next: float32 [1536, 1536], P('dp', 'mp')
- expand_next: float32 [2, 1536, 8960], P(None, 'dp', 'mp')
- expand_moment_next: float32 [2, 1536, 8960], P(None, 'dp', 'mp')
- expand_square_next: float32 [2, 1536, 8960], P(None, 'dp', 'mp')
- shrink_next: float32 [8960, 1536], P('mp', 'dp')
- shrink_moment_next: float32 [8960, 1536], P('mp', 'dp')
- shrink_square_next: float32 [8960, 1536], P('mp', 'dp')
- vector_next: float32 [5120], P(('dp', 'mp'))
- vector_moment_next: float32 [5120], P(('dp', 'mp'))
- vector_square_next: float32 [5120], P(('dp', 'mp'))
The draws below stay inside these ranges and needn't reach their ends.
Inputs may be any that keep to these rules, and one draw needn't show every extreme that they name: `lengths`: valid positions of each row, counted from its start; some row is full.
All inputs are finite; a program needn't handle non-finite values.
Results may differ from the reference program's by a relative error of at most 0.02.
Values may be sent and summed in bfloat16 or wider, within the bound.
No kernel may reach another device: no remote copies, remote signals or barrier semaphores. Data moves between devices by JAX's collectives and lax.ppermute only.
A program may use at most 192 MiB of HBM per device.

```python
import math
import jax
import jax.numpy as jnp
from jax import lax

D = 1536
QUERY_HEADS = 12
KEY_VALUE_HEADS = 2
HEAD_SIZE = 128
FF = 8960
ROW_LENGTH = 512
STEP = 5
ROWS = 16
ATT = 1536
QKV = 2048
VEC = 5120
NPARAMS = 46797824


def ramp(count, start_value, end_value):
    return start_value + (end_value - start_value) * jnp.arange(count, dtype=jnp.float32) / max(count - 1, 1)


def first_moment(key, shape, boost):
    size = boost / math.sqrt(NPARAMS)
    return jax.random.normal(key, shape, jnp.float32) * (size * 0.1 / 0.9)


def second_moment(key, shape, boost):
    size = boost / math.sqrt(NPARAMS)
    factor = jnp.exp(jax.random.uniform(key, shape, jnp.float32, 0.0, math.log(4.0)))
    return factor * (size * size * 0.05 / 0.95)


def draw_lengths(key, part):
    key = jax.random.fold_in(key, 5)
    key_jitter, key_pick = jax.random.split(key)
    index = jnp.arange(ROWS, dtype=jnp.int32)
    base = ROW_LENGTH * (3 * (ROWS - 1) + 7 * index) // (10 * (ROWS - 1))
    spread = max(ROW_LENGTH // 16, 1)
    jitter = jax.random.randint(key_jitter, (ROWS,), -spread, spread + 1)
    value_rows = jnp.clip(base + jitter, 1, ROW_LENGTH)
    pick = jax.random.randint(key_pick, (), ROWS // 2, ROWS)
    return jnp.where(index == pick, ROW_LENGTH, value_rows).astype(jnp.int32)


def draw_expand_weight(key, part):
    key = jax.random.fold_in(key, 31)
    key_gate, key_up = jax.random.split(key)
    gate = jax.random.normal(key_gate, (D, FF), jnp.float32)
    upper = jax.random.normal(key_up, (D, FF), jnp.float32)
    rise = ramp(FF, 0.6, 1.8)
    return jnp.stack([gate, upper * rise[None, :]]) / math.sqrt(D)


def draw_shrink_weight(key, part):
    key = jax.random.fold_in(key, 37)
    base = jax.random.normal(key, (FF, D), jnp.float32)
    rise = ramp(FF, 0.6, 1.8)
    return base * rise[:, None] / math.sqrt(FF)


def draw_vector_params(key, part):
    key = jax.random.fold_in(key, 41)
    key_gain, key_bias = jax.random.split(key)
    noise = 0.1 * jax.random.normal(key_gain, (2, D), jnp.float32)
    rise = ramp(D, 0.6, 1.8)
    gains = (1.0 + noise) * rise[None, :]
    bias = 0.3 * jax.random.normal(key_bias, (QKV,), jnp.float32)
    return jnp.concatenate([gains.reshape(2 * D), bias])


def draw_joint_moment(key, part):
    key = jax.random.fold_in(key, 51)
    return first_moment(key, (D, QKV), 1.0)


def draw_joint_square(key, part):
    key = jax.random.fold_in(key, 52)
    return second_moment(key, (D, QKV), 1.0)


def draw_mixer_moment(key, part):
    key = jax.random.fold_in(key, 53)
    return first_moment(key, (ATT, D), 1.0)


def draw_mixer_square(key, part):
    key = jax.random.fold_in(key, 54)
    return second_moment(key, (ATT, D), 1.0)


def draw_expand_moment(key, part):
    key = jax.random.fold_in(key, 55)
    return first_moment(key, (2, D, FF), 1.0)


def draw_expand_square(key, part):
    key = jax.random.fold_in(key, 56)
    return second_moment(key, (2, D, FF), 1.0)


def draw_shrink_moment(key, part):
    key = jax.random.fold_in(key, 57)
    return first_moment(key, (FF, D), 1.0)


def draw_shrink_square(key, part):
    key = jax.random.fold_in(key, 58)
    return second_moment(key, (FF, D), 1.0)


def draw_vector_moment(key, part):
    key = jax.random.fold_in(key, 59)
    return first_moment(key, (VEC,), 3.0)


def draw_vector_square(key, part):
    key = jax.random.fold_in(key, 60)
    return second_moment(key, (VEC,), 3.0)


def levels(rng, shape, shards, least, top_value):
    def one(axis_at, blocks):
        heights = jax.random.uniform(jax.random.fold_in(jax.random.fold_in(rng, 6), axis_at), (blocks,), jnp.float32, least / len(shards), top_value / len(shards))
        return jnp.repeat(jnp.exp(heights), shape[axis_at] // blocks).reshape((-1,) + (1,) * (len(shape) - axis_at - 1))

    level = one(*shards[0])
    for cut in shards[1:]:
        level = level * one(*cut)
    return level


def gaussian(rng, extent, scale, most, pieces=(), kind=jnp.bfloat16):
    entries = scale * jax.random.normal(rng, extent, jnp.float32)
    if pieces:
        entries = entries * levels(rng, extent, pieces, -0.22, 0.18)
    return jnp.clip(entries, -most, most).astype(kind)


def setup_inputs(seed: int = 0) -> dict:
    splits = jax.random.split(jax.random.key(seed), 19)
    return {
        "tokens": gaussian(splits[0], (ROWS, ROW_LENGTH, D), 1.0, 6.0, ((0, 16),)),
        "lengths": draw_lengths(jax.random.fold_in(splits[18], 71), 0),
        "cotangent": gaussian(splits[2], (ROWS, ROW_LENGTH, D), 1.0, 6.0, ((0, 16),)),
        "joint_weight": gaussian(splits[3], (D, QKV), D ** -0.5, 0.15625, ((0, 16), (1, 8)), jnp.float32),
        "joint_moment": draw_joint_moment(jax.random.fold_in(splits[18], 71), 0),
        "joint_square": draw_joint_square(jax.random.fold_in(splits[18], 71), 0),
        "mixer_weight": gaussian(splits[6], (ATT, D), (max(ATT * 16 // ROW_LENGTH, 1)) ** -0.5, 0.875, ((0, 16), (1, 8)), jnp.float32),
        "mixer_moment": draw_mixer_moment(jax.random.fold_in(splits[18], 71), 0),
        "mixer_square": draw_mixer_square(jax.random.fold_in(splits[18], 71), 0),
        "expand_weight": draw_expand_weight(jax.random.fold_in(splits[18], 71), 0),
        "expand_moment": draw_expand_moment(jax.random.fold_in(splits[18], 71), 0),
        "expand_square": draw_expand_square(jax.random.fold_in(splits[18], 71), 0),
        "shrink_weight": draw_shrink_weight(jax.random.fold_in(splits[18], 71), 0),
        "shrink_moment": draw_shrink_moment(jax.random.fold_in(splits[18], 71), 0),
        "shrink_square": draw_shrink_square(jax.random.fold_in(splits[18], 71), 0),
        "vector_params": draw_vector_params(jax.random.fold_in(splits[18], 71), 0),
        "vector_moment": draw_vector_moment(jax.random.fold_in(splits[18], 71), 0),
        "vector_square": draw_vector_square(jax.random.fold_in(splits[18], 71), 0),
    }


@jax.custom_vjp
def reduced_input(v):
    return lax.optimization_barrier(v.astype(jnp.bfloat16)).astype(jnp.float32)

@jax.custom_vjp
def low_back(v):
    return v

def low_keep(v):
    return (reduced_input(v), None)

def low_pass(kept, grad):
    return (grad,)

def back_keep(v):
    return (v, None)

def back_low(kept, grad):
    return (reduced_input(grad),)
reduced_input.defvjp(low_keep, low_pass)
low_back.defvjp(back_keep, back_low)
EPS_NORM = 1e-06
ROPE_BASE = 1000000.0
MAX_NORM = 1.0
BETA_ONE = 0.9
BETA_TWO = 0.95
ADAM_EPS = 1e-08
DECAY = 0.1
RATE_MATRIX = 0.06
RATE_VECTOR = 0.8
MASKED = -1e+30

def product(left, right):
    return jnp.dot(left, right, precision=lax.Precision.HIGHEST, preferred_element_type=jnp.float32)

def tables(length_all, head):
    places = jnp.arange(length_all, dtype=jnp.float32)
    freq = ROPE_BASE ** (-jnp.arange(0, head, 2, dtype=jnp.float32) / head)
    angle = places[:, None] * freq[None, :]
    cosine_table = jnp.concatenate([jnp.cos(angle), jnp.cos(angle)], -1)
    sine_table = jnp.concatenate([jnp.sin(angle), jnp.sin(angle)], -1)
    return (cosine_table, sine_table)

def apply_rotary(value_rows, cosine_table, sine_table):
    half = value_rows.shape[-1] // 2
    turned = jnp.concatenate([-value_rows[..., half:], value_rows[..., :half]], -1)
    return value_rows * cosine_table[:, None, :] + turned * sine_table[:, None, :]

def row_forward(xrow, length, joint_input, mixer, gate_w, up_w, shrink, gain_first, gain_second, bias):
    attention_width = QUERY_HEADS * HEAD_SIZE
    key_value_width = KEY_VALUE_HEADS * HEAD_SIZE
    query_group = QUERY_HEADS // KEY_VALUE_HEADS
    cosine_table, sine_table = tables(ROW_LENGTH, HEAD_SIZE)
    scale_first = lax.rsqrt(lax.optimization_barrier(jnp.mean(xrow * xrow, -1, keepdims=True)) + EPS_NORM)
    normed = reduced_input(xrow * scale_first * gain_first)
    mixed_output = low_back(product(normed, joint_input) + bias)
    query_rows = reduced_input(apply_rotary(mixed_output[:, :attention_width].reshape(ROW_LENGTH, QUERY_HEADS, HEAD_SIZE), cosine_table, sine_table)).reshape(ROW_LENGTH, KEY_VALUE_HEADS, query_group, HEAD_SIZE)
    key_rows = reduced_input(apply_rotary(mixed_output[:, attention_width:attention_width + key_value_width].reshape(ROW_LENGTH, KEY_VALUE_HEADS, HEAD_SIZE), cosine_table, sine_table))
    value_rows = reduced_input(mixed_output[:, attention_width + key_value_width:].reshape(ROW_LENGTH, KEY_VALUE_HEADS, HEAD_SIZE))
    scores = low_back(jnp.einsum('qhgd,khd->hgqk', query_rows, key_rows, precision=lax.Precision.HIGHEST) * HEAD_SIZE ** (-0.5))
    places = jnp.arange(ROW_LENGTH)
    allowed = (places[:, None] >= places[None, :]) & (places[None, :] < length)
    scores = jnp.where(allowed, scores, MASKED)
    top = lax.optimization_barrier(jnp.max(scores, -1, keepdims=True))
    expo = jnp.exp(scores - top)
    probs = reduced_input(expo / lax.optimization_barrier(jnp.sum(expo, -1, keepdims=True)))
    attended = jnp.einsum('hgqk,khd->qhgd', probs, value_rows, precision=lax.Precision.HIGHEST).reshape(ROW_LENGTH, attention_width)
    attended = reduced_input(low_back(attended))
    hidden = xrow + low_back(product(attended, mixer))
    scale_second = lax.rsqrt(lax.optimization_barrier(jnp.mean(hidden * hidden, -1, keepdims=True)) + EPS_NORM)
    normed_second = reduced_input(hidden * scale_second * gain_second)
    gate = low_back(product(normed_second, gate_w))
    lifted = low_back(product(normed_second, up_w))
    active = reduced_input(jax.nn.silu(gate) * lifted)
    result = hidden + low_back(product(active, shrink))
    return jnp.where((places < length)[:, None], result, 0.0)

def adam_step(weight, grad, moment, square, rate, decay):
    moment_next = BETA_ONE * moment + (1.0 - BETA_ONE) * grad
    square_next = BETA_TWO * square + (1.0 - BETA_TWO) * grad * grad
    first_hat = moment_next / (1.0 - BETA_ONE ** STEP)
    second_hat = square_next / (1.0 - BETA_TWO ** STEP)
    weight_next = weight - rate * (first_hat / (jnp.sqrt(second_hat) + ADAM_EPS) + decay * weight)
    return (weight_next, moment_next, square_next)

def reference(tokens, lengths, cotangent, joint_weight, joint_moment, joint_square, mixer_weight, mixer_moment, mixer_square, expand_weight, expand_moment, expand_square, shrink_weight, shrink_moment, shrink_square, vector_params, vector_moment, vector_square):

    def forward(inputs, joint_input, mixer, expand, shrink, vector):
        joint_low = reduced_input(joint_input)
        mixer_low = reduced_input(mixer)
        expand_low = reduced_input(expand)
        shrink_low = reduced_input(shrink)
        gain_first = vector[:D]
        gain_second = vector[D:2 * D]
        bias = vector[2 * D:]

        def one_row(pair):
            return row_forward(pair[0], pair[1], joint_low, mixer_low, expand_low[0], expand_low[1], shrink_low, gain_first, gain_second, bias)
        return lax.map(jax.checkpoint(one_row), (inputs, lengths))
    output, pullback = jax.vjp(forward, tokens.astype(jnp.float32), joint_weight, mixer_weight, expand_weight, shrink_weight, vector_params)
    input_grad, joint_grad, mixer_grad, expand_grad, shrink_grad, vector_grad = pullback(cotangent.astype(jnp.float32))
    total = jnp.sum(joint_grad * joint_grad) + jnp.sum(mixer_grad * mixer_grad) + jnp.sum(expand_grad * expand_grad) + jnp.sum(shrink_grad * shrink_grad) + jnp.sum(vector_grad * vector_grad)
    grad_norm = jnp.sqrt(total)
    clip = jnp.minimum(1.0, MAX_NORM / (grad_norm + 1e-06))
    joint_next, joint_moment_next, joint_square_next = adam_step(joint_weight, clip * joint_grad, joint_moment, joint_square, RATE_MATRIX, DECAY)
    mixer_next, mixer_moment_next, mixer_square_next = adam_step(mixer_weight, clip * mixer_grad, mixer_moment, mixer_square, RATE_MATRIX, DECAY)
    expand_next, expand_moment_next, expand_square_next = adam_step(expand_weight, clip * expand_grad, expand_moment, expand_square, RATE_MATRIX, DECAY)
    shrink_next, shrink_moment_next, shrink_square_next = adam_step(shrink_weight, clip * shrink_grad, shrink_moment, shrink_square, RATE_MATRIX, DECAY)
    vector_next, vector_moment_next, vector_square_next = adam_step(vector_params, clip * vector_grad, vector_moment, vector_square, RATE_VECTOR, 0.0)
    return (output, input_grad, grad_norm, joint_next, joint_moment_next, joint_square_next, mixer_next, mixer_moment_next, mixer_square_next, expand_next, expand_moment_next, expand_square_next, shrink_next, shrink_moment_next, shrink_square_next, vector_next, vector_moment_next, vector_square_next)
```

```python
import jax
import jax.numpy as jnp
import numpy as np
from jax import lax
from jax.experimental import pallas as pl
from jax.experimental.pallas import tpu as pltpu
from jax.sharding import PartitionSpec as P

QUERY_HEADS = 12
KEY_VALUE_HEADS = 2
HEAD = 128
STEP = 5
EPS_NORM = 1e-06
ROPE_BASE = 1000000.0
MAX_NORM = 1.0
BETA_ONE = 0.9
BETA_TWO = 0.95
ADAM_EPS = 1e-08
DECAY = 0.1
RATE_MATRIX = 0.06
RATE_VECTOR = 0.8
MASKED = -1e30

T = 512
HALF = 256
PART = 64
D = 1536
FF = 1120
FP = 1152
DP = 16
MP = 8
ROWS = D // DP
JC = 256
MC = 192
KEY_AT = 6
SCALE = HEAD ** (-0.5)

f32 = jnp.float32
bf16 = jnp.bfloat16
VM = pl.BlockSpec(memory_space=pltpu.VMEM)
SM = pl.BlockSpec(memory_space=pltpu.SMEM)
MiB = 1 << 20
SMALL = pl.CostEstimate(flops=1, bytes_accessed=1, transcendentals=0)


def shift_y(v, k):
    return lax.ppermute(v, "mp", [(i, (i + 2 * k) % MP) for i in range(MP)])


def from_last_chip(v, k):
    return lax.ppermute(v, "mp", [(i, (i + 2 * k) % MP) for i in (MP - 2, MP - 1)])


def swap_core(v):
    return lax.ppermute(v, "mp", [(i, i ^ 1) for i in range(MP)])


def exchange(v, axis):
    return lax.all_to_all(v, axis, split_axis=0, concat_axis=0, tiled=True)


RELATIVE = (0, -1, 1, 2)


def gather(shift, v):
    return [v, shift(v, 1), shift(v, -1), shift(v, 2)]


def nn(a, b):
    return lax.dot_general(a, b, (((1,), (0,)), ((), ())), preferred_element_type=f32)


def nt(a, b):
    return lax.dot_general(a, b, (((1,), (1,)), ((), ())), preferred_element_type=f32)


def tn(a, b):
    return lax.dot_general(a, b, (((0,), (0,)), ((), ())), preferred_element_type=f32)


def whole(body, outs, args, scratch=(), limit=60, after=()):
    n = len(args)

    def bare(*refs):
        body(*refs[:n], *refs[n + len(after) :])

    return pl.pallas_call(
        bare,
        out_shape=[jax.ShapeDtypeStruct(s, d) for s, d in outs],
        in_specs=[SM] + [VM] * (n - 1) + [pl.BlockSpec(memory_space=pl.ANY)] * len(after),
        out_specs=[VM] * len(outs),
        scratch_shapes=list(scratch),
        compiler_params=pltpu.CompilerParams(vmem_limit_bytes=limit * MiB),
        cost_estimate=SMALL,
    )(*args, *after)


def at(start, size, step):
    return pl.ds(pl.multiple_of(start, step), size)


def prepare(ids, cotangent, tok, back, back_t, back_part, tok_part):
    length, y, c = ids[0], ids[3], ids[4]
    for h in range(2):
        start = HALF * ((c + h) % 2)
        t = lax.broadcasted_iota(jnp.int32, (HALF, 1), 0) + start
        v = cotangent[at(start, HALF, HALF), :]
        v = jnp.where(t < length, v, jnp.zeros_like(v))
        back[HALF * h : HALF * (h + 1), :] = v
        back_t[:, HALF * h : HALF * (h + 1)] = v.T
    back_part[...] = back[at(PART * y, PART, PART), :]
    tok_part[...] = tok[at(HALF * c + PART * y, PART, PART), :]


def kept(i, n, length):
    t = lax.broadcasted_iota(jnp.int32, (128, n), 0) + 128 * i
    s = lax.broadcasted_iota(jnp.int32, (128, n), 1)
    return (s <= t) & (s < length)


def attend(
    ids, tok, gain, bias, cosine, sine, query_w, pair_w,
    normed, heads, out, lse, w,
):
    w[:, :JC] = query_w[:, :ROWS, :].reshape(D, JC)
    w[:, JC:] = pair_w[:, :ROWS, :].reshape(D, JC)

    @pl.loop(0, T // 128)
    def _(i):
        rows = at(i * 128, 128, 128)
        x = tok[rows, :].astype(f32)
        s = lax.rsqrt(jnp.mean(x * x, -1, keepdims=True) + EPS_NORM)
        n = (x * s * gain[...]).astype(bf16)
        normed[rows, :] = n
        j = nn(n, w[...]) + bias[...]
        for h in range(4):
            cols = slice(HEAD * h, HEAD * (h + 1))
            u = j[:, cols]
            if h < 3:
                u = u * cosine[rows, :] + pltpu.roll(u, HEAD // 2, 1) * sine[rows, :]
            heads[rows, cols] = u.astype(bf16)

    for h in range(2):
        for i in range(4):
            n = 128 * (i + 1)
            q = heads[128 * i : n, HEAD * h : HEAD * (h + 1)]
            k, v = heads[:n, 2 * HEAD : 3 * HEAD], heads[:n, 3 * HEAD :]
            s = jnp.where(kept(i, n, ids[0]), nt(q, k) * SCALE, MASKED)
            m = jnp.max(s, -1, keepdims=True)
            e = jnp.exp(s - m)
            total = jnp.sum(e, -1, keepdims=True)
            o = nn((e / total).astype(bf16), v).astype(bf16)
            lse[128 * i : n, HEAD * h : HEAD * (h + 1)] = jnp.broadcast_to(
                m + jnp.log(total), (128, HEAD)
            )
            at_row = 128 * (i % 2)
            for y in range(4):
                out[2 * y + i // 2, at_row : at_row + 128, HEAD * h : HEAD * (h + 1)] = o


def mix(
    ids, att, a0, a1, a2, a3, b0, b1, b2, b3, tok, gain,
    hidden_part, normed, rows_w, hidden, side, mixer,
):
    y, c = ids[3], ids[4]
    for j in range(KEY_AT):
        side[:, JC * j : JC * (j + 1)] = att[j]
    mine = at(HALF * c, HALF, HALF)
    for e, a, b in zip(RELATIVE, (a0, a1, a2, a3), (b0, b1, b2, b3)):
        cols = at(384 * lax.rem(y + e + 4, 4), 384, 384)
        first = 384 * lax.rem(y + e + 4, 4)
        left, right = at(first, JC, 128), at(first + JC, HEAD, 128)
        for d in range(DP):
            for half, v in ((c, a), (1 - c, b)):
                row = ROWS * d + 48 * half
                mixer[at(row, 48, 16), left] = v[d, :48, :]
                mixer[at(row, 32, 16), right] = v[d, 48:80, :HEAD]
                mixer[at(row + 32, 16, 16), right] = v[d, 48:64, HEAD:]
        hidden[:, cols] = nn(side[...], mixer[:, cols]) + tok[mine, cols].astype(f32)
    hidden_part[...] = hidden[at(PART * y, PART, PART), :]
    rows_w[...] = mixer[at(JC * jnp.minimum(ids[2], KEY_AT - 1), JC, JC), :]
    for r in range(0, HALF, 64):
        v = hidden[r : r + 64, :]
        s = lax.rsqrt(jnp.mean(v * v, -1, keepdims=True) + EPS_NORM)
        normed[r : r + 64, :] = (v * s * gain[...]).astype(bf16)


def gated(near, far, back, back_t, w, act, gate_grad, up_grad, grads, near_t):
    @pl.when(pl.program_id(0) == 0)
    def _():
        near_t[:, :HALF] = near[...].T
        near_t[:, HALF:] = far[...].T

    gate_w, up_w, down_w = [w[:, m].reshape(D, 256) for m in range(3)]
    for r, normed in ((0, near), (HALF, far)):
        rows = slice(r, r + HALF)
        g = nn(normed[...], gate_w)
        u = nn(normed[...], up_w)
        a = nn(back[rows, :], down_w)
        sigma = 1.0 / (1.0 + jnp.exp(-g))
        swished = g * sigma
        act[rows, :] = (swished * u).astype(bf16)
        gate_grad[rows, :] = (a * u * sigma * (1.0 + g * (1.0 - sigma))).astype(bf16)
        up_grad[rows, :] = (a * swished).astype(bf16)
    for m, (left, right) in enumerate(((near_t, gate_grad), (near_t, up_grad), (back_t, act))):
        for r in range(4):
            part = nn(left[384 * r : 384 * (r + 1), :], right[...]).astype(bf16)
            grads[4 * r : 4 * (r + 1), m] = part.reshape(4, ROWS, 256)


def spread(gate_grad, up_grad, w, near, far):
    gate_w, up_w = [w[:, m].reshape(768, FP) for m in range(2)]
    for b in range(3):
        cols = slice(256 * b, 256 * (b + 1))
        part = nt(gate_grad[...], gate_w[cols]) + nt(up_grad[...], up_w[cols])
        near[:, cols] = part[:HALF].astype(bf16)
        far[:, cols] = part[HALF:].astype(bf16)


def spread_out(act, w, near, far):
    down_w = w[:, 0].reshape(768, FP)
    for b in range(3):
        cols = slice(256 * b, 256 * (b + 1))
        part = nt(act[...], down_w[cols])
        near[:, cols] = part[:HALF].astype(bf16)
        far[:, cols] = part[HALF:].astype(bf16)


def halve(ids, near, other, own, p1, p2, p3):
    y = ids[3]
    for k, out in ((0, own), (1, p1), (3, p2), (2, p3)):
        rows = at(PART * lax.rem(y + k, 4), PART, PART)
        out[...] = (near[rows, :].astype(f32) + other[rows, :].astype(f32)).astype(out.dtype)


def summed(own, parts):
    total = own[...]
    for part in parts:
        total += part[...].astype(f32)
    return total


def hidden_back(ids, own, a1, a2, a3, hidden, back, gain, grad, low, gain_part):
    h = hidden[...]
    g = summed(own, (a1, a2, a3))
    scale = lax.rsqrt(jnp.mean(h * h, -1, keepdims=True) + EPS_NORM)
    gain_part[...] = jnp.sum(g * h * scale, 0, keepdims=True)
    v = back[...].astype(f32) + norm_back(h, scale, gain[...], g)
    grad[...] = v
    low[...] = v.astype(bf16)


def add_parts(ids, own, a1, a2, a3, total):
    total[...] = summed(own, (a1, a2, a3))


def finish(ids, out_sum, own_b, b1, b2, b3, hidden, tok, grad, gain, done):
    length, y, c = ids[0], ids[3], ids[4]
    o, g = out_sum[...], summed(own_b, (b1, b2, b3))
    t = lax.broadcasted_iota(jnp.int32, (PART, 1), 0) + HALF * c + PART * y
    done[0] = jnp.where(t < length, o + hidden[...], 0.0).astype(bf16)
    x = tok[...].astype(f32)
    scale = lax.rsqrt(jnp.mean(x * x, -1, keepdims=True) + EPS_NORM)
    done[1] = (grad[...] + norm_back(x, scale, gain[...], g)).astype(bf16)


def attend_back(
    ids, near, far, rows_w, heads, lse, cosine, sine,
    grads, low, att_grad, key_grad, value_grad,
):
    length, y, c = ids[0], ids[3], ids[4]
    for k, e in enumerate(RELATIVE):
        place = PART * lax.rem(y + e + 4, 4)
        low[at(HALF * c + place, PART, PART), :] = near[k]
        low[at(HALF * (1 - c) + place, PART, PART), :] = far[k]
    has_heads = (ids[2] < KEY_AT).astype(f32)
    att_grad[...] = (nt(low[...], rows_w[...]) * has_heads).astype(bf16)
    key_grad[...] = jnp.zeros_like(key_grad)
    value_grad[...] = jnp.zeros_like(value_grad)
    for h in range(2):
        cols = slice(HEAD * h, HEAD * (h + 1))
        for i in range(4):
            n = 128 * (i + 1)
            rows = slice(128 * i, n)
            q = heads[rows, cols]
            k, v = heads[:n, 2 * HEAD : 3 * HEAD], heads[:n, 3 * HEAD :]
            o = att_grad[rows, cols]
            s = nt(q, k) * SCALE
            p = jnp.where(kept(i, n, length), jnp.exp(s - lse[rows, HEAD * h : HEAD * h + 1]), 0.0)
            d = nt(o, v)
            g = (p * (d - jnp.sum(p * d, -1, keepdims=True))).astype(bf16)
            value_grad[:n, :] += tn(p.astype(bf16), o)
            key_grad[:n, :] += tn(g, q)
            dq = nn(g, k) * SCALE
            dq = dq * cosine[rows, :] - pltpu.roll(dq, HEAD // 2, 1) * sine[rows, :]
            grads[rows, cols] = dq.astype(bf16)
    dk = key_grad[...] * SCALE
    dk = dk * cosine[...] - pltpu.roll(dk, HEAD // 2, 1) * sine[...]
    grads[:, 2 * HEAD : 3 * HEAD] = dk.astype(bf16)
    grads[:, 3 * HEAD :] = value_grad[...].astype(bf16)


def joint_back(
    ids, grads, w, tok, second_part,
    near, far, chunks, gain_part, vec, blocks,
):
    g = grads[...]
    gain_part[...] = jnp.zeros_like(gain_part)
    for r in range(0, T, 128):
        rows = slice(r, r + 128)
        back = nt(g[rows], w[...])
        half, place = r // HALF, slice(r % HALF, r % HALF + 128)
        moves = back.astype(bf16)

        @pl.when(ids[4] == half)
        def _():
            near[place, :] = moves

        @pl.when(ids[4] != half)
        def _():
            far[place, :] = moves

        x = tok[rows, :].astype(f32)
        s = lax.rsqrt(jnp.mean(x * x, -1, keepdims=True) + EPS_NORM)
        gain_part[...] += jnp.sum(back * x * s, 0, keepdims=True)
    vec[...] = jnp.zeros_like(vec)
    vec[:, :D] = gain_part[...]
    vec[:, D : 2 * D] = second_part[...]
    bias = jnp.sum(g.astype(f32), 0, keepdims=True)
    head_at = jnp.minimum(ids[2], KEY_AT - 1)
    key_start = 2 * D + JC * KEY_AT + HEAD * lax.div(head_at, 3)
    vec[:, at(2 * D + JC * head_at, JC, JC)] = bias[:, :JC]
    vec[:, at(key_start, HEAD, HEAD)] = bias[:, JC : JC + HEAD]
    vec[:, at(key_start + JC, HEAD, HEAD)] = bias[:, JC + HEAD :]
    for d in range(DP):
        blocks[d : d + 1, :] = vec[:, 320 * d : 320 * (d + 1)]
    for m in range(MP):
        chunks[m, :T, :] = g[:, 2 * HEAD : 3 * HEAD] if m < MP - 1 else g[:, 3 * HEAD :]
        piece = blocks[:, 40 * m : 40 * (m + 1)]
        piece = jnp.concatenate([piece, jnp.zeros((DP, HEAD - 40), f32)], 1)
        high = piece.astype(bf16)
        chunks[m, T : T + DP, :] = high
        chunks[m, T + DP :, :] = (piece - high.astype(f32)).astype(bf16)


def weigh_joint(ids, normed, grads, moved, mixer_parts, parts):
    keys = [moved[j, :T, :].astype(f32) for j in range(KEY_AT)]
    pair = jnp.concatenate([keys[0] + keys[1] + keys[2], keys[3] + keys[4] + keys[5]], 1)
    own = grads[:, :JC].astype(f32)
    g = jnp.where(ids[2] < KEY_AT, own, pair).astype(bf16)
    for r in range(4):
        cols = slice(384 * r, 384 * (r + 1))
        part = tn(normed[:, cols], g).astype(bf16)
        parts[4 * r : 4 * (r + 1), :ROWS, :JC] = part.reshape(4, ROWS, JC)
    parts[:, :ROWS, JC:] = mixer_parts[...]
    vec = moved[0, T:, :].astype(f32)
    for j in range(1, MP):
        vec += moved[j, T:, :].astype(f32)
    vec = vec[:DP] + vec[DP:]
    high = vec.astype(bf16).astype(f32)
    rest = jnp.zeros((8, MC), bf16)
    for d in range(DP):
        parts[d, ROWS:, :HEAD] = jnp.broadcast_to(high[d : d + 1], (8, HEAD)).astype(bf16)
        low = (vec - high)[d : d + 1]
        parts[d, ROWS:, HEAD:JC] = jnp.broadcast_to(low, (8, HEAD)).astype(bf16)
        parts[d, ROWS:, JC:] = rest


def weigh_mixer(ids, near, far, low, parts):
    y, c = ids[3], ids[4]

    def own_columns(half):
        v = low[at(HALF * half, HALF, HALF), at(384 * y, 384, 384)].astype(f32)
        return jnp.where(c == 0, v[:, :MC], v[:, MC:]).astype(bf16)

    mine, other = own_columns(c), own_columns(1 - c)
    for j in range(KEY_AT):
        part = (tn(near[j], mine) + tn(far[j], other)).astype(bf16)
        start = JC * j
        while start < JC * (j + 1):
            stop = min((start // ROWS + 1) * ROWS, JC * (j + 1))
            first = start % ROWS
            parts[start // ROWS, first : first + stop - start, :] = part[
                start - JC * j : stop - JC * j
            ]
            start = stop


def settle_grads(ids, moved, ff, joint, mixer, vector, squares):
    total = moved[0].astype(f32)
    for d in range(1, DP):
        total += moved[d].astype(f32)
    joint[...] = total[:ROWS, :JC]
    mixer[...] = total[:ROWS, JC:]
    vec = total[ROWS : ROWS + 1, :HEAD] + total[ROWS : ROWS + 1, HEAD:JC]
    vector[...] = vec
    total = total[:ROWS]
    total = jnp.sum(total * total) + jnp.sum(vec * vec)
    for m in range(3):
        v = ff[m].astype(f32)
        total += jnp.sum(v * v)
    squares[...] = jnp.full(squares.shape, total, f32)


def update(
    squares, joint_grad, mixer_grad, ff_grad, vector_grad,
    joint_w, joint_m, joint_v, mixer_w, mixer_m, mixer_v, expand_w, expand_m, expand_v,
    shrink_w, shrink_m, shrink_v, vector_w, vector_m, vector_v,
    norm_out, joint_wn, joint_mn, joint_vn, mixer_wn, mixer_mn, mixer_vn,
    expand_wn, expand_mn, expand_vn, shrink_wn, shrink_mn, shrink_vn,
    vector_wn, vector_mn, vector_vn,
):
    norm = jnp.sqrt(jnp.sum(squares[:, 0, :], 0, keepdims=True))
    norm_out[...] = norm
    clip = jnp.minimum(1.0, MAX_NORM / (norm[:, :1] + 1e-06))

    def step(grad, before, after, rate, decay, part=Ellipsis):
        w, m, v = [ref[part] for ref in before]
        results = adam_step(w, clip * grad, m, v, rate, decay)
        for ref, new in zip(after, results):
            ref[part] = new

    step(
        joint_grad[...], (joint_w, joint_m, joint_v), (joint_wn, joint_mn, joint_vn),
        RATE_MATRIX, DECAY,
    )
    step(
        mixer_grad[...], (mixer_w, mixer_m, mixer_v), (mixer_wn, mixer_mn, mixer_vn),
        RATE_MATRIX, DECAY,
    )
    for m in range(2):
        step(
            ff_grad[m, :, :FF].astype(f32),
            (expand_w, expand_m, expand_v), (expand_wn, expand_mn, expand_vn),
            RATE_MATRIX, DECAY, m,
        )
    step(
        ff_grad[2, :, :FF].astype(f32),
        (shrink_w, shrink_m, shrink_v), (shrink_wn, shrink_mn, shrink_vn),
        RATE_MATRIX, DECAY,
    )
    step(
        vector_grad[:, :40], (vector_w, vector_m, vector_v), (vector_wn, vector_mn, vector_vn),
        RATE_VECTOR, 0.0,
    )


def settle(ids, near, far, output, input_grad):
    y, c = ids[3], ids[4]
    for n, out in enumerate((output, input_grad)):
        for k, e in enumerate(RELATIVE):
            place = PART * lax.rem(y + e + 4, 4)
            out[0, at(HALF * c + place, PART, PART), :] = near[k, n].astype(f32)
            out[0, at(HALF * (1 - c) + place, PART, PART), :] = far[k, n].astype(f32)


def pile(ids, p0, p1, p2, p3, out):
    for k, p in enumerate((p0, p1, p2, p3)):
        out[k] = p[...]


def norm_back(v, scale, gain, grad):
    scaled = gain * grad
    return scale * scaled - v * scale * scale * scale * jnp.mean(scaled * v, -1, keepdims=True)


def adam_step(weight, grad, moment, square, rate, decay):
    moment_next = BETA_ONE * moment + (1.0 - BETA_ONE) * grad
    square_next = BETA_TWO * square + (1.0 - BETA_TWO) * grad * grad
    first_hat = moment_next / (1.0 - BETA_ONE**STEP)
    second_hat = square_next / (1.0 - BETA_TWO**STEP)
    weight_next = weight - rate * (first_hat / (jnp.sqrt(second_hat) + ADAM_EPS) + decay * weight)
    return (weight_next, moment_next, square_next)


def tables():
    freq = np.float32(ROPE_BASE) ** (-np.arange(0, HEAD, 2, dtype=np.float32) / np.float32(HEAD))
    angle = np.arange(T, dtype=np.float32)[:, None] * freq.astype(np.float32)[None, :]
    cosine, sine = np.cos(angle), np.sin(angle)
    return (
        np.concatenate([cosine, cosine], -1).astype(np.float32),
        np.concatenate([-sine, sine], -1).astype(np.float32),
    )


def split_low(v):
    high = lax.reduce_precision(v, 8, 7)
    middle = lax.reduce_precision(v - high, 8, 7)
    return [part.astype(bf16) for part in (high, middle, v - high - middle)]


def body(
    tokens, lengths, cotangent,
    joint_weight, joint_moment, joint_square,
    mixer_weight, mixer_moment, mixer_square,
    expand_weight, expand_moment, expand_square,
    shrink_weight, shrink_moment, shrink_square,
    vector_params, vector_moment, vector_square,
):
    dp, mp = lax.axis_index("dp"), lax.axis_index("mp")
    y, c = mp // 2, mp % 2
    tok, length = tokens[0], lengths[0]
    ids = jnp.stack([length, dp, mp, y, c]).astype(jnp.int32)

    stack = jnp.concatenate(
        [expand_weight.astype(bf16), shrink_weight.T.astype(bf16)[None]], 0
    )
    stack = jnp.pad(stack, ((0, 0), (0, 0), (0, FP - FF)))
    ff = lax.all_gather(stack, "dp", axis=0, tiled=False)

    low = jnp.concatenate([joint_weight.astype(bf16), mixer_weight.astype(bf16)], 1)
    vec = jnp.pad(jnp.stack(split_low(vector_params)), ((0, 13), (0, JC + MC - 40)))
    low = jnp.concatenate([low, vec], 0)
    other = swap_core(low)
    first, second = jnp.where(c == 0, low, other), jnp.where(c == 0, other, low)
    pairs = [
        jnp.concatenate([first[:ROWS, cols], second[:ROWS, cols]], 1)
        for cols in (slice(0, HEAD), slice(HEAD, JC))
    ]
    chip = jnp.concatenate([first[:ROWS, JC:], second[:ROWS, JC:]], 1)
    chip = lax.dynamic_slice_in_dim(chip, 48 * c, 48, 0)
    rest = jnp.concatenate([chip[:32, JC:], jnp.pad(chip[32:, JC:], ((0, 16), (0, 0)))], 1)
    sent = jnp.concatenate([low[:ROWS, :JC], chip[:, :JC], rest], 0)
    query_w = exchange(jnp.broadcast_to(sent, (DP,) + sent.shape), "dp")
    vec = jnp.concatenate([first[ROWS:, :HEAD], second[ROWS:, :HEAD]], 1)
    sends = [pairs[0], pairs[1], jnp.where(c == 0, pairs[0], pairs[1])]
    sends = [jnp.concatenate([v, vec], 0) for v in sends]
    a1, a2, a3 = [shift_y(v, k) for v, k in zip(sends, (1, -1, 2))]
    pair = jnp.where(y == 0, a1[:ROWS], jnp.where(y == 2, a2[:ROWS], a3[:ROWS]))
    vec = jnp.stack([vec, a2[ROWS:], a3[ROWS:], a1[ROWS:]])[:, :3]
    vec = lax.dynamic_slice_in_dim(jnp.concatenate([vec, vec]), (4 - y) % 4, 4, 0)
    sent = jnp.concatenate([pair, vec.reshape(12, JC), query_w[0, :4]], 0)
    pair_w = exchange(jnp.broadcast_to(sent, (DP,) + sent.shape), "dp")
    vec = pair_w[:, ROWS : ROWS + 12].astype(f32).reshape(DP, 4, 3, 2, HEAD)[..., :40]
    vec = vec[:, :, 0] + vec[:, :, 1] + vec[:, :, 2]
    vec = vec.reshape(-1)

    gain_first, gain_second = vec[None, :D], vec[None, D : 2 * D]
    key_start = JC * KEY_AT + HEAD * (jnp.minimum(mp, KEY_AT - 1) // 3)
    starts = ((JC * mp, JC), (key_start, HEAD), (key_start + JC, HEAD))
    bias = jnp.concatenate(
        [lax.dynamic_slice_in_dim(vec, 2 * D + start, size, 0) for start, size in starts]
    )[None]

    cosine, sine = tables()
    back, back_t, back_part, tok_part = whole(
        prepare,
        [((T, D), bf16), ((D, T), bf16), ((PART, D), bf16), ((PART, D), bf16)],
        [ids, cotangent[0], tok],
    )
    normed, heads, att_sent, lse, joint_w = whole(
        attend,
        [
            ((T, D), bf16), ((T, 2 * JC), bf16), ((MP, HALF, JC), bf16),
            ((T, JC), f32), ((D, 2 * JC), bf16),
        ],
        [ids, tok, gain_first, bias, cosine, sine, query_w, pair_w],
        after=[back],
    )
    att_near = exchange(att_sent, "mp")
    att_far = swap_core(att_near)
    mixer_near = gather(shift_y, query_w[:, ROWS:])
    mixer_far = [swap_core(v) for v in mixer_near]
    hidden_part, normed_near, rows_w = whole(
        mix,
        [((PART, D), f32), ((HALF, D), bf16), ((JC, D), bf16)],
        [ids, att_near] + mixer_near + mixer_far + [tok, gain_second],
        scratch=[
            pltpu.VMEM((HALF, D), f32), pltpu.VMEM((HALF, D), bf16), pltpu.VMEM((D, D), bf16),
        ],
    )
    normed_far = swap_core(normed_near)

    def columns(n):
        return pl.BlockSpec((n, 256), lambda i: (0, i))

    def fixed(shape):
        return pl.BlockSpec(shape, lambda i: (0,) * len(shape))

    block = pl.BlockSpec((DP, 3, ROWS, 256), lambda i: (0, 0, 0, i))
    act, gate_grad, up_grad, ff_grads = pl.pallas_call(
        gated,
        grid=(pl.cdiv(FP, 256),),
        out_shape=[jax.ShapeDtypeStruct((T, FP), bf16)] * 3
        + [jax.ShapeDtypeStruct((DP, 3, ROWS, FP), bf16)],
        in_specs=[fixed((HALF, D)), fixed((HALF, D)), fixed((T, D)), fixed((D, T)), block],
        out_specs=[columns(T)] * 3 + [block],
        scratch_shapes=[pltpu.VMEM((D, T), bf16)],
        compiler_params=pltpu.CompilerParams(vmem_limit_bytes=60 * MiB),
        cost_estimate=SMALL,
    )(normed_near, normed_far, back, back_t, ff)
    ff_shard = lax.psum_scatter(ff_grads, "dp", scatter_dimension=0, tiled=False)

    near, far = pl.pallas_call(
        spread,
        grid=(2,),
        out_shape=[jax.ShapeDtypeStruct((HALF, D), bf16)] * 2,
        in_specs=[fixed((T, FP))] * 2
        + [pl.BlockSpec((DP // 2, 2, ROWS, FP), lambda i: (i, 0, 0, 0))],
        out_specs=[pl.BlockSpec((HALF, 768), lambda i: (0, i))] * 2,
        compiler_params=pltpu.CompilerParams(vmem_limit_bytes=60 * MiB),
        cost_estimate=SMALL,
    )(gate_grad, up_grad, ff)

    def half_sum(near, far, after=()):
        own, *parts = whole(
            halve,
            [((PART, D), f32)] + [((PART, D), bf16)] * 3,
            [ids, near, swap_core(far)],
            after=after,
            limit=8,
        )
        return [own] + [shift_y(v, k) for v, k in zip(parts, (1, -1, 2))]

    normed_second_parts = half_sum(near, far)
    out_near, out_far = pl.pallas_call(
        spread_out,
        grid=(2,),
        out_shape=[jax.ShapeDtypeStruct((HALF, D), bf16)] * 2,
        in_specs=[
            fixed((T, FP)),
            pl.BlockSpec((DP // 2, 1, ROWS, FP), lambda i: (i, 2, 0, 0)),
        ],
        out_specs=[pl.BlockSpec((HALF, 768), lambda i: (0, i))] * 2,
        compiler_params=pltpu.CompilerParams(vmem_limit_bytes=60 * MiB),
        cost_estimate=SMALL,
    )(act, ff)
    hidden_grad, low, gain_second_part = whole(
        hidden_back,
        [((PART, D), f32), ((PART, D), bf16), ((1, D), f32)],
        [ids] + normed_second_parts + [hidden_part, back_part, gain_second],
        after=[out_far],
        limit=8,
    )
    low_near = jnp.stack(gather(shift_y, low))
    low_far = swap_core(low_near)
    out_parts = half_sum(out_near, out_far)
    heads_grad, hidden_low = whole(
        attend_back,
        [((T, 2 * JC), bf16), ((T, D), bf16)],
        [ids, low_near, low_far, rows_w, heads, lse, cosine, sine],
        scratch=[
            pltpu.VMEM((T, JC), bf16),
            pltpu.VMEM((T, HEAD), f32),
            pltpu.VMEM((T, HEAD), f32),
        ],
        after=[out_parts[0]],
    )
    (out_sum,) = whole(add_parts, [((PART, D), f32)], [ids] + out_parts, limit=8, after=[heads_grad])
    input_near, input_far, chunks = whole(
        joint_back,
        [((HALF, D), bf16), ((HALF, D), bf16), ((MP, T + 2 * DP, HEAD), bf16)],
        [ids, heads_grad, joint_w, tok, gain_second_part],
        scratch=[
            pltpu.VMEM((1, D), f32),
            pltpu.VMEM((1, DP * MP * 40), f32),
            pltpu.VMEM((DP, MP * 40), f32),
        ],
        after=[out_sum],
    )
    moved = exchange(chunks, "mp")
    (mixer_parts,) = whole(
        weigh_mixer,
        [((DP, ROWS, MC), bf16)],
        [ids, att_near, att_far, hidden_low],
    )
    (joint_parts,) = whole(
        weigh_joint,
        [((DP, ROWS + 8, JC + MC), bf16)],
        [ids, normed, heads_grad, moved, mixer_parts],
    )
    joint_shard, mixer_shard, vector_shard, squares = whole(
        settle_grads,
        [((ROWS, JC), f32), ((ROWS, MC), f32), ((1, HEAD), f32), ((DP * MP, 1, HEAD), f32)],
        [ids, exchange(joint_parts, "dp"), ff_shard],
    )

    squares = exchange(squares, ("dp", "mp"))

    input_parts = half_sum(input_near, input_far, after=[joint_parts])
    (done,) = whole(
        finish,
        [((2, PART, D), bf16)],
        [ids, out_sum] + input_parts + [hidden_part, tok_part, hidden_grad, gain_first],
        limit=8,
    )
    (done_near,) = whole(
        pile, [((4, 2, PART, D), bf16)], [ids] + gather(shift_y, done), after=[squares], limit=8
    )
    done_far = swap_core(done_near)
    output, input_grad = whole(settle, [((1, T, D), f32)] * 2, [ids, done_near, done_far])

    matrices = [joint_weight, joint_moment, joint_square]
    matrices += [mixer_weight, mixer_moment, mixer_square]
    matrices += [expand_weight, expand_moment, expand_square]
    matrices += [v.T for v in (shrink_weight, shrink_moment, shrink_square)]
    matrices += [v[None] for v in (vector_params, vector_moment, vector_square)]
    def sixth(shape):
        n = len(shape)
        if shape[-2] != ROWS:
            return pl.BlockSpec(shape, lambda i: (0,) * n)
        return pl.BlockSpec(
            shape[:-2] + (ROWS // 6, shape[-1]), lambda i: (0,) * (n - 2) + (i, 0)
        )

    given = [squares, joint_shard, mixer_shard, ff_shard, vector_shard] + matrices
    made = [(1, HEAD)] + [v.shape for v in matrices]
    norm, *new = pl.pallas_call(
        update,
        grid=(6,),
        out_shape=[jax.ShapeDtypeStruct(shape, f32) for shape in made],
        in_specs=[sixth(v.shape) for v in given],
        out_specs=[sixth(shape) for shape in made],
        compiler_params=pltpu.CompilerParams(vmem_limit_bytes=60 * MiB),
        cost_estimate=SMALL,
    )(*given)
    new[9:12] = [v.T for v in new[9:12]]
    new[12:] = [v[0] for v in new[12:]]
    return (output, input_grad, norm[0, 0], *new)


def solution(mesh):
    row = P("dp", None, None)
    matrix = [P("dp", "mp")] * 6 + [P(None, "dp", "mp")] * 3 + [P("mp", "dp")] * 3
    vector = [P(("dp", "mp"))] * 3
    return jax.shard_map(
        body,
        mesh=mesh,
        in_specs=tuple([row, P("dp"), row] + matrix + vector),
        out_specs=tuple([row, row, P()] + matrix + vector),
        check_vma=False,
    )
```

```python
import jax
import jax.numpy as jnp
import numpy as np
from jax import lax
from jax.experimental import pallas as pl
from jax.experimental.pallas import tpu as pltpu
from jax.sharding import PartitionSpec as P

QUERY_HEADS = 12
KEY_VALUE_HEADS = 2
HEAD = 128
STEP = 5
EPS_NORM = 1e-06
ROPE_BASE = 1000000.0
MAX_NORM = 1.0
BETA_ONE = 0.9
BETA_TWO = 0.95
ADAM_EPS = 1e-08
DECAY = 0.1
RATE_MATRIX = 0.06
RATE_VECTOR = 0.8
MASKED = -1e30

T = 512
HALF = 256
PART = 64
D = 1536
FF = 1120
FP = 1152
DP = 16
MP = 8
ROWS = D // DP
JC = 256
MC = 192
KEY_AT = 6
SCALE = HEAD ** (-0.5)

f32 = jnp.float32
bf16 = jnp.bfloat16
VM = pl.BlockSpec(memory_space=pltpu.VMEM)
SM = pl.BlockSpec(memory_space=pltpu.SMEM)
MiB = 1 << 20
SMALL = pl.CostEstimate(flops=1, bytes_accessed=1, transcendentals=0)


def shift_y(v, k):
    return lax.ppermute(v, "mp", [(i, (i + 2 * k) % MP) for i in range(MP)])


def from_last_chip(v, k):
    return lax.ppermute(v, "mp", [(i, (i + 2 * k) % MP) for i in (MP - 2, MP - 1)])


def swap_core(v):
    return lax.ppermute(v, "mp", [(i, i ^ 1) for i in range(MP)])


def exchange(v, axis):
    return lax.all_to_all(v, axis, split_axis=0, concat_axis=0, tiled=True)


RELATIVE = (0, -1, 1, 2)


def gather(shift, v):
    return [v, shift(v, 1), shift(v, -1), shift(v, 2)]


def nn(a, b):
    return lax.dot_general(a, b, (((1,), (0,)), ((), ())), preferred_element_type=f32)


def nt(a, b):
    return lax.dot_general(a, b, (((1,), (1,)), ((), ())), preferred_element_type=f32)


def tn(a, b):
    return lax.dot_general(a, b, (((0,), (0,)), ((), ())), preferred_element_type=f32)


def whole(body, outs, args, scratch=(), limit=60, after=()):
    n = len(args)

    def bare(*refs):
        body(*refs[:n], *refs[n + len(after) :])

    return pl.pallas_call(
        bare,
        out_shape=[jax.ShapeDtypeStruct(s, d) for s, d in outs],
        in_specs=[SM] + [VM] * (n - 1) + [pl.BlockSpec(memory_space=pl.ANY)] * len(after),
        out_specs=[VM] * len(outs),
        scratch_shapes=list(scratch),
        compiler_params=pltpu.CompilerParams(vmem_limit_bytes=limit * MiB),
        cost_estimate=SMALL,
    )(*args, *after)


def at(start, size, step):
    return pl.ds(pl.multiple_of(start, step), size)


def prepare(ids, cotangent, tok, back, back_t, back_part, tok_part):
    length, y, c = ids[0], ids[3], ids[4]
    for h in range(2):
        start = HALF * ((c + h) % 2)
        t = lax.broadcasted_iota(jnp.int32, (HALF, 1), 0) + start
        v = cotangent[at(start, HALF, HALF), :]
        v = jnp.where(t < length, v, jnp.zeros_like(v))
        back[HALF * h : HALF * (h + 1), :] = v
        back_t[:, HALF * h : HALF * (h + 1)] = v.T
    back_part[...] = back[at(PART * y, PART, PART), :]
    tok_part[...] = tok[at(HALF * c + PART * y, PART, PART), :]


def kept(i, n, length):
    t = lax.broadcasted_iota(jnp.int32, (128, n), 0) + 128 * i
    s = lax.broadcasted_iota(jnp.int32, (128, n), 1)
    return (s <= t) & (s < length)


def attend(
    ids, tok, gain, bias, cosine, sine, query_w, pair_w,
    normed, heads, out, lse, w,
):
    w[:, :JC] = query_w[:, :ROWS, :].reshape(D, JC)
    w[:, JC:] = pair_w[:, :ROWS, :].reshape(D, JC)

    @pl.loop(0, T // 128)
    def _(i):
        rows = at(i * 128, 128, 128)
        x = tok[rows, :].astype(f32)
        s = lax.rsqrt(jnp.mean(x * x, -1, keepdims=True) + EPS_NORM)
        n = (x * s * gain[...]).astype(bf16)
        normed[rows, :] = n
        j = nn(n, w[...]) + bias[...]
        for h in range(4):
            cols = slice(HEAD * h, HEAD * (h + 1))
            u = j[:, cols]
            if h < 3:
                u = u * cosine[rows, :] + pltpu.roll(u, HEAD // 2, 1) * sine[rows, :]
            heads[rows, cols] = u.astype(bf16)

    for h in range(2):
        for i in range(4):
            n = 128 * (i + 1)
            q = heads[128 * i : n, HEAD * h : HEAD * (h + 1)]
            k, v = heads[:n, 2 * HEAD : 3 * HEAD], heads[:n, 3 * HEAD :]
            s = jnp.where(kept(i, n, ids[0]), nt(q, k) * SCALE, MASKED)
            m = jnp.max(s, -1, keepdims=True)
            e = jnp.exp(s - m)
            total = jnp.sum(e, -1, keepdims=True)
            o = nn((e / total).astype(bf16), v).astype(bf16)
            lse[128 * i : n, HEAD * h : HEAD * (h + 1)] = jnp.broadcast_to(
                m + jnp.log(total), (128, HEAD)
            )
            at_row = 128 * (i % 2)
            for y in range(4):
                out[2 * y + i // 2, at_row : at_row + 128, HEAD * h : HEAD * (h + 1)] = o


def mix(
    ids, att, a0, a1, a2, a3, b0, b1, b2, b3, tok, gain,
    hidden_part, normed, rows_w, hidden, side, mixer,
):
    y, c = ids[3], ids[4]
    for j in range(KEY_AT):
        side[:, JC * j : JC * (j + 1)] = att[j]
    mine = at(HALF * c, HALF, HALF)
    for e, a, b in zip(RELATIVE, (a0, a1, a2, a3), (b0, b1, b2, b3)):
        cols = at(384 * lax.rem(y + e + 4, 4), 384, 384)
        first = 384 * lax.rem(y + e + 4, 4)
        left, right = at(first, JC, 128), at(first + JC, HEAD, 128)
        for d in range(DP):
            for half, v in ((c, a), (1 - c, b)):
                row = ROWS * d + 48 * half
                mixer[at(row, 48, 16), left] = v[d, :48, :]
                mixer[at(row, 32, 16), right] = v[d, 48:80, :HEAD]
                mixer[at(row + 32, 16, 16), right] = v[d, 48:64, HEAD:]
        hidden[:, cols] = nn(side[...], mixer[:, cols]) + tok[mine, cols].astype(f32)
    hidden_part[...] = hidden[at(PART * y, PART, PART), :]
    rows_w[...] = mixer[at(JC * jnp.minimum(ids[2], KEY_AT - 1), JC, JC), :]
    for r in range(0, HALF, 64):
        v = hidden[r : r + 64, :]
        s = lax.rsqrt(jnp.mean(v * v, -1, keepdims=True) + EPS_NORM)
        normed[r : r + 64, :] = (v * s * gain[...]).astype(bf16)


def gated(near, far, back, back_t, w, act, gate_grad, up_grad, grads, near_t):
    @pl.when(pl.program_id(0) == 0)
    def _():
        near_t[:, :HALF] = near[...].T
        near_t[:, HALF:] = far[...].T

    gate_w, up_w, down_w = [w[:, m].reshape(D, 256) for m in range(3)]
    for r, normed in ((0, near), (HALF, far)):
        rows = slice(r, r + HALF)
        g = nn(normed[...], gate_w)
        u = nn(normed[...], up_w)
        a = nn(back[rows, :], down_w)
        sigma = 1.0 / (1.0 + jnp.exp(-g))
        swished = g * sigma
        act[rows, :] = (swished * u).astype(bf16)
        gate_grad[rows, :] = (a * u * sigma * (1.0 + g * (1.0 - sigma))).astype(bf16)
        up_grad[rows, :] = (a * swished).astype(bf16)
    for m, (left, right) in enumerate(((near_t, gate_grad), (near_t, up_grad), (back_t, act))):
        for r in range(4):
            part = nn(left[384 * r : 384 * (r + 1), :], right[...]).astype(bf16)
            grads[4 * r : 4 * (r + 1), m] = part.reshape(4, ROWS, 256)


def spread(gate_grad, up_grad, w, near, far):
    gate_w, up_w = [w[:, m].reshape(768, FP) for m in range(2)]
    for b in range(3):
        cols = slice(256 * b, 256 * (b + 1))
        part = nt(gate_grad[...], gate_w[cols]) + nt(up_grad[...], up_w[cols])
        near[:, cols] = part[:HALF].astype(bf16)
        far[:, cols] = part[HALF:].astype(bf16)


def spread_out(act, w, near, far):
    down_w = w[:, 0].reshape(768, FP)
    for b in range(3):
        cols = slice(256 * b, 256 * (b + 1))
        part = nt(act[...], down_w[cols])
        near[:, cols] = part[:HALF].astype(bf16)
        far[:, cols] = part[HALF:].astype(bf16)


def halve(ids, near, other, own, p1, p2, p3):
    y = ids[3]
    for k, out in ((0, own), (1, p1), (3, p2), (2, p3)):
        rows = at(PART * lax.rem(y + k, 4), PART, PART)
        out[...] = (near[rows, :].astype(f32) + other[rows, :].astype(f32)).astype(out.dtype)


def halve_two(ids, near_a, other_a, near_b, other_b, own, p1, p2, p3):
    for n, (near, other) in enumerate(((near_a, other_a), (near_b, other_b))):
        halve(ids, near, other, own.at[n], p1.at[n], p2.at[n], p3.at[n])


def summed(own, parts):
    total = own[...]
    for part in parts:
        total += part[...].astype(f32)
    return total


def hidden_back(ids, own, a1, a2, a3, hidden, back, gain, grad, low, gain_part):
    h = hidden[...]
    g = summed(own, (a1, a2, a3))
    scale = lax.rsqrt(jnp.mean(h * h, -1, keepdims=True) + EPS_NORM)
    gain_part[...] = jnp.sum(g * h * scale, 0, keepdims=True)
    v = back[...].astype(f32) + norm_back(h, scale, gain[...], g)
    grad[...] = v
    low[...] = v.astype(bf16)


def finish(ids, own, a1, a2, a3, hidden, tok, grad, gain, done):
    length, y, c = ids[0], ids[3], ids[4]
    o, g = [summed(own.at[n], [a.at[n] for a in (a1, a2, a3)]) for n in range(2)]
    t = lax.broadcasted_iota(jnp.int32, (PART, 1), 0) + HALF * c + PART * y
    done[0] = jnp.where(t < length, o + hidden[...], 0.0).astype(bf16)
    x = tok[...].astype(f32)
    scale = lax.rsqrt(jnp.mean(x * x, -1, keepdims=True) + EPS_NORM)
    done[1] = (grad[...] + norm_back(x, scale, gain[...], g)).astype(bf16)


def attend_back(
    ids, near, far, rows_w, heads, lse, cosine, sine,
    grads, window, low, att_grad, key_grad, value_grad,
):
    length, y, c = ids[0], ids[3], ids[4]
    for k, e in enumerate(RELATIVE):
        place = PART * lax.rem(y + e + 4, 4)
        low[at(HALF * c + place, PART, PART), :] = near[k]
        low[at(HALF * (1 - c) + place, PART, PART), :] = far[k]
    window[...] = low[:, at(384 * y, 384, 384)]
    has_heads = (ids[2] < KEY_AT).astype(f32)
    att_grad[...] = (nt(low[...], rows_w[...]) * has_heads).astype(bf16)
    key_grad[...] = jnp.zeros_like(key_grad)
    value_grad[...] = jnp.zeros_like(value_grad)
    for h in range(2):
        cols = slice(HEAD * h, HEAD * (h + 1))
        for i in range(4):
            n = 128 * (i + 1)
            rows = slice(128 * i, n)
            q = heads[rows, cols]
            k, v = heads[:n, 2 * HEAD : 3 * HEAD], heads[:n, 3 * HEAD :]
            o = att_grad[rows, cols]
            s = nt(q, k) * SCALE
            p = jnp.where(kept(i, n, length), jnp.exp(s - lse[rows, HEAD * h : HEAD * h + 1]), 0.0)
            d = nt(o, v)
            g = (p * (d - jnp.sum(p * d, -1, keepdims=True))).astype(bf16)
            value_grad[:n, :] += tn(p.astype(bf16), o)
            key_grad[:n, :] += tn(g, q)
            dq = nn(g, k) * SCALE
            dq = dq * cosine[rows, :] - pltpu.roll(dq, HEAD // 2, 1) * sine[rows, :]
            grads[rows, cols] = dq.astype(bf16)
    dk = key_grad[...] * SCALE
    dk = dk * cosine[...] - pltpu.roll(dk, HEAD // 2, 1) * sine[...]
    grads[:, 2 * HEAD : 3 * HEAD] = dk.astype(bf16)
    grads[:, 3 * HEAD :] = value_grad[...].astype(bf16)


def joint_back(
    ids, grads, w, tok, second_part,
    near, far, chunks, gain_part, vec, blocks,
):
    g = grads[...]
    gain_part[...] = jnp.zeros_like(gain_part)
    for r in range(0, T, 128):
        rows = slice(r, r + 128)
        back = nt(g[rows], w[...])
        half, place = r // HALF, slice(r % HALF, r % HALF + 128)
        moves = back.astype(bf16)

        @pl.when(ids[4] == half)
        def _():
            near[place, :] = moves

        @pl.when(ids[4] != half)
        def _():
            far[place, :] = moves

        x = tok[rows, :].astype(f32)
        s = lax.rsqrt(jnp.mean(x * x, -1, keepdims=True) + EPS_NORM)
        gain_part[...] += jnp.sum(back * x * s, 0, keepdims=True)
    vec[...] = jnp.zeros_like(vec)
    vec[:, :D] = gain_part[...]
    vec[:, D : 2 * D] = second_part[...]
    bias = jnp.sum(g.astype(f32), 0, keepdims=True)
    head_at = jnp.minimum(ids[2], KEY_AT - 1)
    key_start = 2 * D + JC * KEY_AT + HEAD * lax.div(head_at, 3)
    vec[:, at(2 * D + JC * head_at, JC, JC)] = bias[:, :JC]
    vec[:, at(key_start, HEAD, HEAD)] = bias[:, JC : JC + HEAD]
    vec[:, at(key_start + JC, HEAD, HEAD)] = bias[:, JC + HEAD :]
    for d in range(DP):
        blocks[d : d + 1, :] = vec[:, 320 * d : 320 * (d + 1)]
    for m in range(MP):
        chunks[m, :T, :] = g[:, 2 * HEAD : 3 * HEAD] if m < MP - 1 else g[:, 3 * HEAD :]
        piece = blocks[:, 40 * m : 40 * (m + 1)]
        piece = jnp.concatenate([piece, jnp.zeros((DP, HEAD - 40), f32)], 1)
        high = piece.astype(bf16)
        chunks[m, T : T + DP, :] = high
        chunks[m, T + DP :, :] = (piece - high.astype(f32)).astype(bf16)


def back_to_input(
    ids, near_low, far_low, rows_w, heads, lse, cosine, sine, w, tok, second_part,
    grads, window, near, far, chunks,
    low, att_grad, key_grad, value_grad, gain_part, vec, blocks,
):
    attend_back(
        ids, near_low, far_low, rows_w, heads, lse, cosine, sine,
        grads, window, low, att_grad, key_grad, value_grad,
    )
    joint_back(ids, grads, w, tok, second_part, near, far, chunks, gain_part, vec, blocks)


def weigh_joint(ids, normed, grads, moved, mixer_parts, parts):
    keys = [moved[j, :T, :].astype(f32) for j in range(KEY_AT)]
    pair = jnp.concatenate([keys[0] + keys[1] + keys[2], keys[3] + keys[4] + keys[5]], 1)
    own = grads[:, :JC].astype(f32)
    g = jnp.where(ids[2] < KEY_AT, own, pair).astype(bf16)
    for r in range(4):
        cols = slice(384 * r, 384 * (r + 1))
        part = tn(normed[:, cols], g).astype(bf16)
        parts[4 * r : 4 * (r + 1), :ROWS, :JC] = part.reshape(4, ROWS, JC)
    parts[:, :ROWS, JC:] = mixer_parts[...]
    vec = moved[0, T:, :].astype(f32)
    for j in range(1, MP):
        vec += moved[j, T:, :].astype(f32)
    vec = vec[:DP] + vec[DP:]
    high = vec.astype(bf16).astype(f32)
    rest = jnp.zeros((8, MC), bf16)
    for d in range(DP):
        parts[d, ROWS:, :HEAD] = jnp.broadcast_to(high[d : d + 1], (8, HEAD)).astype(bf16)
        low = (vec - high)[d : d + 1]
        parts[d, ROWS:, HEAD:JC] = jnp.broadcast_to(low, (8, HEAD)).astype(bf16)
        parts[d, ROWS:, JC:] = rest


def weigh_mixer(ids, near, far, low, parts):
    c = ids[4]

    def own_columns(half):
        v = low[at(HALF * half, HALF, HALF), :].astype(f32)
        return jnp.where(c == 0, v[:, :MC], v[:, MC:]).astype(bf16)

    mine, other = own_columns(c), own_columns(1 - c)
    for j in range(KEY_AT):
        part = (tn(near[j], mine) + tn(far[j], other)).astype(bf16)
        start = JC * j
        while start < JC * (j + 1):
            stop = min((start // ROWS + 1) * ROWS, JC * (j + 1))
            first = start % ROWS
            parts[start // ROWS, first : first + stop - start, :] = part[
                start - JC * j : stop - JC * j
            ]
            start = stop


def settle_grads(ids, moved, ff, joint, mixer, vector, squares):
    total = moved[0].astype(f32)
    for d in range(1, DP):
        total += moved[d].astype(f32)
    joint[...] = total[:ROWS, :JC]
    mixer[...] = total[:ROWS, JC:]
    vec = total[ROWS : ROWS + 1, :HEAD] + total[ROWS : ROWS + 1, HEAD:JC]
    vector[...] = vec
    total = total[:ROWS]
    total = jnp.sum(total * total) + jnp.sum(vec * vec)
    for m in range(3):
        v = ff[m].astype(f32)
        total += jnp.sum(v * v)
    squares[...] = jnp.full(squares.shape, total, f32)


def update(
    squares, joint_grad, mixer_grad, ff_grad, vector_grad,
    joint_w, joint_m, joint_v, mixer_w, mixer_m, mixer_v, expand_w, expand_m, expand_v,
    shrink_w, shrink_m, shrink_v, vector_w, vector_m, vector_v,
    norm_out, joint_wn, joint_mn, joint_vn, mixer_wn, mixer_mn, mixer_vn,
    expand_wn, expand_mn, expand_vn, shrink_wn, shrink_mn, shrink_vn,
    vector_wn, vector_mn, vector_vn,
):
    norm = jnp.sqrt(jnp.sum(squares[:, 0, :], 0, keepdims=True))
    norm_out[...] = norm
    clip = jnp.minimum(1.0, MAX_NORM / (norm[:, :1] + 1e-06))

    def step(grad, before, after, rate, decay, part=Ellipsis):
        w, m, v = [ref[part] for ref in before]
        results = adam_step(w, clip * grad, m, v, rate, decay)
        for ref, new in zip(after, results):
            ref[part] = new

    step(
        joint_grad[...], (joint_w, joint_m, joint_v), (joint_wn, joint_mn, joint_vn),
        RATE_MATRIX, DECAY,
    )
    step(
        mixer_grad[...], (mixer_w, mixer_m, mixer_v), (mixer_wn, mixer_mn, mixer_vn),
        RATE_MATRIX, DECAY,
    )
    for m in range(2):
        step(
            ff_grad[m, :, :FF].astype(f32),
            (expand_w, expand_m, expand_v), (expand_wn, expand_mn, expand_vn),
            RATE_MATRIX, DECAY, m,
        )
    step(
        ff_grad[2, :, :FF].astype(f32),
        (shrink_w, shrink_m, shrink_v), (shrink_wn, shrink_mn, shrink_vn),
        RATE_MATRIX, DECAY,
    )
    step(
        vector_grad[:, :40], (vector_w, vector_m, vector_v), (vector_wn, vector_mn, vector_vn),
        RATE_VECTOR, 0.0,
    )


def settle(ids, near, far, output, input_grad):
    y, c = ids[3], ids[4]
    for n, out in enumerate((output, input_grad)):
        for k, e in enumerate(RELATIVE):
            place = PART * lax.rem(y + e + 4, 4)
            out[0, at(HALF * c + place, PART, PART), :] = near[k, n].astype(f32)
            out[0, at(HALF * (1 - c) + place, PART, PART), :] = far[k, n].astype(f32)


def pile(ids, p0, p1, p2, p3, out):
    for k, p in enumerate((p0, p1, p2, p3)):
        out[k] = p[...]


def norm_back(v, scale, gain, grad):
    scaled = gain * grad
    return scale * scaled - v * scale * scale * scale * jnp.mean(scaled * v, -1, keepdims=True)


def adam_step(weight, grad, moment, square, rate, decay):
    moment_next = BETA_ONE * moment + (1.0 - BETA_ONE) * grad
    square_next = BETA_TWO * square + (1.0 - BETA_TWO) * grad * grad
    first_hat = moment_next / (1.0 - BETA_ONE**STEP)
    second_hat = square_next / (1.0 - BETA_TWO**STEP)
    weight_next = weight - rate * (first_hat / (jnp.sqrt(second_hat) + ADAM_EPS) + decay * weight)
    return (weight_next, moment_next, square_next)


def tables():
    freq = np.float32(ROPE_BASE) ** (-np.arange(0, HEAD, 2, dtype=np.float32) / np.float32(HEAD))
    angle = np.arange(T, dtype=np.float32)[:, None] * freq.astype(np.float32)[None, :]
    cosine, sine = np.cos(angle), np.sin(angle)
    return (
        np.concatenate([cosine, cosine], -1).astype(np.float32),
        np.concatenate([-sine, sine], -1).astype(np.float32),
    )


def split_low(v):
    high = lax.reduce_precision(v, 8, 7)
    middle = lax.reduce_precision(v - high, 8, 7)
    return [part.astype(bf16) for part in (high, middle, v - high - middle)]


def body(
    tokens, lengths, cotangent,
    joint_weight, joint_moment, joint_square,
    mixer_weight, mixer_moment, mixer_square,
    expand_weight, expand_moment, expand_square,
    shrink_weight, shrink_moment, shrink_square,
    vector_params, vector_moment, vector_square,
):
    dp, mp = lax.axis_index("dp"), lax.axis_index("mp")
    y, c = mp // 2, mp % 2
    tok, length = tokens[0], lengths[0]
    ids = jnp.stack([length, dp, mp, y, c]).astype(jnp.int32)

    stack = jnp.concatenate(
        [expand_weight.astype(bf16), shrink_weight.T.astype(bf16)[None]], 0
    )
    stack = jnp.pad(stack, ((0, 0), (0, 0), (0, FP - FF)))
    ff = lax.all_gather(stack, "dp", axis=0, tiled=False)

    low = jnp.concatenate([joint_weight.astype(bf16), mixer_weight.astype(bf16)], 1)
    vec = jnp.pad(jnp.stack(split_low(vector_params)), ((0, 13), (0, JC + MC - 40)))
    low = jnp.concatenate([low, vec], 0)
    other = swap_core(low)
    first, second = jnp.where(c == 0, low, other), jnp.where(c == 0, other, low)
    pairs = [
        jnp.concatenate([first[:ROWS, cols], second[:ROWS, cols]], 1)
        for cols in (slice(0, HEAD), slice(HEAD, JC))
    ]
    chip = jnp.concatenate([first[:ROWS, JC:], second[:ROWS, JC:]], 1)
    chip = lax.dynamic_slice_in_dim(chip, 48 * c, 48, 0)
    rest = jnp.concatenate([chip[:32, JC:], jnp.pad(chip[32:, JC:], ((0, 16), (0, 0)))], 1)
    sent = jnp.concatenate([low[:ROWS, :JC], chip[:, :JC], rest], 0)
    query_w = exchange(jnp.broadcast_to(sent, (DP,) + sent.shape), "dp")
    vec = jnp.concatenate([first[ROWS:, :HEAD], second[ROWS:, :HEAD]], 1)
    sends = [pairs[0], pairs[1], jnp.where(c == 0, pairs[0], pairs[1])]
    sends = [jnp.concatenate([v, vec], 0) for v in sends]
    a1, a2, a3 = [shift_y(v, k) for v, k in zip(sends, (1, -1, 2))]
    pair = jnp.where(y == 0, a1[:ROWS], jnp.where(y == 2, a2[:ROWS], a3[:ROWS]))
    vec = jnp.stack([vec, a2[ROWS:], a3[ROWS:], a1[ROWS:]])[:, :3]
    vec = lax.dynamic_slice_in_dim(jnp.concatenate([vec, vec]), (4 - y) % 4, 4, 0)
    sent = jnp.concatenate([pair, vec.reshape(12, JC), query_w[0, :4]], 0)
    pair_w = exchange(jnp.broadcast_to(sent, (DP,) + sent.shape), "dp")
    vec = pair_w[:, ROWS : ROWS + 12].astype(f32).reshape(DP, 4, 3, 2, HEAD)[..., :40]
    vec = vec[:, :, 0] + vec[:, :, 1] + vec[:, :, 2]
    vec = vec.reshape(-1)

    gain_first, gain_second = vec[None, :D], vec[None, D : 2 * D]
    key_start = JC * KEY_AT + HEAD * (jnp.minimum(mp, KEY_AT - 1) // 3)
    starts = ((JC * mp, JC), (key_start, HEAD), (key_start + JC, HEAD))
    bias = jnp.concatenate(
        [lax.dynamic_slice_in_dim(vec, 2 * D + start, size, 0) for start, size in starts]
    )[None]

    cosine, sine = tables()
    back, back_t, back_part, tok_part = whole(
        prepare,
        [((T, D), bf16), ((D, T), bf16), ((PART, D), bf16), ((PART, D), bf16)],
        [ids, cotangent[0], tok],
    )
    normed, heads, att_sent, lse, joint_w = whole(
        attend,
        [
            ((T, D), bf16), ((T, 2 * JC), bf16), ((MP, HALF, JC), bf16),
            ((T, JC), f32), ((D, 2 * JC), bf16),
        ],
        [ids, tok, gain_first, bias, cosine, sine, query_w, pair_w],
        after=[back],
    )
    att_near = exchange(att_sent, "mp")
    att_far = swap_core(att_near)
    mixer_near = gather(shift_y, query_w[:, ROWS:])
    mixer_far = [swap_core(v) for v in mixer_near]
    hidden_part, normed_near, rows_w = whole(
        mix,
        [((PART, D), f32), ((HALF, D), bf16), ((JC, D), bf16)],
        [ids, att_near] + mixer_near + mixer_far + [tok, gain_second],
        scratch=[
            pltpu.VMEM((HALF, D), f32), pltpu.VMEM((HALF, D), bf16), pltpu.VMEM((D, D), bf16),
        ],
    )
    normed_far = swap_core(normed_near)

    def columns(n):
        return pl.BlockSpec((n, 256), lambda i: (0, i))

    def fixed(shape):
        return pl.BlockSpec(shape, lambda i: (0,) * len(shape))

    block = pl.BlockSpec((DP, 3, ROWS, 256), lambda i: (0, 0, 0, i))
    act, gate_grad, up_grad, ff_grads = pl.pallas_call(
        gated,
        grid=(pl.cdiv(FP, 256),),
        out_shape=[jax.ShapeDtypeStruct((T, FP), bf16)] * 3
        + [jax.ShapeDtypeStruct((DP, 3, ROWS, FP), bf16)],
        in_specs=[fixed((HALF, D)), fixed((HALF, D)), fixed((T, D)), fixed((D, T)), block],
        out_specs=[columns(T)] * 3 + [block],
        scratch_shapes=[pltpu.VMEM((D, T), bf16)],
        compiler_params=pltpu.CompilerParams(vmem_limit_bytes=60 * MiB),
        cost_estimate=SMALL,
    )(normed_near, normed_far, back, back_t, ff)
    ff_shard = lax.psum_scatter(ff_grads, "dp", scatter_dimension=0, tiled=False)

    near, far = pl.pallas_call(
        spread,
        grid=(2,),
        out_shape=[jax.ShapeDtypeStruct((HALF, D), bf16)] * 2,
        in_specs=[fixed((T, FP))] * 2
        + [pl.BlockSpec((DP // 2, 2, ROWS, FP), lambda i: (i, 0, 0, 0))],
        out_specs=[pl.BlockSpec((HALF, 768), lambda i: (0, i))] * 2,
        compiler_params=pltpu.CompilerParams(vmem_limit_bytes=60 * MiB),
        cost_estimate=SMALL,
    )(gate_grad, up_grad, ff)

    def half_sum(body, pairs, after=()):
        shape = (PART, D) if len(pairs) == 1 else (len(pairs), PART, D)
        given = [v for near, far in pairs for v in (near, swap_core(far))]
        own, *parts = whole(
            body, [(shape, f32)] + [(shape, bf16)] * 3, [ids] + given, after=after, limit=16
        )
        return [own] + [shift_y(v, k) for v, k in zip(parts, (1, -1, 2))]

    normed_second_parts = half_sum(halve, [(near, far)])
    out_near, out_far = pl.pallas_call(
        spread_out,
        grid=(2,),
        out_shape=[jax.ShapeDtypeStruct((HALF, D), bf16)] * 2,
        in_specs=[
            fixed((T, FP)),
            pl.BlockSpec((DP // 2, 1, ROWS, FP), lambda i: (i, 2, 0, 0)),
        ],
        out_specs=[pl.BlockSpec((HALF, 768), lambda i: (0, i))] * 2,
        compiler_params=pltpu.CompilerParams(vmem_limit_bytes=60 * MiB),
        cost_estimate=SMALL,
    )(act, ff)
    hidden_grad, low, gain_second_part = whole(
        hidden_back,
        [((PART, D), f32), ((PART, D), bf16), ((1, D), f32)],
        [ids] + normed_second_parts + [hidden_part, back_part, gain_second],
        after=[out_far],
        limit=8,
    )
    low_near = jnp.stack(gather(shift_y, low))
    low_far = swap_core(low_near)
    heads_grad, hidden_low, input_near, input_far, chunks = whole(
        back_to_input,
        [
            ((T, 2 * JC), bf16), ((T, 2 * MC), bf16), ((HALF, D), bf16), ((HALF, D), bf16),
            ((MP, T + 2 * DP, HEAD), bf16),
        ],
        [ids, low_near, low_far, rows_w, heads, lse, cosine, sine, joint_w, tok, gain_second_part],
        scratch=[
            pltpu.VMEM((T, D), bf16),
            pltpu.VMEM((T, JC), bf16),
            pltpu.VMEM((T, HEAD), f32),
            pltpu.VMEM((T, HEAD), f32),
            pltpu.VMEM((1, D), f32),
            pltpu.VMEM((1, DP * MP * 40), f32),
            pltpu.VMEM((DP, MP * 40), f32),
        ],
    )
    moved = exchange(chunks, "mp")
    (mixer_parts,) = whole(
        weigh_mixer,
        [((DP, ROWS, MC), bf16)],
        [ids, att_near, att_far, hidden_low],
    )
    (joint_parts,) = whole(
        weigh_joint,
        [((DP, ROWS + 8, JC + MC), bf16)],
        [ids, normed, heads_grad, moved, mixer_parts],
    )
    joint_shard, mixer_shard, vector_shard, squares = whole(
        settle_grads,
        [((ROWS, JC), f32), ((ROWS, MC), f32), ((1, HEAD), f32), ((DP * MP, 1, HEAD), f32)],
        [ids, exchange(joint_parts, "dp"), ff_shard],
    )

    squares = exchange(squares, ("dp", "mp"))

    parts = half_sum(
        halve_two, [(out_near, out_far), (input_near, input_far)], after=[joint_parts]
    )
    (done,) = whole(
        finish,
        [((2, PART, D), bf16)],
        [ids] + parts + [hidden_part, tok_part, hidden_grad, gain_first],
        limit=8,
    )
    (done_near,) = whole(
        pile, [((4, 2, PART, D), bf16)], [ids] + gather(shift_y, done), after=[squares], limit=8
    )
    done_far = swap_core(done_near)
    output, input_grad = whole(settle, [((1, T, D), f32)] * 2, [ids, done_near, done_far])

    matrices = [joint_weight, joint_moment, joint_square]
    matrices += [mixer_weight, mixer_moment, mixer_square]
    matrices += [expand_weight, expand_moment, expand_square]
    matrices += [v.T for v in (shrink_weight, shrink_moment, shrink_square)]
    matrices += [v[None] for v in (vector_params, vector_moment, vector_square)]
    def third(shape):
        n = len(shape)
        if shape[-2] != ROWS:
            return pl.BlockSpec(shape, lambda i: (0,) * n)
        return pl.BlockSpec(
            shape[:-2] + (ROWS // 3, shape[-1]), lambda i: (0,) * (n - 2) + (i, 0)
        )

    given = [squares, joint_shard, mixer_shard, ff_shard, vector_shard] + matrices
    made = [(1, HEAD)] + [v.shape for v in matrices]
    norm, *new = pl.pallas_call(
        update,
        grid=(3,),
        out_shape=[jax.ShapeDtypeStruct(shape, f32) for shape in made],
        in_specs=[third(v.shape) for v in given],
        out_specs=[third(shape) for shape in made],
        compiler_params=pltpu.CompilerParams(vmem_limit_bytes=60 * MiB),
        cost_estimate=SMALL,
    )(*given)
    new[9:12] = [v.T for v in new[9:12]]
    new[12:] = [v[0] for v in new[12:]]
    return (output, input_grad, norm[0, 0], *new)


def solution(mesh):
    row = P("dp", None, None)
    matrix = [P("dp", "mp")] * 6 + [P(None, "dp", "mp")] * 3 + [P("mp", "dp")] * 3
    vector = [P(("dp", "mp"))] * 3
    return jax.shard_map(
        body,
        mesh=mesh,
        in_specs=tuple([row, P("dp"), row] + matrix + vector),
        out_specs=tuple([row, row, P()] + matrix + vector),
        check_vma=False,
    )
```

```python
import jax
import jax.numpy as jnp
import numpy as np
from jax import lax
from jax.experimental import pallas as pl
from jax.experimental.pallas import tpu as pltpu
from jax.sharding import PartitionSpec as P

QUERY_HEADS = 12
KEY_VALUE_HEADS = 2
HEAD = 128
STEP = 5
EPS_NORM = 1e-06
ROPE_BASE = 1000000.0
MAX_NORM = 1.0
BETA_ONE = 0.9
BETA_TWO = 0.95
ADAM_EPS = 1e-08
DECAY = 0.1
RATE_MATRIX = 0.06
RATE_VECTOR = 0.8
MASKED = -1e30

T = 512
HALF = 256
PART = 64
D = 1536
FF = 1120
FP = 1152
DP = 16
MP = 8
ROWS = D // DP
JC = 256
MC = 192
KEY_AT = 6
SCALE = HEAD ** (-0.5)

f32 = jnp.float32
bf16 = jnp.bfloat16
VM = pl.BlockSpec(memory_space=pltpu.VMEM)
SM = pl.BlockSpec(memory_space=pltpu.SMEM)
MiB = 1 << 20
SMALL = pl.CostEstimate(flops=1, bytes_accessed=1, transcendentals=0)


def shift_y(v, k):
    return lax.ppermute(v, "mp", [(i, (i + 2 * k) % MP) for i in range(MP)])


def from_last_chip(v, k):
    return lax.ppermute(v, "mp", [(i, (i + 2 * k) % MP) for i in (MP - 2, MP - 1)])


def to_last_chip(v, y):
    return lax.ppermute(v, "mp", [(2 * y + c, MP - 2 + c) for c in range(2)])


def swap_core(v):
    return lax.ppermute(v, "mp", [(i, i ^ 1) for i in range(MP)])


def exchange(v, axis):
    return lax.all_to_all(v, axis, split_axis=0, concat_axis=0, tiled=True)


RELATIVE = (0, -1, 1, 2)


def gather(shift, v):
    return [v, shift(v, 1), shift(v, -1), shift(v, 2)]


def nn(a, b):
    return lax.dot_general(a, b, (((1,), (0,)), ((), ())), preferred_element_type=f32)


def nt(a, b):
    return lax.dot_general(a, b, (((1,), (1,)), ((), ())), preferred_element_type=f32)


def tn(a, b):
    return lax.dot_general(a, b, (((0,), (0,)), ((), ())), preferred_element_type=f32)


def whole(body, outs, args, scratch=(), limit=60, after=()):
    n = len(args)

    def bare(*refs):
        body(*refs[:n], *refs[n + len(after) :])

    return pl.pallas_call(
        bare,
        out_shape=[jax.ShapeDtypeStruct(s, d) for s, d in outs],
        in_specs=[SM] + [VM] * (n - 1) + [pl.BlockSpec(memory_space=pl.ANY)] * len(after),
        out_specs=[VM] * len(outs),
        scratch_shapes=list(scratch),
        compiler_params=pltpu.CompilerParams(vmem_limit_bytes=limit * MiB),
        cost_estimate=SMALL,
    )(*args, *after)


def at(start, size, step):
    return pl.ds(pl.multiple_of(start, step), size)


def prepare(ids, cotangent, tok, back, back_t, back_part, tok_part):
    length, y, c = ids[0], ids[3], ids[4]
    for h in range(2):
        start = HALF * ((c + h) % 2)
        t = lax.broadcasted_iota(jnp.int32, (HALF, 1), 0) + start
        v = cotangent[at(start, HALF, HALF), :]
        v = jnp.where(t < length, v, jnp.zeros_like(v))
        back[HALF * h : HALF * (h + 1), :] = v
        back_t[:, HALF * h : HALF * (h + 1)] = v.T
    back_part[...] = back[at(PART * y, PART, PART), :]
    tok_part[...] = tok[at(HALF * c + PART * y, PART, PART), :]


def kept(i, n, length):
    t = lax.broadcasted_iota(jnp.int32, (128, n), 0) + 128 * i
    s = lax.broadcasted_iota(jnp.int32, (128, n), 1)
    return (s <= t) & (s < length)


def attend(
    ids, tok, gain, bias, cosine, sine, query_w, pair_w,
    normed, heads, out, lse, w,
):
    w[:, :JC] = query_w[:, :ROWS, :].reshape(D, JC)
    w[:, JC:] = pair_w[:, :ROWS, :].reshape(D, JC)

    @pl.loop(0, T // 128)
    def _(i):
        rows = at(i * 128, 128, 128)
        x = tok[rows, :].astype(f32)
        s = lax.rsqrt(jnp.mean(x * x, -1, keepdims=True) + EPS_NORM)
        n = (x * s * gain[...]).astype(bf16)
        normed[rows, :] = n
        j = nn(n, w[...]) + bias[...]
        for h in range(4):
            cols = slice(HEAD * h, HEAD * (h + 1))
            u = j[:, cols]
            if h < 3:
                u = u * cosine[rows, :] + pltpu.roll(u, HEAD // 2, 1) * sine[rows, :]
            heads[rows, cols] = u.astype(bf16)

    for h in range(2):
        for i in range(4):
            n = 128 * (i + 1)
            q = heads[128 * i : n, HEAD * h : HEAD * (h + 1)]
            k, v = heads[:n, 2 * HEAD : 3 * HEAD], heads[:n, 3 * HEAD :]
            s = jnp.where(kept(i, n, ids[0]), nt(q, k) * SCALE, MASKED)
            m = jnp.max(s, -1, keepdims=True)
            e = jnp.exp(s - m)
            total = jnp.sum(e, -1, keepdims=True)
            o = nn((e / total).astype(bf16), v).astype(bf16)
            lse[128 * i : n, HEAD * h : HEAD * (h + 1)] = jnp.broadcast_to(
                m + jnp.log(total), (128, HEAD)
            )
            at_row = 128 * (i % 2)
            for y in range(4):
                out[2 * y + i // 2, at_row : at_row + 128, HEAD * h : HEAD * (h + 1)] = o


def mix(
    ids, att, a0, a1, a2, a3, b0, b1, b2, b3, tok, gain,
    hidden_part, normed, rows_w, hidden, side, mixer,
):
    y, c = ids[3], ids[4]
    for j in range(KEY_AT):
        side[:, JC * j : JC * (j + 1)] = att[j]
    mine = at(HALF * c, HALF, HALF)
    for e, a, b in zip(RELATIVE, (a0, a1, a2, a3), (b0, b1, b2, b3)):
        cols = at(384 * lax.rem(y + e + 4, 4), 384, 384)
        first = 384 * lax.rem(y + e + 4, 4)
        left, right = at(first, JC, 128), at(first + JC, HEAD, 128)
        for d in range(DP):
            for half, v in ((c, a), (1 - c, b)):
                row = ROWS * d + 48 * half
                mixer[at(row, 48, 16), left] = v[d, :48, :]
                mixer[at(row, 32, 16), right] = v[d, 48:80, :HEAD]
                mixer[at(row + 32, 16, 16), right] = v[d, 48:64, HEAD:]
        hidden[:, cols] = nn(side[...], mixer[:, cols]) + tok[mine, cols].astype(f32)
    hidden_part[...] = hidden[at(PART * y, PART, PART), :]
    rows_w[...] = mixer[at(JC * jnp.minimum(ids[2], KEY_AT - 1), JC, JC), :]
    for r in range(0, HALF, 64):
        v = hidden[r : r + 64, :]
        s = lax.rsqrt(jnp.mean(v * v, -1, keepdims=True) + EPS_NORM)
        normed[r : r + 64, :] = (v * s * gain[...]).astype(bf16)


def gated(near, far, back, back_t, w, act, gate_grad, up_grad, grads, near_t):
    @pl.when(pl.program_id(0) == 0)
    def _():
        near_t[:, :HALF] = near[...].T
        near_t[:, HALF:] = far[...].T

    gate_w, up_w, down_w = [w[:, m].reshape(D, 256) for m in range(3)]
    for r, normed in ((0, near), (HALF, far)):
        rows = slice(r, r + HALF)
        g = nn(normed[...], gate_w)
        u = nn(normed[...], up_w)
        a = nn(back[rows, :], down_w)
        sigma = 1.0 / (1.0 + jnp.exp(-g))
        swished = g * sigma
        act[rows, :] = (swished * u).astype(bf16)
        gate_grad[rows, :] = (a * u * sigma * (1.0 + g * (1.0 - sigma))).astype(bf16)
        up_grad[rows, :] = (a * swished).astype(bf16)
    for m, (left, right) in enumerate(((near_t, gate_grad), (near_t, up_grad), (back_t, act))):
        for r in range(4):
            part = nn(left[384 * r : 384 * (r + 1), :], right[...]).astype(bf16)
            grads[4 * r : 4 * (r + 1), m] = part.reshape(4, ROWS, 256)


def spread(gate_grad, up_grad, w, near, far):
    gate_w, up_w = [w[:, m].reshape(768, FP) for m in range(2)]
    for b in range(3):
        cols = slice(256 * b, 256 * (b + 1))
        part = nt(gate_grad[...], gate_w[cols]) + nt(up_grad[...], up_w[cols])
        near[:, cols] = part[:HALF].astype(bf16)
        far[:, cols] = part[HALF:].astype(bf16)


def spread_out(act, w, near, far):
    down_w = w[:, 0].reshape(768, FP)
    for b in range(3):
        cols = slice(256 * b, 256 * (b + 1))
        part = nt(act[...], down_w[cols])
        near[:, cols] = part[:HALF].astype(bf16)
        far[:, cols] = part[HALF:].astype(bf16)


def halve(ids, near, other, own, p1, p2, p3):
    y = ids[3]
    for k, out in ((0, own), (1, p1), (3, p2), (2, p3)):
        rows = at(PART * lax.rem(y + k, 4), PART, PART)
        out[...] = (near[rows, :].astype(f32) + other[rows, :].astype(f32)).astype(out.dtype)


def halve_two(ids, near_a, other_a, near_b, other_b, own, p1, p2, p3):
    for n, (near, other) in enumerate(((near_a, other_a), (near_b, other_b))):
        halve(ids, near, other, own.at[n], p1.at[n], p2.at[n], p3.at[n])


def summed(own, parts):
    total = own[...]
    for part in parts:
        total += part[...].astype(f32)
    return total


def hidden_back(ids, own, a1, a2, a3, hidden, back, gain, grad, low, gain_part):
    h = hidden[...]
    g = summed(own, (a1, a2, a3))
    scale = lax.rsqrt(jnp.mean(h * h, -1, keepdims=True) + EPS_NORM)
    gain_part[...] = jnp.sum(g * h * scale, 0, keepdims=True)
    v = back[...].astype(f32) + norm_back(h, scale, gain[...], g)
    grad[...] = v
    low[...] = v.astype(bf16)


def finish(ids, own, a1, a2, a3, hidden, tok, grad, gain, done):
    length, y, c = ids[0], ids[3], ids[4]
    o, g = [summed(own.at[n], [a.at[n] for a in (a1, a2, a3)]) for n in range(2)]
    t = lax.broadcasted_iota(jnp.int32, (PART, 1), 0) + HALF * c + PART * y
    done[0] = jnp.where(t < length, o + hidden[...], 0.0).astype(bf16)
    x = tok[...].astype(f32)
    scale = lax.rsqrt(jnp.mean(x * x, -1, keepdims=True) + EPS_NORM)
    done[1] = (grad[...] + norm_back(x, scale, gain[...], g)).astype(bf16)


def attend_back(
    ids, near, far, rows_w, heads, lse, cosine, sine,
    grads, window, own_kind, other_kind, low, att_grad, key_grad, value_grad,
):
    length, y, c = ids[0], ids[3], ids[4]
    for k, e in enumerate(RELATIVE):
        place = PART * lax.rem(y + e + 4, 4)
        low[at(HALF * c + place, PART, PART), :] = near[k]
        low[at(HALF * (1 - c) + place, PART, PART), :] = far[k]
    window[...] = low[:, at(384 * y, 384, 384)]
    has_heads = (ids[2] < KEY_AT).astype(f32)
    att_grad[...] = (nt(low[...], rows_w[...]) * has_heads).astype(bf16)
    key_grad[...] = jnp.zeros_like(key_grad)
    value_grad[...] = jnp.zeros_like(value_grad)
    for h in range(2):
        cols = slice(HEAD * h, HEAD * (h + 1))
        for i in range(4):
            n = 128 * (i + 1)
            rows = slice(128 * i, n)
            q = heads[rows, cols]
            k, v = heads[:n, 2 * HEAD : 3 * HEAD], heads[:n, 3 * HEAD :]
            o = att_grad[rows, cols]
            s = nt(q, k) * SCALE
            p = jnp.where(kept(i, n, length), jnp.exp(s - lse[rows, HEAD * h : HEAD * h + 1]), 0.0)
            d = nt(o, v)
            g = (p * (d - jnp.sum(p * d, -1, keepdims=True))).astype(bf16)
            value_grad[:n, :] += tn(p.astype(bf16), o)
            key_grad[:n, :] += tn(g, q)
            dq = nn(g, k) * SCALE
            dq = dq * cosine[rows, :] - pltpu.roll(dq, HEAD // 2, 1) * sine[rows, :]
            grads[rows, cols] = dq.astype(bf16)
    dk = key_grad[...] * SCALE
    dk = dk * cosine[...] - pltpu.roll(dk, HEAD // 2, 1) * sine[...]
    grads[:, 2 * HEAD : 3 * HEAD] = dk.astype(bf16)
    grads[:, 3 * HEAD :] = value_grad[...].astype(bf16)
    k, v = grads[:, 2 * HEAD : 3 * HEAD], grads[:, 3 * HEAD :]

    @pl.when(c == 0)
    def _():
        own_kind[...] = k
        other_kind[...] = v

    @pl.when(c != 0)
    def _():
        own_kind[...] = v
        other_kind[...] = k


def joint_back(
    ids, grads, w, tok, second_part,
    near, far, chunks, gain_part, vec, blocks,
):
    g = grads[...]
    gain_part[...] = jnp.zeros_like(gain_part)
    for r in range(0, T, 128):
        rows = slice(r, r + 128)
        back = nt(g[rows], w[...])
        half, place = r // HALF, slice(r % HALF, r % HALF + 128)
        moves = back.astype(bf16)

        @pl.when(ids[4] == half)
        def _():
            near[place, :] = moves

        @pl.when(ids[4] != half)
        def _():
            far[place, :] = moves

        x = tok[rows, :].astype(f32)
        s = lax.rsqrt(jnp.mean(x * x, -1, keepdims=True) + EPS_NORM)
        gain_part[...] += jnp.sum(back * x * s, 0, keepdims=True)
    vec[...] = jnp.zeros_like(vec)
    vec[:, :D] = gain_part[...]
    vec[:, D : 2 * D] = second_part[...]
    bias = jnp.sum(g.astype(f32), 0, keepdims=True)
    head_at = jnp.minimum(ids[2], KEY_AT - 1)
    key_start = 2 * D + JC * KEY_AT + HEAD * lax.div(head_at, 3)
    vec[:, at(2 * D + JC * head_at, JC, JC)] = bias[:, :JC]
    vec[:, at(key_start, HEAD, HEAD)] = bias[:, JC : JC + HEAD]
    vec[:, at(key_start + JC, HEAD, HEAD)] = bias[:, JC + HEAD :]
    for d in range(DP):
        blocks[d : d + 1, :] = vec[:, 320 * d : 320 * (d + 1)]
    for m in range(MP):
        piece = blocks[:, 40 * m : 40 * (m + 1)]
        piece = jnp.concatenate([piece, jnp.zeros((DP, HEAD - 40), f32)], 1)
        high = piece.astype(bf16)
        chunks[m, :DP, :] = high
        chunks[m, DP:, :] = (piece - high.astype(f32)).astype(bf16)


def back_to_input(
    ids, near_low, far_low, rows_w, heads, lse, cosine, sine, w, tok, second_part,
    grads, window, own_kind, other_kind, near, far, chunks,
    low, att_grad, key_grad, value_grad, gain_part, vec, blocks,
):
    attend_back(
        ids, near_low, far_low, rows_w, heads, lse, cosine, sine,
        grads, window, own_kind, other_kind, low, att_grad, key_grad, value_grad,
    )
    joint_back(ids, grads, w, tok, second_part, near, far, chunks, gain_part, vec, blocks)


def group_parts(ids, own, other, both, left, right):
    own_group = lax.div(jnp.minimum(ids[2], KEY_AT - 1), 3)
    partner = ids[2] + 1 - 2 * ids[4]
    other_group = lax.div(jnp.minimum(partner, KEY_AT - 1), 3)
    a, b = own[...].astype(f32), other[...].astype(f32)
    for g, out in ((0, left), (1, right)):
        part = a * (own_group == g).astype(f32) + b * (other_group == g).astype(f32)
        out[...] = part.astype(bf16)
        both[:, HEAD * g : HEAD * (g + 1)] = part.astype(bf16)


def weigh_joint(ids, normed, grads, left, right, both, moved, mixer_parts, parts):
    pair = jnp.concatenate([left[...].astype(f32), right[...].astype(f32)], 1)
    pair = pair + both[...].astype(f32)
    own = grads[:, :JC].astype(f32)
    g = jnp.where(ids[2] < KEY_AT, own, pair).astype(bf16)
    for r in range(4):
        cols = slice(384 * r, 384 * (r + 1))
        part = tn(normed[:, cols], g).astype(bf16)
        parts[4 * r : 4 * (r + 1), :ROWS, :JC] = part.reshape(4, ROWS, JC)
    parts[:, :ROWS, JC:] = mixer_parts[...]
    vec = moved[0].astype(f32)
    for j in range(1, MP):
        vec += moved[j].astype(f32)
    vec = vec[:DP] + vec[DP:]
    high = vec.astype(bf16).astype(f32)
    rest = jnp.zeros((8, MC), bf16)
    for d in range(DP):
        parts[d, ROWS:, :HEAD] = jnp.broadcast_to(high[d : d + 1], (8, HEAD)).astype(bf16)
        low = (vec - high)[d : d + 1]
        parts[d, ROWS:, HEAD:JC] = jnp.broadcast_to(low, (8, HEAD)).astype(bf16)
        parts[d, ROWS:, JC:] = rest


def weigh_mixer(ids, near, far, low, parts):
    c = ids[4]

    def own_columns(half):
        v = low[at(HALF * half, HALF, HALF), :].astype(f32)
        return jnp.where(c == 0, v[:, :MC], v[:, MC:]).astype(bf16)

    mine, other = own_columns(c), own_columns(1 - c)
    for j in range(KEY_AT):
        part = (tn(near[j], mine) + tn(far[j], other)).astype(bf16)
        start = JC * j
        while start < JC * (j + 1):
            stop = min((start // ROWS + 1) * ROWS, JC * (j + 1))
            first = start % ROWS
            parts[start // ROWS, first : first + stop - start, :] = part[
                start - JC * j : stop - JC * j
            ]
            start = stop


def settle_grads(ids, moved, ff, joint, mixer, vector, squares):
    total = moved[0].astype(f32)
    for d in range(1, DP):
        total += moved[d].astype(f32)
    joint[...] = total[:ROWS, :JC]
    mixer[...] = total[:ROWS, JC:]
    vec = total[ROWS : ROWS + 1, :HEAD] + total[ROWS : ROWS + 1, HEAD:JC]
    vector[...] = vec
    total = total[:ROWS]
    total = jnp.sum(total * total) + jnp.sum(vec * vec)
    for m in range(3):
        v = ff[m].astype(f32)
        total += jnp.sum(v * v)
    squares[...] = jnp.full(squares.shape, total, f32)


def update(
    squares, joint_grad, mixer_grad, ff_grad, vector_grad,
    joint_w, joint_m, joint_v, mixer_w, mixer_m, mixer_v, expand_w, expand_m, expand_v,
    shrink_w, shrink_m, shrink_v, vector_w, vector_m, vector_v,
    norm_out, joint_wn, joint_mn, joint_vn, mixer_wn, mixer_mn, mixer_vn,
    expand_wn, expand_mn, expand_vn, shrink_wn, shrink_mn, shrink_vn,
    vector_wn, vector_mn, vector_vn,
):
    norm = jnp.sqrt(jnp.sum(squares[:, 0, :], 0, keepdims=True))
    norm_out[...] = norm
    clip = jnp.minimum(1.0, MAX_NORM / (norm[:, :1] + 1e-06))

    def step(grad, before, after, rate, decay, part=Ellipsis):
        w, m, v = [ref[part] for ref in before]
        results = adam_step(w, clip * grad, m, v, rate, decay)
        for ref, new in zip(after, results):
            ref[part] = new

    step(
        joint_grad[...], (joint_w, joint_m, joint_v), (joint_wn, joint_mn, joint_vn),
        RATE_MATRIX, DECAY,
    )
    step(
        mixer_grad[...], (mixer_w, mixer_m, mixer_v), (mixer_wn, mixer_mn, mixer_vn),
        RATE_MATRIX, DECAY,
    )
    for m in range(2):
        step(
            ff_grad[m, :, :FF].astype(f32),
            (expand_w, expand_m, expand_v), (expand_wn, expand_mn, expand_vn),
            RATE_MATRIX, DECAY, m,
        )
    step(
        ff_grad[2, :, :FF].astype(f32),
        (shrink_w, shrink_m, shrink_v), (shrink_wn, shrink_mn, shrink_vn),
        RATE_MATRIX, DECAY,
    )
    step(
        vector_grad[:, :40], (vector_w, vector_m, vector_v), (vector_wn, vector_mn, vector_vn),
        RATE_VECTOR, 0.0,
    )


def write_half(ids, half, pieces, outs, rows, sems):
    for k, e in enumerate(RELATIVE):
        place = at(PART * lax.rem(ids[3] + e + 4, 4), PART, PART)
        for n in range(2):
            rows[n, place, :] = pieces[k][n].astype(f32)
    copies = [
        pltpu.make_async_copy(rows.at[n], out.at[0, at(HALF * half, HALF, HALF)], sems.at[n])
        for n, out in enumerate(outs)
    ]
    for copy in copies:
        copy.start()
    for copy in copies:
        copy.wait()


def settle_near(ids, p0, p1, p2, p3, output, input_grad, token, rows, sems):
    token[...] = jnp.zeros_like(token)
    write_half(ids, ids[4], (p0, p1, p2, p3), (output, input_grad), rows, sems)


def settle_far(ids, far, _a, _b, output, input_grad, rows, sems):
    pieces = [far.at[k] for k in range(4)]
    write_half(ids, 1 - ids[4], pieces, (output, input_grad), rows, sems)


def pile(ids, p0, p1, p2, p3, out):
    for k, p in enumerate((p0, p1, p2, p3)):
        out[k] = p[...]


def norm_back(v, scale, gain, grad):
    scaled = gain * grad
    return scale * scaled - v * scale * scale * scale * jnp.mean(scaled * v, -1, keepdims=True)


def adam_step(weight, grad, moment, square, rate, decay):
    moment_next = BETA_ONE * moment + (1.0 - BETA_ONE) * grad
    square_next = BETA_TWO * square + (1.0 - BETA_TWO) * grad * grad
    first_hat = moment_next * (1.0 / (1.0 - BETA_ONE**STEP))
    second_hat = square_next * (1.0 / (1.0 - BETA_TWO**STEP))
    weight_next = weight - rate * (first_hat / (jnp.sqrt(second_hat) + ADAM_EPS) + decay * weight)
    return (weight_next, moment_next, square_next)


def tables():
    freq = np.float32(ROPE_BASE) ** (-np.arange(0, HEAD, 2, dtype=np.float32) / np.float32(HEAD))
    angle = np.arange(T, dtype=np.float32)[:, None] * freq.astype(np.float32)[None, :]
    cosine, sine = np.cos(angle), np.sin(angle)
    return (
        np.concatenate([cosine, cosine], -1).astype(np.float32),
        np.concatenate([-sine, sine], -1).astype(np.float32),
    )


def split_low(v):
    high = lax.reduce_precision(v, 8, 7)
    middle = lax.reduce_precision(v - high, 8, 7)
    return [part.astype(bf16) for part in (high, middle, v - high - middle)]


def body(
    tokens, lengths, cotangent,
    joint_weight, joint_moment, joint_square,
    mixer_weight, mixer_moment, mixer_square,
    expand_weight, expand_moment, expand_square,
    shrink_weight, shrink_moment, shrink_square,
    vector_params, vector_moment, vector_square,
):
    dp, mp = lax.axis_index("dp"), lax.axis_index("mp")
    y, c = mp // 2, mp % 2
    tok, length = tokens[0], lengths[0]
    ids = jnp.stack([length, dp, mp, y, c]).astype(jnp.int32)

    stack = jnp.concatenate(
        [expand_weight.astype(bf16), shrink_weight.T.astype(bf16)[None]], 0
    )
    stack = jnp.pad(stack, ((0, 0), (0, 0), (0, FP - FF)))
    ff = lax.all_gather(stack, "dp", axis=0, tiled=False)

    low = jnp.concatenate([joint_weight.astype(bf16), mixer_weight.astype(bf16)], 1)
    vec = jnp.pad(jnp.stack(split_low(vector_params)), ((0, 13), (0, JC + MC - 40)))
    low = jnp.concatenate([low, vec], 0)
    other = swap_core(low)
    first, second = jnp.where(c == 0, low, other), jnp.where(c == 0, other, low)
    pairs = [
        jnp.concatenate([first[:ROWS, cols], second[:ROWS, cols]], 1)
        for cols in (slice(0, HEAD), slice(HEAD, JC))
    ]
    chip = jnp.concatenate([first[:ROWS, JC:], second[:ROWS, JC:]], 1)
    chip = lax.dynamic_slice_in_dim(chip, 48 * c, 48, 0)
    rest = jnp.concatenate([chip[:32, JC:], jnp.pad(chip[32:, JC:], ((0, 16), (0, 0)))], 1)
    sent = jnp.concatenate([low[:ROWS, :JC], chip[:, :JC], rest], 0)
    query_w = exchange(jnp.broadcast_to(sent, (DP,) + sent.shape), "dp")
    vec = jnp.concatenate([first[ROWS:, :HEAD], second[ROWS:, :HEAD]], 1)
    sends = [pairs[0], pairs[1], jnp.where(c == 0, pairs[0], pairs[1])]
    sends = [jnp.concatenate([v, vec], 0) for v in sends]
    a1, a2, a3 = [shift_y(v, k) for v, k in zip(sends, (1, -1, 2))]
    pair = jnp.where(y == 0, a1[:ROWS], jnp.where(y == 2, a2[:ROWS], a3[:ROWS]))
    vec = jnp.stack([vec, a2[ROWS:], a3[ROWS:], a1[ROWS:]])[:, :3]
    vec = lax.dynamic_slice_in_dim(jnp.concatenate([vec, vec]), (4 - y) % 4, 4, 0)
    sent = jnp.concatenate([pair, vec.reshape(12, JC), query_w[0, :4]], 0)
    pair_w = exchange(jnp.broadcast_to(sent, (DP,) + sent.shape), "dp")
    vec = pair_w[:, ROWS : ROWS + 12].astype(f32).reshape(DP, 4, 3, 2, HEAD)[..., :40]
    vec = vec[:, :, 0] + vec[:, :, 1] + vec[:, :, 2]
    vec = vec.reshape(-1)

    gain_first, gain_second = vec[None, :D], vec[None, D : 2 * D]
    key_start = JC * KEY_AT + HEAD * (jnp.minimum(mp, KEY_AT - 1) // 3)
    starts = ((JC * mp, JC), (key_start, HEAD), (key_start + JC, HEAD))
    bias = jnp.concatenate(
        [lax.dynamic_slice_in_dim(vec, 2 * D + start, size, 0) for start, size in starts]
    )[None]

    cosine, sine = tables()
    back, back_t, back_part, tok_part = whole(
        prepare,
        [((T, D), bf16), ((D, T), bf16), ((PART, D), bf16), ((PART, D), bf16)],
        [ids, cotangent[0], tok],
    )
    normed, heads, att_sent, lse, joint_w = whole(
        attend,
        [
            ((T, D), bf16), ((T, 2 * JC), bf16), ((MP, HALF, JC), bf16),
            ((T, JC), f32), ((D, 2 * JC), bf16),
        ],
        [ids, tok, gain_first, bias, cosine, sine, query_w, pair_w],
        after=[back],
    )
    att_near = exchange(att_sent, "mp")
    att_far = swap_core(att_near)
    mixer_near = gather(shift_y, query_w[:, ROWS:])
    mixer_far = [swap_core(v) for v in mixer_near]
    hidden_part, normed_near, rows_w = whole(
        mix,
        [((PART, D), f32), ((HALF, D), bf16), ((JC, D), bf16)],
        [ids, att_near] + mixer_near + mixer_far + [tok, gain_second],
        scratch=[
            pltpu.VMEM((HALF, D), f32), pltpu.VMEM((HALF, D), bf16), pltpu.VMEM((D, D), bf16),
        ],
    )
    normed_far = swap_core(normed_near)

    def columns(n):
        return pl.BlockSpec((n, 256), lambda i: (0, i))

    def fixed(shape):
        return pl.BlockSpec(shape, lambda i: (0,) * len(shape))

    block = pl.BlockSpec((DP, 3, ROWS, 256), lambda i: (0, 0, 0, i))
    act, gate_grad, up_grad, ff_grads = pl.pallas_call(
        gated,
        grid=(pl.cdiv(FP, 256),),
        out_shape=[jax.ShapeDtypeStruct((T, FP), bf16)] * 3
        + [jax.ShapeDtypeStruct((DP, 3, ROWS, FP), bf16)],
        in_specs=[fixed((HALF, D)), fixed((HALF, D)), fixed((T, D)), fixed((D, T)), block],
        out_specs=[columns(T)] * 3 + [block],
        scratch_shapes=[pltpu.VMEM((D, T), bf16)],
        compiler_params=pltpu.CompilerParams(vmem_limit_bytes=60 * MiB),
        cost_estimate=SMALL,
    )(normed_near, normed_far, back, back_t, ff)
    ff_shard = lax.psum_scatter(ff_grads, "dp", scatter_dimension=0, tiled=False)

    near, far = pl.pallas_call(
        spread,
        grid=(2,),
        out_shape=[jax.ShapeDtypeStruct((HALF, D), bf16)] * 2,
        in_specs=[fixed((T, FP))] * 2
        + [pl.BlockSpec((DP // 2, 2, ROWS, FP), lambda i: (i, 0, 0, 0))],
        out_specs=[pl.BlockSpec((HALF, 768), lambda i: (0, i))] * 2,
        compiler_params=pltpu.CompilerParams(vmem_limit_bytes=60 * MiB),
        cost_estimate=SMALL,
    )(gate_grad, up_grad, ff)

    def half_sum(body, pairs, after=()):
        shape = (PART, D) if len(pairs) == 1 else (len(pairs), PART, D)
        given = [v for near, far in pairs for v in (near, swap_core(far))]
        own, *parts = whole(
            body, [(shape, f32)] + [(shape, bf16)] * 3, [ids] + given, after=after, limit=16
        )
        return [own] + [shift_y(v, k) for v, k in zip(parts, (1, -1, 2))]

    normed_second_parts = half_sum(halve, [(near, far)])
    out_near, out_far = pl.pallas_call(
        spread_out,
        grid=(2,),
        out_shape=[jax.ShapeDtypeStruct((HALF, D), bf16)] * 2,
        in_specs=[
            fixed((T, FP)),
            pl.BlockSpec((DP // 2, 1, ROWS, FP), lambda i: (i, 2, 0, 0)),
        ],
        out_specs=[pl.BlockSpec((HALF, 768), lambda i: (0, i))] * 2,
        compiler_params=pltpu.CompilerParams(vmem_limit_bytes=60 * MiB),
        cost_estimate=SMALL,
    )(act, ff)
    hidden_grad, low, gain_second_part = whole(
        hidden_back,
        [((PART, D), f32), ((PART, D), bf16), ((1, D), f32)],
        [ids] + normed_second_parts + [hidden_part, back_part, gain_second],
        after=[out_far],
        limit=8,
    )
    low_near = jnp.stack(gather(shift_y, low))
    low_far = swap_core(low_near)
    heads_grad, hidden_low, own_kind, other_kind, input_near, input_far, chunks = whole(
        back_to_input,
        [
            ((T, 2 * JC), bf16), ((T, 2 * MC), bf16), ((T, HEAD), bf16), ((T, HEAD), bf16),
            ((HALF, D), bf16), ((HALF, D), bf16), ((MP, 2 * DP, HEAD), bf16),
        ],
        [ids, low_near, low_far, rows_w, heads, lse, cosine, sine, joint_w, tok, gain_second_part],
        scratch=[
            pltpu.VMEM((T, D), bf16),
            pltpu.VMEM((T, JC), bf16),
            pltpu.VMEM((T, HEAD), f32),
            pltpu.VMEM((T, HEAD), f32),
            pltpu.VMEM((1, D), f32),
            pltpu.VMEM((1, DP * MP * 40), f32),
            pltpu.VMEM((DP, MP * 40), f32),
        ],
    )
    both, left, right = whole(
        group_parts,
        [((T, JC), bf16), ((T, HEAD), bf16), ((T, HEAD), bf16)],
        [ids, own_kind, swap_core(other_kind)],
        limit=8,
    )
    left, right, both = to_last_chip(left, 0), to_last_chip(right, 2), to_last_chip(both, 1)
    moved = exchange(chunks, "mp")
    (mixer_parts,) = whole(
        weigh_mixer,
        [((DP, ROWS, MC), bf16)],
        [ids, att_near, att_far, hidden_low],
    )
    (joint_parts,) = whole(
        weigh_joint,
        [((DP, ROWS + 8, JC + MC), bf16)],
        [ids, normed, heads_grad, left, right, both, moved, mixer_parts],
    )
    joint_shard, mixer_shard, vector_shard, squares = whole(
        settle_grads,
        [((ROWS, JC), f32), ((ROWS, MC), f32), ((1, HEAD), f32), ((DP * MP, 1, HEAD), f32)],
        [ids, exchange(joint_parts, "dp"), ff_shard],
    )

    squares = exchange(squares, ("dp", "mp"))

    parts = half_sum(
        halve_two, [(out_near, out_far), (input_near, input_far)], after=[joint_parts]
    )
    (done,) = whole(
        finish,
        [((2, PART, D), bf16)],
        [ids] + parts + [hidden_part, tok_part, hidden_grad, gain_first],
        limit=8,
    )
    done_parts = gather(shift_y, done)
    anywhere = pl.BlockSpec(memory_space=pl.ANY)
    results = [jax.ShapeDtypeStruct((1, T, D), f32)] * 2
    held = [pltpu.VMEM((2, HALF, D), f32), pltpu.SemaphoreType.DMA((2,))]
    *halves, token = pl.pallas_call(
        settle_near,
        out_shape=results + [jax.ShapeDtypeStruct((8, HEAD), f32)],
        in_specs=[SM] + [VM] * 4,
        out_specs=[anywhere] * 2 + [VM],
        scratch_shapes=held,
        compiler_params=pltpu.CompilerParams(vmem_limit_bytes=16 * MiB),
        cost_estimate=SMALL,
    )(ids, *done_parts)
    (done_near,) = whole(
        pile, [((4, 2, PART, D), bf16)], [ids] + done_parts, after=[squares, token], limit=8
    )
    output, input_grad = pl.pallas_call(
        settle_far,
        out_shape=results,
        in_specs=[SM, VM] + [anywhere] * 2,
        out_specs=[anywhere] * 2,
        input_output_aliases={2: 0, 3: 1},
        scratch_shapes=held,
        compiler_params=pltpu.CompilerParams(vmem_limit_bytes=16 * MiB),
        cost_estimate=SMALL,
    )(ids, swap_core(done_near), *halves)

    matrices = [joint_weight, joint_moment, joint_square]
    matrices += [mixer_weight, mixer_moment, mixer_square]
    matrices += [expand_weight, expand_moment, expand_square]
    matrices += [v.T for v in (shrink_weight, shrink_moment, shrink_square)]
    matrices += [v[None] for v in (vector_params, vector_moment, vector_square)]
    def third(shape):
        n = len(shape)
        if shape[-2] != ROWS:
            return pl.BlockSpec(shape, lambda i: (0,) * n)
        return pl.BlockSpec(
            shape[:-2] + (ROWS // 3, shape[-1]), lambda i: (0,) * (n - 2) + (i, 0)
        )

    given = [squares, joint_shard, mixer_shard, ff_shard, vector_shard] + matrices
    made = [(1, HEAD)] + [v.shape for v in matrices]
    norm, *new = pl.pallas_call(
        update,
        grid=(3,),
        out_shape=[jax.ShapeDtypeStruct(shape, f32) for shape in made],
        in_specs=[third(v.shape) for v in given],
        out_specs=[third(shape) for shape in made],
        compiler_params=pltpu.CompilerParams(vmem_limit_bytes=60 * MiB),
        cost_estimate=SMALL,
    )(*given)
    new[9:12] = [v.T for v in new[9:12]]
    new[12:] = [v[0] for v in new[12:]]
    return (output, input_grad, norm[0, 0], *new)


def solution(mesh):
    row = P("dp", None, None)
    matrix = [P("dp", "mp")] * 6 + [P(None, "dp", "mp")] * 3 + [P("mp", "dp")] * 3
    vector = [P(("dp", "mp"))] * 3
    return jax.shard_map(
        body,
        mesh=mesh,
        in_specs=tuple([row, P("dp"), row] + matrix + vector),
        out_specs=tuple([row, row, P()] + matrix + vector),
        check_vma=False,
    )
```

```python
import jax
import jax.numpy as jnp
import numpy as np
from jax import lax
from jax.experimental import pallas as pl
from jax.experimental.pallas import tpu as pltpu
from jax.sharding import PartitionSpec as P

QUERY_HEADS = 12
KEY_VALUE_HEADS = 2
HEAD = 128
STEP = 5
EPS_NORM = 1e-06
ROPE_BASE = 1000000.0
MAX_NORM = 1.0
BETA_ONE = 0.9
BETA_TWO = 0.95
ADAM_EPS = 1e-08
DECAY = 0.1
RATE_MATRIX = 0.06
RATE_VECTOR = 0.8
MASKED = -1e30

T = 512
HALF = 256
PART = 64
D = 1536
FF = 1120
FP = 1152
DP = 16
MP = 8
ROWS = D // DP
JC = 256
MC = 192
KEY_AT = 6
SCALE = HEAD ** (-0.5)

f32 = jnp.float32
bf16 = jnp.bfloat16
VM = pl.BlockSpec(memory_space=pltpu.VMEM)
SM = pl.BlockSpec(memory_space=pltpu.SMEM)
MiB = 1 << 20
SMALL = pl.CostEstimate(flops=1, bytes_accessed=1, transcendentals=0)


def shift_y(v, k):
    return lax.ppermute(v, "mp", [(i, (i + 2 * k) % MP) for i in range(MP)])


def from_last_chip(v, k):
    return lax.ppermute(v, "mp", [(i, (i + 2 * k) % MP) for i in (MP - 2, MP - 1)])


def to_last_chip(v, y):
    return lax.ppermute(v, "mp", [(2 * y + c, MP - 2 + c) for c in range(2)])


def swap_core(v):
    return lax.ppermute(v, "mp", [(i, i ^ 1) for i in range(MP)])


def exchange(v, axis):
    return lax.all_to_all(v, axis, split_axis=0, concat_axis=0, tiled=True)


RELATIVE = (0, -1, 1, 2)


def gather(shift, v):
    return [v, shift(v, 1), shift(v, -1), shift(v, 2)]


def nn(a, b):
    return lax.dot_general(a, b, (((1,), (0,)), ((), ())), preferred_element_type=f32)


def nt(a, b):
    return lax.dot_general(a, b, (((1,), (1,)), ((), ())), preferred_element_type=f32)


def tn(a, b):
    return lax.dot_general(a, b, (((0,), (0,)), ((), ())), preferred_element_type=f32)


def whole(body, outs, args, scratch=(), limit=60, after=()):
    n = len(args)

    def bare(*refs):
        body(*refs[:n], *refs[n + len(after) :])

    return pl.pallas_call(
        bare,
        out_shape=[jax.ShapeDtypeStruct(s, d) for s, d in outs],
        in_specs=[SM] + [VM] * (n - 1) + [pl.BlockSpec(memory_space=pl.ANY)] * len(after),
        out_specs=[VM] * len(outs),
        scratch_shapes=list(scratch),
        compiler_params=pltpu.CompilerParams(vmem_limit_bytes=limit * MiB),
        cost_estimate=SMALL,
    )(*args, *after)


def at(start, size, step):
    return pl.ds(pl.multiple_of(start, step), size)


def prepare(ids, cotangent, tok, back, back_t, back_part, tok_part, tok_half):
    length, y, c = ids[0], ids[3], ids[4]
    for h in range(2):
        start = HALF * ((c + h) % 2)
        t = lax.broadcasted_iota(jnp.int32, (HALF, 1), 0) + start
        v = cotangent[at(start, HALF, HALF), :]
        v = jnp.where(t < length, v, jnp.zeros_like(v))
        back[HALF * h : HALF * (h + 1), :] = v
        back_t[:, HALF * h : HALF * (h + 1)] = v.T
    back_part[...] = back[at(PART * y, PART, PART), :]
    tok_part[...] = tok[at(HALF * c + PART * y, PART, PART), :]
    tok_half[...] = tok[at(HALF * c, HALF, HALF), :]


def kept(i, n, length):
    t = lax.broadcasted_iota(jnp.int32, (128, n), 0) + 128 * i
    s = lax.broadcasted_iota(jnp.int32, (128, n), 1)
    return (s <= t) & (s < length)


def attend(
    ids, tok, gain, bias, cosine, sine, query_w, pair_w,
    normed, heads_out, out, lse, w, heads,
):
    step = pl.program_id(0)

    @pl.when(step == 0)
    def _():
        w[:, :JC] = query_w[:, :ROWS, :].reshape(D, JC)
        w[:, JC:] = pair_w[:, :ROWS, :].reshape(D, JC)

    x = tok[...].astype(f32)
    s = lax.rsqrt(jnp.mean(x * x, -1, keepdims=True) + EPS_NORM)
    n = (x * s * gain[...]).astype(bf16)
    normed[...] = n
    j = nn(n, w[...]) + bias[...]
    rows = at(128 * step, 128, 128)
    for h in range(4):
        cols = slice(HEAD * h, HEAD * (h + 1))
        u = j[:, cols]
        if h < 3:
            u = u * cosine[...] + pltpu.roll(u, HEAD // 2, 1) * sine[...]
        heads[rows, cols] = u.astype(bf16)
        heads_out[:, cols] = u.astype(bf16)

    for i in range(4):

        @pl.when(step == i)
        def _():
            n = 128 * (i + 1)
            k, v = heads[:n, 2 * HEAD : 3 * HEAD], heads[:n, 3 * HEAD :]
            for h in range(2):
                cols = slice(HEAD * h, HEAD * (h + 1))
                s = nt(heads[128 * i : n, cols], k) * SCALE
                s = jnp.where(kept(i, n, ids[0]), s, MASKED)
                m = jnp.max(s, -1, keepdims=True)
                e = jnp.exp(s - m)
                total = jnp.sum(e, -1, keepdims=True)
                o = nn((e / total).astype(bf16), v).astype(bf16)
                lse[:, cols] = jnp.broadcast_to(m + jnp.log(total), (128, HEAD))
                for y in range(4):
                    out[y, 0, 0, :, cols] = o


def assemble(ids, a0, a1, a2, a3, b0, b1, b2, b3, mixer, rows_w):
    y, c = ids[3], ids[4]
    for e, a, b in zip(RELATIVE, (a0, a1, a2, a3), (b0, b1, b2, b3)):
        first = 384 * lax.rem(y + e + 4, 4)
        left, right = at(first, JC, 128), at(first + JC, HEAD, 128)
        for d in range(DP):
            for half, v in ((c, a), (1 - c, b)):
                row = ROWS * d + 48 * half
                mixer[at(row, 48, 16), left] = v[d, :48, :]
                mixer[at(row, 32, 16), right] = v[d, 48:80, :HEAD]
                mixer[at(row + 32, 16, 16), right] = v[d, 48:64, HEAD:]
    rows_w[...] = mixer[at(JC * jnp.minimum(ids[2], KEY_AT - 1), JC, JC), :]


def mix(ids, att, mixer, tok, gain, hidden_part, normed, hidden, side):
    i = pl.program_id(0)

    @pl.when(i == 0)
    def _():
        for j in range(KEY_AT):
            side[:, JC * j : JC * (j + 1)] = att[j]

    cols = at(384 * i, 384, 384)
    hidden[:, cols] = nn(side[...], mixer[...]) + tok[...].astype(f32)

    @pl.when(i == 3)
    def _():
        hidden_part[...] = hidden[at(PART * ids[3], PART, PART), :]
        for r in range(0, HALF, 64):
            v = hidden[r : r + 64, :]
            s = lax.rsqrt(jnp.mean(v * v, -1, keepdims=True) + EPS_NORM)
            normed[r : r + 64, :] = (v * s * gain[...]).astype(bf16)


def gated(near, far, back, back_t, w, act, gate_grad, up_grad, grads, near_t):
    @pl.when(pl.program_id(0) == 0)
    def _():
        near_t[:, :HALF] = near[...].T
        near_t[:, HALF:] = far[...].T

    gate_w, up_w, down_w = [w[:, m].reshape(D, 256) for m in range(3)]
    for r, normed in ((0, near), (HALF, far)):
        rows = slice(r, r + HALF)
        g = nn(normed[...], gate_w)
        u = nn(normed[...], up_w)
        a = nn(back[rows, :], down_w)
        sigma = 1.0 / (1.0 + jnp.exp(-g))
        swished = g * sigma
        act[rows, :] = (swished * u).astype(bf16)
        gate_grad[rows, :] = (a * u * sigma * (1.0 + g * (1.0 - sigma))).astype(bf16)
        up_grad[rows, :] = (a * swished).astype(bf16)
    for m, (left, right) in enumerate(((near_t, gate_grad), (near_t, up_grad), (back_t, act))):
        for r in range(4):
            part = nn(left[384 * r : 384 * (r + 1), :], right[...]).astype(bf16)
            grads[4 * r : 4 * (r + 1), m] = part.reshape(4, ROWS, 256)


def spread(gate_grad, up_grad, w, near, far):
    gate_w, up_w = [w[:, m].reshape(768, FP) for m in range(2)]
    for b in range(3):
        cols = slice(256 * b, 256 * (b + 1))
        part = nt(gate_grad[...], gate_w[cols]) + nt(up_grad[...], up_w[cols])
        near[:, cols] = part[:HALF].astype(bf16)
        far[:, cols] = part[HALF:].astype(bf16)


def spread_out(act, w, near, far):
    down_w = w[:, 0].reshape(768, FP)
    for b in range(3):
        cols = slice(256 * b, 256 * (b + 1))
        part = nt(act[...], down_w[cols])
        near[:, cols] = part[:HALF].astype(bf16)
        far[:, cols] = part[HALF:].astype(bf16)


def halve(ids, near, other, own, p1, p2, p3):
    y = ids[3]
    for k, out in ((0, own), (1, p1), (3, p2), (2, p3)):
        rows = at(PART * lax.rem(y + k, 4), PART, PART)
        out[...] = (near[rows, :].astype(f32) + other[rows, :].astype(f32)).astype(out.dtype)


def halve_two(ids, near_a, other_a, near_b, other_b, own, p1, p2, p3):
    for n, (near, other) in enumerate(((near_a, other_a), (near_b, other_b))):
        halve(ids, near, other, own.at[n], p1.at[n], p2.at[n], p3.at[n])


def summed(own, parts):
    total = own[...]
    for part in parts:
        total += part[...].astype(f32)
    return total


def hidden_back(ids, own, a1, a2, a3, hidden, back, gain, grad, low, gain_part):
    h = hidden[...]
    g = summed(own, (a1, a2, a3))
    scale = lax.rsqrt(jnp.mean(h * h, -1, keepdims=True) + EPS_NORM)
    gain_part[...] = jnp.sum(g * h * scale, 0, keepdims=True)
    v = back[...].astype(f32) + norm_back(h, scale, gain[...], g)
    grad[...] = v
    low[...] = v.astype(bf16)


def finish(ids, own, a1, a2, a3, hidden, tok, grad, gain, done):
    length, y, c = ids[0], ids[3], ids[4]
    o, g = [summed(own.at[n], [a.at[n] for a in (a1, a2, a3)]) for n in range(2)]
    t = lax.broadcasted_iota(jnp.int32, (PART, 1), 0) + HALF * c + PART * y
    done[0] = jnp.where(t < length, o + hidden[...], 0.0).astype(bf16)
    x = tok[...].astype(f32)
    scale = lax.rsqrt(jnp.mean(x * x, -1, keepdims=True) + EPS_NORM)
    done[1] = (grad[...] + norm_back(x, scale, gain[...], g)).astype(bf16)


def attend_back(
    ids, near, far, rows_w, heads, lse, cosine, sine,
    grads, window, own_kind, other_kind, low, att_grad, key_grad, value_grad,
):
    length, y, c = ids[0], ids[3], ids[4]
    for k, e in enumerate(RELATIVE):
        place = PART * lax.rem(y + e + 4, 4)
        low[at(HALF * c + place, PART, PART), :] = near[k]
        low[at(HALF * (1 - c) + place, PART, PART), :] = far[k]
    window[...] = low[:, at(384 * y, 384, 384)]
    has_heads = (ids[2] < KEY_AT).astype(f32)
    att_grad[...] = (nt(low[...], rows_w[...]) * has_heads).astype(bf16)
    key_grad[...] = jnp.zeros_like(key_grad)
    value_grad[...] = jnp.zeros_like(value_grad)
    for h in range(2):
        cols = slice(HEAD * h, HEAD * (h + 1))
        for i in range(4):
            n = 128 * (i + 1)
            rows = slice(128 * i, n)
            q = heads[rows, cols]
            k, v = heads[:n, 2 * HEAD : 3 * HEAD], heads[:n, 3 * HEAD :]
            o = att_grad[rows, cols]
            s = nt(q, k) * SCALE
            p = jnp.where(kept(i, n, length), jnp.exp(s - lse[rows, HEAD * h : HEAD * h + 1]), 0.0)
            d = nt(o, v)
            g = (p * (d - jnp.sum(p * d, -1, keepdims=True))).astype(bf16)
            value_grad[:n, :] += tn(p.astype(bf16), o)
            key_grad[:n, :] += tn(g, q)
            dq = nn(g, k) * SCALE
            dq = dq * cosine[rows, :] - pltpu.roll(dq, HEAD // 2, 1) * sine[rows, :]
            grads[rows, cols] = dq.astype(bf16)
    dk = key_grad[...] * SCALE
    dk = dk * cosine[...] - pltpu.roll(dk, HEAD // 2, 1) * sine[...]
    grads[:, 2 * HEAD : 3 * HEAD] = dk.astype(bf16)
    grads[:, 3 * HEAD :] = value_grad[...].astype(bf16)
    k, v = grads[:, 2 * HEAD : 3 * HEAD], grads[:, 3 * HEAD :]

    @pl.when(c == 0)
    def _():
        own_kind[...] = k
        other_kind[...] = v

    @pl.when(c != 0)
    def _():
        own_kind[...] = v
        other_kind[...] = k


def joint_back(
    ids, grads, w, tok, second_part,
    near, far, chunks, gain_part, vec, blocks,
):
    g = grads[...]
    gain_part[...] = jnp.zeros_like(gain_part)
    for r in range(0, T, 128):
        rows = slice(r, r + 128)
        back = nt(g[rows], w[...])
        half, place = r // HALF, slice(r % HALF, r % HALF + 128)
        moves = back.astype(bf16)

        @pl.when(ids[4] == half)
        def _():
            near[place, :] = moves

        @pl.when(ids[4] != half)
        def _():
            far[place, :] = moves

        x = tok[rows, :].astype(f32)
        s = lax.rsqrt(jnp.mean(x * x, -1, keepdims=True) + EPS_NORM)
        gain_part[...] += jnp.sum(back * x * s, 0, keepdims=True)
    vec[...] = jnp.zeros_like(vec)
    vec[:, :D] = gain_part[...]
    vec[:, D : 2 * D] = second_part[...]
    bias = jnp.sum(g.astype(f32), 0, keepdims=True)
    head_at = jnp.minimum(ids[2], KEY_AT - 1)
    key_start = 2 * D + JC * KEY_AT + HEAD * lax.div(head_at, 3)
    vec[:, at(2 * D + JC * head_at, JC, JC)] = bias[:, :JC]
    vec[:, at(key_start, HEAD, HEAD)] = bias[:, JC : JC + HEAD]
    vec[:, at(key_start + JC, HEAD, HEAD)] = bias[:, JC + HEAD :]
    for d in range(DP):
        blocks[d : d + 1, :] = vec[:, 320 * d : 320 * (d + 1)]
    for m in range(MP):
        piece = blocks[:, 40 * m : 40 * (m + 1)]
        piece = jnp.concatenate([piece, jnp.zeros((DP, HEAD - 40), f32)], 1)
        high = piece.astype(bf16)
        chunks[m, :DP, :] = high
        chunks[m, DP:, :] = (piece - high.astype(f32)).astype(bf16)


def back_to_input(
    ids, near_low, far_low, rows_w, heads, lse, cosine, sine, w, tok, second_part,
    grads, window, own_kind, other_kind, near, far, chunks,
    low, att_grad, key_grad, value_grad, gain_part, vec, blocks,
):
    attend_back(
        ids, near_low, far_low, rows_w, heads, lse, cosine, sine,
        grads, window, own_kind, other_kind, low, att_grad, key_grad, value_grad,
    )
    joint_back(ids, grads, w, tok, second_part, near, far, chunks, gain_part, vec, blocks)


def group_parts(ids, own, other, both, left, right):
    own_group = lax.div(jnp.minimum(ids[2], KEY_AT - 1), 3)
    partner = ids[2] + 1 - 2 * ids[4]
    other_group = lax.div(jnp.minimum(partner, KEY_AT - 1), 3)
    a, b = own[...].astype(f32), other[...].astype(f32)
    for g, out in ((0, left), (1, right)):
        part = a * (own_group == g).astype(f32) + b * (other_group == g).astype(f32)
        out[...] = part.astype(bf16)
        both[:, HEAD * g : HEAD * (g + 1)] = part.astype(bf16)


def weigh_joint(ids, normed, grads, left, right, both, moved, mixer_parts, parts):
    pair = jnp.concatenate([left[...].astype(f32), right[...].astype(f32)], 1)
    pair = pair + both[...].astype(f32)
    own = grads[:, :JC].astype(f32)
    g = jnp.where(ids[2] < KEY_AT, own, pair).astype(bf16)
    for r in range(4):
        cols = slice(384 * r, 384 * (r + 1))
        part = tn(normed[:, cols], g).astype(bf16)
        parts[4 * r : 4 * (r + 1), :ROWS, :JC] = part.reshape(4, ROWS, JC)
    parts[:, :ROWS, JC:] = mixer_parts[...]
    vec = moved[0].astype(f32)
    for j in range(1, MP):
        vec += moved[j].astype(f32)
    vec = vec[:DP] + vec[DP:]
    high = vec.astype(bf16).astype(f32)
    rest = jnp.zeros((8, MC), bf16)
    for d in range(DP):
        parts[d, ROWS:, :HEAD] = jnp.broadcast_to(high[d : d + 1], (8, HEAD)).astype(bf16)
        low = (vec - high)[d : d + 1]
        parts[d, ROWS:, HEAD:JC] = jnp.broadcast_to(low, (8, HEAD)).astype(bf16)
        parts[d, ROWS:, JC:] = rest


def weigh_mixer(ids, near, far, low, parts):
    c = ids[4]

    def own_columns(half):
        v = low[at(HALF * half, HALF, HALF), :].astype(f32)
        return jnp.where(c == 0, v[:, :MC], v[:, MC:]).astype(bf16)

    mine, other = own_columns(c), own_columns(1 - c)
    for j in range(KEY_AT):
        part = (tn(near[j], mine) + tn(far[j], other)).astype(bf16)
        start = JC * j
        while start < JC * (j + 1):
            stop = min((start // ROWS + 1) * ROWS, JC * (j + 1))
            first = start % ROWS
            parts[start // ROWS, first : first + stop - start, :] = part[
                start - JC * j : stop - JC * j
            ]
            start = stop


def settle_grads(ids, moved, ff, joint, mixer, vector, squares):
    total = moved[0].astype(f32)
    for d in range(1, DP):
        total += moved[d].astype(f32)
    joint[...] = total[:ROWS, :JC]
    mixer[...] = total[:ROWS, JC:]
    vec = total[ROWS : ROWS + 1, :HEAD] + total[ROWS : ROWS + 1, HEAD:JC]
    vector[...] = vec
    total = total[:ROWS]
    total = jnp.sum(total * total) + jnp.sum(vec * vec)
    for m in range(3):
        v = ff[m].astype(f32)
        total += jnp.sum(v * v)
    squares[...] = jnp.full(squares.shape, total, f32)


def update(
    squares, joint_grad, mixer_grad, ff_grad, vector_grad,
    joint_w, joint_m, joint_v, mixer_w, mixer_m, mixer_v, expand_w, expand_m, expand_v,
    shrink_w, shrink_m, shrink_v, vector_w, vector_m, vector_v,
    norm_out, joint_wn, joint_mn, joint_vn, mixer_wn, mixer_mn, mixer_vn,
    expand_wn, expand_mn, expand_vn, shrink_wn, shrink_mn, shrink_vn,
    vector_wn, vector_mn, vector_vn,
):
    norm = jnp.sqrt(jnp.sum(squares[:, 0, :], 0, keepdims=True))
    norm_out[...] = norm
    clip = jnp.minimum(1.0, MAX_NORM / (norm[:, :1] + 1e-06))

    def step(grad, before, after, rate, decay, part=Ellipsis):
        w, m, v = [ref[part] for ref in before]
        results = adam_step(w, clip * grad, m, v, rate, decay)
        for ref, new in zip(after, results):
            ref[part] = new

    step(
        joint_grad[...], (joint_w, joint_m, joint_v), (joint_wn, joint_mn, joint_vn),
        RATE_MATRIX, DECAY,
    )
    step(
        mixer_grad[...], (mixer_w, mixer_m, mixer_v), (mixer_wn, mixer_mn, mixer_vn),
        RATE_MATRIX, DECAY,
    )
    for m in range(2):
        step(
            ff_grad[m, :, :FF].astype(f32),
            (expand_w, expand_m, expand_v), (expand_wn, expand_mn, expand_vn),
            RATE_MATRIX, DECAY, m,
        )
    step(
        ff_grad[2, :, :FF].astype(f32),
        (shrink_w, shrink_m, shrink_v), (shrink_wn, shrink_mn, shrink_vn),
        RATE_MATRIX, DECAY,
    )
    step(
        vector_grad[:, :40], (vector_w, vector_m, vector_v), (vector_wn, vector_mn, vector_vn),
        RATE_VECTOR, 0.0,
    )


def write_half(ids, half, pieces, outs, rows, sems):
    for k, e in enumerate(RELATIVE):
        place = at(PART * lax.rem(ids[3] + e + 4, 4), PART, PART)
        for n in range(2):
            rows[n, place, :] = pieces[k][n].astype(f32)
    copies = [
        pltpu.make_async_copy(rows.at[n], out.at[0, at(HALF * half, HALF, HALF)], sems.at[n])
        for n, out in enumerate(outs)
    ]
    for copy in copies:
        copy.start()
    for copy in copies:
        copy.wait()


def settle_near(ids, p0, p1, p2, p3, output, input_grad, token, rows, sems):
    token[...] = jnp.zeros_like(token)
    write_half(ids, ids[4], (p0, p1, p2, p3), (output, input_grad), rows, sems)


def settle_far(ids, far, _a, _b, output, input_grad, rows, sems):
    pieces = [far.at[k] for k in range(4)]
    write_half(ids, 1 - ids[4], pieces, (output, input_grad), rows, sems)


def pile(ids, p0, p1, p2, p3, out):
    for k, p in enumerate((p0, p1, p2, p3)):
        out[k] = p[...]


def norm_back(v, scale, gain, grad):
    scaled = gain * grad
    return scale * scaled - v * scale * scale * scale * jnp.mean(scaled * v, -1, keepdims=True)


def adam_step(weight, grad, moment, square, rate, decay):
    moment_next = BETA_ONE * moment + (1.0 - BETA_ONE) * grad
    square_next = BETA_TWO * square + (1.0 - BETA_TWO) * grad * grad
    first_hat = moment_next * (1.0 / (1.0 - BETA_ONE**STEP))
    second_hat = square_next * (1.0 / (1.0 - BETA_TWO**STEP))
    weight_next = weight - rate * (first_hat / (jnp.sqrt(second_hat) + ADAM_EPS) + decay * weight)
    return (weight_next, moment_next, square_next)


def tables():
    freq = np.float32(ROPE_BASE) ** (-np.arange(0, HEAD, 2, dtype=np.float32) / np.float32(HEAD))
    angle = np.arange(T, dtype=np.float32)[:, None] * freq.astype(np.float32)[None, :]
    cosine, sine = np.cos(angle), np.sin(angle)
    return (
        np.concatenate([cosine, cosine], -1).astype(np.float32),
        np.concatenate([-sine, sine], -1).astype(np.float32),
    )


def split_low(v):
    high = lax.reduce_precision(v, 8, 7)
    middle = lax.reduce_precision(v - high, 8, 7)
    return [part.astype(bf16) for part in (high, middle, v - high - middle)]


def body(
    tokens, lengths, cotangent,
    joint_weight, joint_moment, joint_square,
    mixer_weight, mixer_moment, mixer_square,
    expand_weight, expand_moment, expand_square,
    shrink_weight, shrink_moment, shrink_square,
    vector_params, vector_moment, vector_square,
):
    dp, mp = lax.axis_index("dp"), lax.axis_index("mp")
    y, c = mp // 2, mp % 2
    tok, length = tokens[0], lengths[0]
    ids = jnp.stack([length, dp, mp, y, c]).astype(jnp.int32)

    stack = jnp.concatenate(
        [expand_weight.astype(bf16), shrink_weight.T.astype(bf16)[None]], 0
    )
    stack = jnp.pad(stack, ((0, 0), (0, 0), (0, FP - FF)))
    ff = lax.all_gather(stack, "dp", axis=0, tiled=False)

    low = jnp.concatenate([joint_weight.astype(bf16), mixer_weight.astype(bf16)], 1)
    vec = jnp.pad(jnp.stack(split_low(vector_params)), ((0, 13), (0, JC + MC - 40)))
    low = jnp.concatenate([low, vec], 0)
    other = swap_core(low)
    first, second = jnp.where(c == 0, low, other), jnp.where(c == 0, other, low)
    pairs = [
        jnp.concatenate([first[:ROWS, cols], second[:ROWS, cols]], 1)
        for cols in (slice(0, HEAD), slice(HEAD, JC))
    ]
    chip = jnp.concatenate([first[:ROWS, JC:], second[:ROWS, JC:]], 1)
    chip = lax.dynamic_slice_in_dim(chip, 48 * c, 48, 0)
    rest = jnp.concatenate([chip[:32, JC:], jnp.pad(chip[32:, JC:], ((0, 16), (0, 0)))], 1)
    sent = jnp.concatenate([low[:ROWS, :JC], chip[:, :JC], rest], 0)
    query_w = exchange(jnp.broadcast_to(sent, (DP,) + sent.shape), "dp")
    vec = jnp.concatenate([first[ROWS:, :HEAD], second[ROWS:, :HEAD]], 1)
    sends = [pairs[0], pairs[1], jnp.where(c == 0, pairs[0], pairs[1])]
    sends = [jnp.concatenate([v, vec], 0) for v in sends]
    a1, a2, a3 = [shift_y(v, k) for v, k in zip(sends, (1, -1, 2))]
    pair = jnp.where(y == 0, a1[:ROWS], jnp.where(y == 2, a2[:ROWS], a3[:ROWS]))
    vec = jnp.stack([vec, a2[ROWS:], a3[ROWS:], a1[ROWS:]])[:, :3]
    vec = lax.dynamic_slice_in_dim(jnp.concatenate([vec, vec]), (4 - y) % 4, 4, 0)
    sent = jnp.concatenate([pair, vec.reshape(12, JC), query_w[0, :4]], 0)
    pair_w = exchange(jnp.broadcast_to(sent, (DP,) + sent.shape), "dp")
    vec = pair_w[:, ROWS : ROWS + 12].astype(f32).reshape(DP, 4, 3, 2, HEAD)[..., :40]
    vec = vec[:, :, 0] + vec[:, :, 1] + vec[:, :, 2]
    vec = vec.reshape(-1)

    gain_first, gain_second = vec[None, :D], vec[None, D : 2 * D]
    key_start = JC * KEY_AT + HEAD * (jnp.minimum(mp, KEY_AT - 1) // 3)
    starts = ((JC * mp, JC), (key_start, HEAD), (key_start + JC, HEAD))
    bias = jnp.concatenate(
        [lax.dynamic_slice_in_dim(vec, 2 * D + start, size, 0) for start, size in starts]
    )[None]

    cosine, sine = tables()
    back, back_t, back_part, tok_part, tok_half = whole(
        prepare,
        [
            ((T, D), bf16), ((D, T), bf16),
            ((PART, D), bf16), ((PART, D), bf16), ((HALF, D), bf16),
        ],
        [ids, cotangent[0], tok],
    )
    def fixed(shape):
        return pl.BlockSpec(shape, lambda i: (0,) * len(shape))

    def rows(columns):
        return pl.BlockSpec((128, columns), lambda i: (i, 0))

    normed, heads, att_sent, lse, joint_w = pl.pallas_call(
        lambda *refs: attend(*refs[:8], *refs[9:]),
        grid=(4,),
        out_shape=[
            jax.ShapeDtypeStruct((T, D), bf16),
            jax.ShapeDtypeStruct((T, 2 * JC), bf16),
            jax.ShapeDtypeStruct((4, 2, 2, 128, JC), bf16),
            jax.ShapeDtypeStruct((T, JC), f32),
            jax.ShapeDtypeStruct((D, 2 * JC), bf16),
        ],
        in_specs=[
            SM, rows(D), fixed((1, D)), fixed((1, 2 * JC)), rows(HEAD), rows(HEAD),
            fixed(query_w.shape), fixed(pair_w.shape), pl.BlockSpec(memory_space=pl.ANY),
        ],
        out_specs=[
            rows(D), rows(2 * JC),
            pl.BlockSpec((4, 1, 1, 128, JC), lambda i: (0, i // 2, i % 2, 0, 0)),
            rows(JC), fixed((D, 2 * JC)),
        ],
        scratch_shapes=[pltpu.VMEM((T, 2 * JC), bf16)],
        compiler_params=pltpu.CompilerParams(vmem_limit_bytes=60 * MiB),
        cost_estimate=SMALL,
    )(ids, tok, gain_first, bias, cosine, sine, query_w, pair_w, back)
    att_sent = att_sent.reshape(MP, HALF, JC)
    att_near = exchange(att_sent, "mp")
    att_far = swap_core(att_near)
    mixer_near = gather(shift_y, query_w[:, ROWS:])
    mixer_far = [swap_core(v) for v in mixer_near]
    mixer, rows_w = whole(
        assemble, [((D, D), bf16), ((JC, D), bf16)], [ids] + mixer_near + mixer_far
    )

    hidden_part, normed_near = pl.pallas_call(
        mix,
        grid=(4,),
        out_shape=[jax.ShapeDtypeStruct((PART, D), f32), jax.ShapeDtypeStruct((HALF, D), bf16)],
        in_specs=[
            SM,
            fixed((MP, HALF, JC)),
            pl.BlockSpec((D, 384), lambda i: (0, i)),
            pl.BlockSpec((HALF, 384), lambda i: (0, i)),
            fixed((1, D)),
        ],
        out_specs=[fixed((PART, D)), fixed((HALF, D))],
        scratch_shapes=[pltpu.VMEM((HALF, D), f32), pltpu.VMEM((HALF, D), bf16)],
        compiler_params=pltpu.CompilerParams(vmem_limit_bytes=60 * MiB),
        cost_estimate=SMALL,
    )(ids, att_near, mixer, tok_half, gain_second)
    normed_far = swap_core(normed_near)

    def columns(n):
        return pl.BlockSpec((n, 256), lambda i: (0, i))

    block = pl.BlockSpec((DP, 3, ROWS, 256), lambda i: (0, 0, 0, i))
    act, gate_grad, up_grad, ff_grads = pl.pallas_call(
        gated,
        grid=(pl.cdiv(FP, 256),),
        out_shape=[jax.ShapeDtypeStruct((T, FP), bf16)] * 3
        + [jax.ShapeDtypeStruct((DP, 3, ROWS, FP), bf16)],
        in_specs=[fixed((HALF, D)), fixed((HALF, D)), fixed((T, D)), fixed((D, T)), block],
        out_specs=[columns(T)] * 3 + [block],
        scratch_shapes=[pltpu.VMEM((D, T), bf16)],
        compiler_params=pltpu.CompilerParams(vmem_limit_bytes=60 * MiB),
        cost_estimate=SMALL,
    )(normed_near, normed_far, back, back_t, ff)
    ff_shard = lax.psum_scatter(ff_grads, "dp", scatter_dimension=0, tiled=False)

    near, far = pl.pallas_call(
        spread,
        grid=(2,),
        out_shape=[jax.ShapeDtypeStruct((HALF, D), bf16)] * 2,
        in_specs=[fixed((T, FP))] * 2
        + [pl.BlockSpec((DP // 2, 2, ROWS, FP), lambda i: (i, 0, 0, 0))],
        out_specs=[pl.BlockSpec((HALF, 768), lambda i: (0, i))] * 2,
        compiler_params=pltpu.CompilerParams(vmem_limit_bytes=60 * MiB),
        cost_estimate=SMALL,
    )(gate_grad, up_grad, ff)

    def half_sum(body, pairs, after=()):
        shape = (PART, D) if len(pairs) == 1 else (len(pairs), PART, D)
        given = [v for near, far in pairs for v in (near, swap_core(far))]
        own, *parts = whole(
            body, [(shape, f32)] + [(shape, bf16)] * 3, [ids] + given, after=after, limit=16
        )
        return [own] + [shift_y(v, k) for v, k in zip(parts, (1, -1, 2))]

    normed_second_parts = half_sum(halve, [(near, far)])
    out_near, out_far = pl.pallas_call(
        spread_out,
        grid=(2,),
        out_shape=[jax.ShapeDtypeStruct((HALF, D), bf16)] * 2,
        in_specs=[
            fixed((T, FP)),
            pl.BlockSpec((DP // 2, 1, ROWS, FP), lambda i: (i, 2, 0, 0)),
        ],
        out_specs=[pl.BlockSpec((HALF, 768), lambda i: (0, i))] * 2,
        compiler_params=pltpu.CompilerParams(vmem_limit_bytes=60 * MiB),
        cost_estimate=SMALL,
    )(act, ff)
    hidden_grad, low, gain_second_part = whole(
        hidden_back,
        [((PART, D), f32), ((PART, D), bf16), ((1, D), f32)],
        [ids] + normed_second_parts + [hidden_part, back_part, gain_second],
        after=[out_far],
        limit=8,
    )
    low_near = jnp.stack(gather(shift_y, low))
    low_far = swap_core(low_near)
    heads_grad, hidden_low, own_kind, other_kind, input_near, input_far, chunks = whole(
        back_to_input,
        [
            ((T, 2 * JC), bf16), ((T, 2 * MC), bf16), ((T, HEAD), bf16), ((T, HEAD), bf16),
            ((HALF, D), bf16), ((HALF, D), bf16), ((MP, 2 * DP, HEAD), bf16),
        ],
        [ids, low_near, low_far, rows_w, heads, lse, cosine, sine, joint_w, tok, gain_second_part],
        scratch=[
            pltpu.VMEM((T, D), bf16),
            pltpu.VMEM((T, JC), bf16),
            pltpu.VMEM((T, HEAD), f32),
            pltpu.VMEM((T, HEAD), f32),
            pltpu.VMEM((1, D), f32),
            pltpu.VMEM((1, DP * MP * 40), f32),
            pltpu.VMEM((DP, MP * 40), f32),
        ],
    )
    both, left, right = whole(
        group_parts,
        [((T, JC), bf16), ((T, HEAD), bf16), ((T, HEAD), bf16)],
        [ids, own_kind, swap_core(other_kind)],
        limit=8,
    )
    left, right, both = to_last_chip(left, 0), to_last_chip(right, 2), to_last_chip(both, 1)
    moved = exchange(chunks, "mp")
    (mixer_parts,) = whole(
        weigh_mixer,
        [((DP, ROWS, MC), bf16)],
        [ids, att_near, att_far, hidden_low],
    )
    (joint_parts,) = whole(
        weigh_joint,
        [((DP, ROWS + 8, JC + MC), bf16)],
        [ids, normed, heads_grad, left, right, both, moved, mixer_parts],
    )
    joint_shard, mixer_shard, vector_shard, squares = whole(
        settle_grads,
        [((ROWS, JC), f32), ((ROWS, MC), f32), ((1, HEAD), f32), ((DP * MP, 1, HEAD), f32)],
        [ids, exchange(joint_parts, "dp"), ff_shard],
    )

    squares = exchange(squares, ("dp", "mp"))

    parts = half_sum(
        halve_two, [(out_near, out_far), (input_near, input_far)], after=[joint_parts]
    )
    (done,) = whole(
        finish,
        [((2, PART, D), bf16)],
        [ids] + parts + [hidden_part, tok_part, hidden_grad, gain_first],
        limit=8,
    )
    done_parts = gather(shift_y, done)
    anywhere = pl.BlockSpec(memory_space=pl.ANY)
    results = [jax.ShapeDtypeStruct((1, T, D), f32)] * 2
    held = [pltpu.VMEM((2, HALF, D), f32), pltpu.SemaphoreType.DMA((2,))]
    *halves, token = pl.pallas_call(
        settle_near,
        out_shape=results + [jax.ShapeDtypeStruct((8, HEAD), f32)],
        in_specs=[SM] + [VM] * 4,
        out_specs=[anywhere] * 2 + [VM],
        scratch_shapes=held,
        compiler_params=pltpu.CompilerParams(vmem_limit_bytes=16 * MiB),
        cost_estimate=SMALL,
    )(ids, *done_parts)
    (done_near,) = whole(
        pile, [((4, 2, PART, D), bf16)], [ids] + done_parts, after=[squares, token], limit=8
    )
    output, input_grad = pl.pallas_call(
        settle_far,
        out_shape=results,
        in_specs=[SM, VM] + [anywhere] * 2,
        out_specs=[anywhere] * 2,
        input_output_aliases={2: 0, 3: 1},
        scratch_shapes=held,
        compiler_params=pltpu.CompilerParams(vmem_limit_bytes=16 * MiB),
        cost_estimate=SMALL,
    )(ids, swap_core(done_near), *halves)

    matrices = [joint_weight, joint_moment, joint_square]
    matrices += [mixer_weight, mixer_moment, mixer_square]
    matrices += [expand_weight, expand_moment, expand_square]
    matrices += [v.T for v in (shrink_weight, shrink_moment, shrink_square)]
    matrices += [v[None] for v in (vector_params, vector_moment, vector_square)]
    def third(shape):
        n = len(shape)
        if shape[-2] != ROWS:
            return pl.BlockSpec(shape, lambda i: (0,) * n)
        return pl.BlockSpec(
            shape[:-2] + (ROWS // 3, shape[-1]), lambda i: (0,) * (n - 2) + (i, 0)
        )

    given = [squares, joint_shard, mixer_shard, ff_shard, vector_shard] + matrices
    made = [(1, HEAD)] + [v.shape for v in matrices]
    norm, *new = pl.pallas_call(
        update,
        grid=(3,),
        out_shape=[jax.ShapeDtypeStruct(shape, f32) for shape in made],
        in_specs=[third(v.shape) for v in given],
        out_specs=[third(shape) for shape in made],
        compiler_params=pltpu.CompilerParams(vmem_limit_bytes=60 * MiB),
        cost_estimate=SMALL,
    )(*given)
    new[9:12] = [v.T for v in new[9:12]]
    new[12:] = [v[0] for v in new[12:]]
    return (output, input_grad, norm[0, 0], *new)


def solution(mesh):
    row = P("dp", None, None)
    matrix = [P("dp", "mp")] * 6 + [P(None, "dp", "mp")] * 3 + [P("mp", "dp")] * 3
    vector = [P(("dp", "mp"))] * 3
    return jax.shard_map(
        body,
        mesh=mesh,
        in_specs=tuple([row, P("dp"), row] + matrix + vector),
        out_specs=tuple([row, row, P()] + matrix + vector),
        check_vma=False,
    )
```

```python
import jax
import jax.numpy as jnp
import numpy as np
from jax import lax
from jax.experimental import pallas as pl
from jax.experimental.pallas import tpu as pltpu
from jax.sharding import PartitionSpec as P

QUERY_HEADS = 12
KEY_VALUE_HEADS = 2
HEAD = 128
STEP = 5
EPS_NORM = 1e-06
ROPE_BASE = 1000000.0
MAX_NORM = 1.0
BETA_ONE = 0.9
BETA_TWO = 0.95
ADAM_EPS = 1e-08
DECAY = 0.1
RATE_MATRIX = 0.06
RATE_VECTOR = 0.8
MASKED = -1e30

T = 512
HALF = 256
PART = 64
D = 1536
FF = 1120
FP = 1152
DP = 16
MP = 8
ROWS = D // DP
JC = 256
MC = 192
KEY_AT = 6
SCALE = HEAD ** (-0.5)

f32 = jnp.float32
bf16 = jnp.bfloat16
VM = pl.BlockSpec(memory_space=pltpu.VMEM)
SM = pl.BlockSpec(memory_space=pltpu.SMEM)
MiB = 1 << 20
SMALL = pl.CostEstimate(flops=1, bytes_accessed=1, transcendentals=0)


def shift_y(v, k):
    return lax.ppermute(v, "mp", [(i, (i + 2 * k) % MP) for i in range(MP)])


def from_last_chip(v, k):
    return lax.ppermute(v, "mp", [(i, (i + 2 * k) % MP) for i in (MP - 2, MP - 1)])


def to_last_chip(v, y):
    return lax.ppermute(v, "mp", [(2 * y + c, MP - 2 + c) for c in range(2)])


def swap_core(v):
    return lax.ppermute(v, "mp", [(i, i ^ 1) for i in range(MP)])


def exchange(v, axis):
    return lax.all_to_all(v, axis, split_axis=0, concat_axis=0, tiled=True)


RELATIVE = (0, -1, 1, 2)


def gather(shift, v):
    return [v, shift(v, 1), shift(v, -1), shift(v, 2)]


def nn(a, b):
    return lax.dot_general(a, b, (((1,), (0,)), ((), ())), preferred_element_type=f32)


def nt(a, b):
    return lax.dot_general(a, b, (((1,), (1,)), ((), ())), preferred_element_type=f32)


def tn(a, b):
    return lax.dot_general(a, b, (((0,), (0,)), ((), ())), preferred_element_type=f32)


def whole(body, outs, args, scratch=(), limit=60, after=()):
    n = len(args)

    def bare(*refs):
        body(*refs[:n], *refs[n + len(after) :])

    return pl.pallas_call(
        bare,
        out_shape=[jax.ShapeDtypeStruct(s, d) for s, d in outs],
        in_specs=[SM] + [VM] * (n - 1) + [pl.BlockSpec(memory_space=pl.ANY)] * len(after),
        out_specs=[VM] * len(outs),
        scratch_shapes=list(scratch),
        compiler_params=pltpu.CompilerParams(vmem_limit_bytes=limit * MiB),
        cost_estimate=SMALL,
    )(*args, *after)


def at(start, size, step):
    return pl.ds(pl.multiple_of(start, step), size)


def prepare(ids, cotangent, tok, back, back_t, back_part, tok_part, tok_half):
    length, y, c = ids[0], ids[3], ids[4]
    for h in range(2):
        start = HALF * ((c + h) % 2)
        t = lax.broadcasted_iota(jnp.int32, (HALF, 1), 0) + start
        v = cotangent[at(start, HALF, HALF), :]
        v = jnp.where(t < length, v, jnp.zeros_like(v))
        back[HALF * h : HALF * (h + 1), :] = v
        back_t[:, HALF * h : HALF * (h + 1)] = v.T
    back_part[...] = back[at(PART * y, PART, PART), :]
    tok_part[...] = tok[at(HALF * c + PART * y, PART, PART), :]
    tok_half[...] = tok[at(HALF * c, HALF, HALF), :]


def kept(i, n, length):
    t = lax.broadcasted_iota(jnp.int32, (128, n), 0) + 128 * i
    s = lax.broadcasted_iota(jnp.int32, (128, n), 1)
    return (s <= t) & (s < length)


def attend(
    ids, tok, gain, bias, cosine, sine, query_w, pair_w,
    normed, heads, out, lse, w,
):
    w[:, :JC] = query_w[:, :ROWS, :].reshape(D, JC)
    w[:, JC:] = pair_w[:, :ROWS, :].reshape(D, JC)

    @pl.loop(0, T // 128)
    def _(i):
        rows = at(i * 128, 128, 128)
        x = tok[rows, :].astype(f32)
        s = lax.rsqrt(jnp.mean(x * x, -1, keepdims=True) + EPS_NORM)
        n = (x * s * gain[...]).astype(bf16)
        normed[rows, :] = n
        j = nn(n, w[...]) + bias[...]
        for h in range(4):
            cols = slice(HEAD * h, HEAD * (h + 1))
            u = j[:, cols]
            if h < 3:
                u = u * cosine[rows, :] + pltpu.roll(u, HEAD // 2, 1) * sine[rows, :]
            heads[rows, cols] = u.astype(bf16)

    for h in range(2):
        for i in range(4):
            n = 128 * (i + 1)
            q = heads[128 * i : n, HEAD * h : HEAD * (h + 1)]
            k, v = heads[:n, 2 * HEAD : 3 * HEAD], heads[:n, 3 * HEAD :]
            s = jnp.where(kept(i, n, ids[0]), nt(q, k) * SCALE, MASKED)
            m = jnp.max(s, -1, keepdims=True)
            e = jnp.exp(s - m)
            total = jnp.sum(e, -1, keepdims=True)
            o = nn((e / total).astype(bf16), v).astype(bf16)
            lse[128 * i : n, HEAD * h : HEAD * (h + 1)] = jnp.broadcast_to(
                m + jnp.log(total), (128, HEAD)
            )
            at_row = 128 * (i % 2)
            for y in range(4):
                out[2 * y + i // 2, at_row : at_row + 128, HEAD * h : HEAD * (h + 1)] = o


def assemble(ids, a0, a1, a2, a3, b0, b1, b2, b3, mixer, rows_w):
    y, c = ids[3], ids[4]
    for e, a, b in zip(RELATIVE, (a0, a1, a2, a3), (b0, b1, b2, b3)):
        first = 384 * lax.rem(y + e + 4, 4)
        left, right = at(first, JC, 128), at(first + JC, HEAD, 128)
        for d in range(DP):
            for half, v in ((c, a), (1 - c, b)):
                row = ROWS * d + 48 * half
                mixer[at(row, 48, 16), left] = v[d, :48, :]
                mixer[at(row, 32, 16), right] = v[d, 48:80, :HEAD]
                mixer[at(row + 32, 16, 16), right] = v[d, 48:64, HEAD:]
    rows_w[...] = mixer[at(JC * jnp.minimum(ids[2], KEY_AT - 1), JC, JC), :]


def mix(ids, att, mixer, tok, gain, hidden_part, normed, hidden, side):
    i = pl.program_id(0)

    @pl.when(i == 0)
    def _():
        for j in range(KEY_AT):
            side[:, JC * j : JC * (j + 1)] = att[j]

    cols = at(384 * i, 384, 384)
    hidden[:, cols] = nn(side[...], mixer[...]) + tok[...].astype(f32)

    @pl.when(i == 3)
    def _():
        hidden_part[...] = hidden[at(PART * ids[3], PART, PART), :]
        for r in range(0, HALF, 64):
            v = hidden[r : r + 64, :]
            s = lax.rsqrt(jnp.mean(v * v, -1, keepdims=True) + EPS_NORM)
            normed[r : r + 64, :] = (v * s * gain[...]).astype(bf16)


def gated(near, far, back, back_t, w, act, gate_grad, up_grad, grads, near_t):
    @pl.when(pl.program_id(0) == 0)
    def _():
        near_t[:, :HALF] = near[...].T
        near_t[:, HALF:] = far[...].T

    gate_w, up_w, down_w = [w[:, m].reshape(D, 256) for m in range(3)]
    for r, normed in ((0, near), (HALF, far)):
        rows = slice(r, r + HALF)
        g = nn(normed[...], gate_w)
        u = nn(normed[...], up_w)
        a = nn(back[rows, :], down_w)
        sigma = 1.0 / (1.0 + jnp.exp(-g))
        swished = g * sigma
        act[rows, :] = (swished * u).astype(bf16)
        gate_grad[rows, :] = (a * u * sigma * (1.0 + g * (1.0 - sigma))).astype(bf16)
        up_grad[rows, :] = (a * swished).astype(bf16)
    for m, (left, right) in enumerate(((near_t, gate_grad), (near_t, up_grad), (back_t, act))):
        for r in range(4):
            part = nn(left[384 * r : 384 * (r + 1), :], right[...]).astype(bf16)
            grads[4 * r : 4 * (r + 1), m] = part.reshape(4, ROWS, 256)


def spread(gate_grad, up_grad, w, near, far):
    gate_w, up_w = [w[:, m].reshape(768, FP) for m in range(2)]
    for b in range(3):
        cols = slice(256 * b, 256 * (b + 1))
        part = nt(gate_grad[...], gate_w[cols]) + nt(up_grad[...], up_w[cols])
        near[:, cols] = part[:HALF].astype(bf16)
        far[:, cols] = part[HALF:].astype(bf16)


def spread_out(act, w, near, far):
    down_w = w[:, 0].reshape(768, FP)
    for b in range(3):
        cols = slice(256 * b, 256 * (b + 1))
        part = nt(act[...], down_w[cols])
        near[:, cols] = part[:HALF].astype(bf16)
        far[:, cols] = part[HALF:].astype(bf16)


def halve(ids, near, other, own, p1, p2, p3):
    y = ids[3]
    for k, out in ((0, own), (1, p1), (3, p2), (2, p3)):
        rows = at(PART * lax.rem(y + k, 4), PART, PART)
        out[...] = (near[rows, :].astype(f32) + other[rows, :].astype(f32)).astype(out.dtype)


def summed(own, parts):
    total = own[...]
    for part in parts:
        total += part[...].astype(f32)
    return total


def hidden_back(ids, own, a1, a2, a3, hidden, back, gain, grad, low, gain_part):
    h = hidden[...]
    g = summed(own, (a1, a2, a3))
    scale = lax.rsqrt(jnp.mean(h * h, -1, keepdims=True) + EPS_NORM)
    gain_part[...] = jnp.sum(g * h * scale, 0, keepdims=True)
    v = back[...].astype(f32) + norm_back(h, scale, gain[...], g)
    grad[...] = v
    low[...] = v.astype(bf16)


def add_parts(ids, own, a1, a2, a3, total):
    total[...] = summed(own, (a1, a2, a3))


def finish(ids, out_sum, own, a1, a2, a3, hidden, tok, grad, gain, done):
    length, y, c = ids[0], ids[3], ids[4]
    o, g = out_sum[...], summed(own, (a1, a2, a3))
    t = lax.broadcasted_iota(jnp.int32, (PART, 1), 0) + HALF * c + PART * y
    done[0] = jnp.where(t < length, o + hidden[...], 0.0).astype(bf16)
    x = tok[...].astype(f32)
    scale = lax.rsqrt(jnp.mean(x * x, -1, keepdims=True) + EPS_NORM)
    done[1] = (grad[...] + norm_back(x, scale, gain[...], g)).astype(bf16)


def attend_back(
    ids, near, far, rows_w, heads, lse, cosine, sine,
    grads, window, own_kind, other_kind, low, att_grad, key_grad, value_grad,
):
    length, y, c = ids[0], ids[3], ids[4]
    for k, e in enumerate(RELATIVE):
        place = PART * lax.rem(y + e + 4, 4)
        low[at(HALF * c + place, PART, PART), :] = near[k]
        low[at(HALF * (1 - c) + place, PART, PART), :] = far[k]
    window[...] = low[:, at(384 * y, 384, 384)]
    has_heads = (ids[2] < KEY_AT).astype(f32)
    att_grad[...] = (nt(low[...], rows_w[...]) * has_heads).astype(bf16)
    key_grad[...] = jnp.zeros_like(key_grad)
    value_grad[...] = jnp.zeros_like(value_grad)
    for h in range(2):
        cols = slice(HEAD * h, HEAD * (h + 1))
        for i in range(4):
            n = 128 * (i + 1)
            rows = slice(128 * i, n)
            q = heads[rows, cols]
            k, v = heads[:n, 2 * HEAD : 3 * HEAD], heads[:n, 3 * HEAD :]
            o = att_grad[rows, cols]
            s = nt(q, k) * SCALE
            p = jnp.where(kept(i, n, length), jnp.exp(s - lse[rows, HEAD * h : HEAD * h + 1]), 0.0)
            d = nt(o, v)
            g = (p * (d - jnp.sum(p * d, -1, keepdims=True))).astype(bf16)
            value_grad[:n, :] += tn(p.astype(bf16), o)
            key_grad[:n, :] += tn(g, q)
            dq = nn(g, k) * SCALE
            dq = dq * cosine[rows, :] - pltpu.roll(dq, HEAD // 2, 1) * sine[rows, :]
            grads[rows, cols] = dq.astype(bf16)
    dk = key_grad[...] * SCALE
    dk = dk * cosine[...] - pltpu.roll(dk, HEAD // 2, 1) * sine[...]
    grads[:, 2 * HEAD : 3 * HEAD] = dk.astype(bf16)
    grads[:, 3 * HEAD :] = value_grad[...].astype(bf16)
    k, v = grads[:, 2 * HEAD : 3 * HEAD], grads[:, 3 * HEAD :]

    @pl.when(c == 0)
    def _():
        own_kind[...] = k
        other_kind[...] = v

    @pl.when(c != 0)
    def _():
        own_kind[...] = v
        other_kind[...] = k


def joint_back(
    ids, grads, w, tok, second_part,
    near, far, chunks, gain_part, vec, blocks,
):
    g = grads[...]
    gain_part[...] = jnp.zeros_like(gain_part)
    for r in range(0, T, 128):
        rows = slice(r, r + 128)
        back = nt(g[rows], w[...])
        half, place = r // HALF, slice(r % HALF, r % HALF + 128)
        moves = back.astype(bf16)

        @pl.when(ids[4] == half)
        def _():
            near[place, :] = moves

        @pl.when(ids[4] != half)
        def _():
            far[place, :] = moves

        x = tok[rows, :].astype(f32)
        s = lax.rsqrt(jnp.mean(x * x, -1, keepdims=True) + EPS_NORM)
        gain_part[...] += jnp.sum(back * x * s, 0, keepdims=True)
    vec[...] = jnp.zeros_like(vec)
    vec[:, :D] = gain_part[...]
    vec[:, D : 2 * D] = second_part[...]
    bias = jnp.sum(g.astype(f32), 0, keepdims=True)
    head_at = jnp.minimum(ids[2], KEY_AT - 1)
    key_start = 2 * D + JC * KEY_AT + HEAD * lax.div(head_at, 3)
    vec[:, at(2 * D + JC * head_at, JC, JC)] = bias[:, :JC]
    vec[:, at(key_start, HEAD, HEAD)] = bias[:, JC : JC + HEAD]
    vec[:, at(key_start + JC, HEAD, HEAD)] = bias[:, JC + HEAD :]
    for d in range(DP):
        blocks[d : d + 1, :] = vec[:, 320 * d : 320 * (d + 1)]
    for m in range(MP):
        piece = blocks[:, 40 * m : 40 * (m + 1)]
        piece = jnp.concatenate([piece, jnp.zeros((DP, HEAD - 40), f32)], 1)
        high = piece.astype(bf16)
        chunks[m, :DP, :] = high
        chunks[m, DP:, :] = (piece - high.astype(f32)).astype(bf16)


def back_to_input(
    ids, near_low, far_low, rows_w, heads, lse, cosine, sine, w, tok, second_part,
    grads, window, own_kind, other_kind, near, far, chunks,
    low, att_grad, key_grad, value_grad, gain_part, vec, blocks,
):
    attend_back(
        ids, near_low, far_low, rows_w, heads, lse, cosine, sine,
        grads, window, own_kind, other_kind, low, att_grad, key_grad, value_grad,
    )
    joint_back(ids, grads, w, tok, second_part, near, far, chunks, gain_part, vec, blocks)


def group_parts(ids, own, other, both, left, right):
    own_group = lax.div(jnp.minimum(ids[2], KEY_AT - 1), 3)
    partner = ids[2] + 1 - 2 * ids[4]
    other_group = lax.div(jnp.minimum(partner, KEY_AT - 1), 3)
    a, b = own[...].astype(f32), other[...].astype(f32)
    for g, out in ((0, left), (1, right)):
        part = a * (own_group == g).astype(f32) + b * (other_group == g).astype(f32)
        out[...] = part.astype(bf16)
        both[:, HEAD * g : HEAD * (g + 1)] = part.astype(bf16)


def weigh_joint(ids, normed, grads, left, right, both, moved, mixer_parts, parts):
    pair = jnp.concatenate([left[...].astype(f32), right[...].astype(f32)], 1)
    pair = pair + both[...].astype(f32)
    own = grads[:, :JC].astype(f32)
    g = jnp.where(ids[2] < KEY_AT, own, pair).astype(bf16)
    for r in range(4):
        cols = slice(384 * r, 384 * (r + 1))
        part = tn(normed[:, cols], g).astype(bf16)
        parts[4 * r : 4 * (r + 1), :ROWS, :JC] = part.reshape(4, ROWS, JC)
    parts[:, :ROWS, JC:] = mixer_parts[...]
    vec = moved[0].astype(f32)
    for j in range(1, MP):
        vec += moved[j].astype(f32)
    vec = vec[:DP] + vec[DP:]
    high = vec.astype(bf16).astype(f32)
    rest = jnp.zeros((8, MC), bf16)
    for d in range(DP):
        parts[d, ROWS:, :HEAD] = jnp.broadcast_to(high[d : d + 1], (8, HEAD)).astype(bf16)
        low = (vec - high)[d : d + 1]
        parts[d, ROWS:, HEAD:JC] = jnp.broadcast_to(low, (8, HEAD)).astype(bf16)
        parts[d, ROWS:, JC:] = rest


def weigh_mixer(ids, near, far, low, parts):
    c = ids[4]

    def own_columns(half):
        v = low[at(HALF * half, HALF, HALF), :].astype(f32)
        return jnp.where(c == 0, v[:, :MC], v[:, MC:]).astype(bf16)

    mine, other = own_columns(c), own_columns(1 - c)
    for j in range(KEY_AT):
        part = (tn(near[j], mine) + tn(far[j], other)).astype(bf16)
        start = JC * j
        while start < JC * (j + 1):
            stop = min((start // ROWS + 1) * ROWS, JC * (j + 1))
            first = start % ROWS
            parts[start // ROWS, first : first + stop - start, :] = part[
                start - JC * j : stop - JC * j
            ]
            start = stop


def settle_grads(ids, moved, ff, joint, mixer, vector, squares):
    total = moved[0].astype(f32)
    for d in range(1, DP):
        total += moved[d].astype(f32)
    joint[...] = total[:ROWS, :JC]
    mixer[...] = total[:ROWS, JC:]
    vec = total[ROWS : ROWS + 1, :HEAD] + total[ROWS : ROWS + 1, HEAD:JC]
    vector[...] = vec
    total = total[:ROWS]
    total = jnp.sum(total * total) + jnp.sum(vec * vec)
    for m in range(3):
        v = ff[m].astype(f32)
        total += jnp.sum(v * v)
    squares[...] = jnp.full(squares.shape, total, f32)


def update(
    squares, joint_grad, mixer_grad, ff_grad, vector_grad,
    joint_w, joint_m, joint_v, mixer_w, mixer_m, mixer_v, expand_w, expand_m, expand_v,
    shrink_w, shrink_m, shrink_v, vector_w, vector_m, vector_v,
    norm_out, joint_wn, joint_mn, joint_vn, mixer_wn, mixer_mn, mixer_vn,
    expand_wn, expand_mn, expand_vn, shrink_wn, shrink_mn, shrink_vn,
    vector_wn, vector_mn, vector_vn,
):
    norm = jnp.sqrt(jnp.sum(squares[:, 0, :], 0, keepdims=True))
    norm_out[...] = norm
    clip = jnp.minimum(1.0, MAX_NORM / (norm[:, :1] + 1e-06))

    def step(grad, before, after, rate, decay, part=Ellipsis):
        w, m, v = [ref[part] for ref in before]
        results = adam_step(w, clip * grad, m, v, rate, decay)
        for ref, new in zip(after, results):
            ref[part] = new

    step(
        joint_grad[...], (joint_w, joint_m, joint_v), (joint_wn, joint_mn, joint_vn),
        RATE_MATRIX, DECAY,
    )
    step(
        mixer_grad[...], (mixer_w, mixer_m, mixer_v), (mixer_wn, mixer_mn, mixer_vn),
        RATE_MATRIX, DECAY,
    )
    for m in range(2):
        step(
            ff_grad[m, :, :FF].astype(f32),
            (expand_w, expand_m, expand_v), (expand_wn, expand_mn, expand_vn),
            RATE_MATRIX, DECAY, m,
        )
    step(
        ff_grad[2, :, :FF].astype(f32),
        (shrink_w, shrink_m, shrink_v), (shrink_wn, shrink_mn, shrink_vn),
        RATE_MATRIX, DECAY,
    )
    step(
        vector_grad[:, :40], (vector_w, vector_m, vector_v), (vector_wn, vector_mn, vector_vn),
        RATE_VECTOR, 0.0,
    )


def write_half(ids, half, pieces, outs, rows, sems):
    for k, e in enumerate(RELATIVE):
        place = at(PART * lax.rem(ids[3] + e + 4, 4), PART, PART)
        for n in range(2):
            rows[n, place, :] = pieces[k][n].astype(f32)
    copies = [
        pltpu.make_async_copy(rows.at[n], out.at[0, at(HALF * half, HALF, HALF)], sems.at[n])
        for n, out in enumerate(outs)
    ]
    for copy in copies:
        copy.start()
    for copy in copies:
        copy.wait()


def settle_near(ids, p0, p1, p2, p3, output, input_grad, token, rows, sems):
    token[...] = jnp.zeros_like(token)
    write_half(ids, ids[4], (p0, p1, p2, p3), (output, input_grad), rows, sems)


def settle_far(ids, far, _a, _b, output, input_grad, rows, sems):
    pieces = [far.at[k] for k in range(4)]
    write_half(ids, 1 - ids[4], pieces, (output, input_grad), rows, sems)


def pile(ids, p0, p1, p2, p3, out):
    for k, p in enumerate((p0, p1, p2, p3)):
        out[k] = p[...]


def norm_back(v, scale, gain, grad):
    scaled = gain * grad
    return scale * scaled - v * scale * scale * scale * jnp.mean(scaled * v, -1, keepdims=True)


def adam_step(weight, grad, moment, square, rate, decay):
    moment_next = BETA_ONE * moment + (1.0 - BETA_ONE) * grad
    square_next = BETA_TWO * square + (1.0 - BETA_TWO) * grad * grad
    first_hat = moment_next * (1.0 / (1.0 - BETA_ONE**STEP))
    second_hat = square_next * (1.0 / (1.0 - BETA_TWO**STEP))
    weight_next = weight - rate * (first_hat / (jnp.sqrt(second_hat) + ADAM_EPS) + decay * weight)
    return (weight_next, moment_next, square_next)


def tables():
    freq = np.float32(ROPE_BASE) ** (-np.arange(0, HEAD, 2, dtype=np.float32) / np.float32(HEAD))
    angle = np.arange(T, dtype=np.float32)[:, None] * freq.astype(np.float32)[None, :]
    cosine, sine = np.cos(angle), np.sin(angle)
    return (
        np.concatenate([cosine, cosine], -1).astype(np.float32),
        np.concatenate([-sine, sine], -1).astype(np.float32),
    )


def split_low(v):
    high = lax.reduce_precision(v, 8, 7)
    middle = lax.reduce_precision(v - high, 8, 7)
    return [part.astype(bf16) for part in (high, middle, v - high - middle)]


def body(
    tokens, lengths, cotangent,
    joint_weight, joint_moment, joint_square,
    mixer_weight, mixer_moment, mixer_square,
    expand_weight, expand_moment, expand_square,
    shrink_weight, shrink_moment, shrink_square,
    vector_params, vector_moment, vector_square,
):
    dp, mp = lax.axis_index("dp"), lax.axis_index("mp")
    y, c = mp // 2, mp % 2
    tok, length = tokens[0], lengths[0]
    ids = jnp.stack([length, dp, mp, y, c]).astype(jnp.int32)

    stack = jnp.concatenate(
        [expand_weight.astype(bf16), shrink_weight.T.astype(bf16)[None]], 0
    )
    stack = jnp.pad(stack, ((0, 0), (0, 0), (0, FP - FF)))
    ff = lax.all_gather(stack, "dp", axis=0, tiled=False)

    low = jnp.concatenate([joint_weight.astype(bf16), mixer_weight.astype(bf16)], 1)
    vec = jnp.pad(jnp.stack(split_low(vector_params)), ((0, 13), (0, JC + MC - 40)))
    low = jnp.concatenate([low, vec], 0)
    other = swap_core(low)
    first, second = jnp.where(c == 0, low, other), jnp.where(c == 0, other, low)
    pairs = [
        jnp.concatenate([first[:ROWS, cols], second[:ROWS, cols]], 1)
        for cols in (slice(0, HEAD), slice(HEAD, JC))
    ]
    chip = jnp.concatenate([first[:ROWS, JC:], second[:ROWS, JC:]], 1)
    chip = lax.dynamic_slice_in_dim(chip, 48 * c, 48, 0)
    rest = jnp.concatenate([chip[:32, JC:], jnp.pad(chip[32:, JC:], ((0, 16), (0, 0)))], 1)
    sent = jnp.concatenate([low[:ROWS, :JC], chip[:, :JC], rest], 0)
    query_w = exchange(jnp.broadcast_to(sent, (DP,) + sent.shape), "dp")
    vec = jnp.concatenate([first[ROWS:, :HEAD], second[ROWS:, :HEAD]], 1)
    sends = [pairs[0], pairs[1], jnp.where(c == 0, pairs[0], pairs[1])]
    sends = [jnp.concatenate([v, vec], 0) for v in sends]
    a1, a2, a3 = [shift_y(v, k) for v, k in zip(sends, (1, -1, 2))]
    pair = jnp.where(y == 0, a1[:ROWS], jnp.where(y == 2, a2[:ROWS], a3[:ROWS]))
    vec = jnp.stack([vec, a2[ROWS:], a3[ROWS:], a1[ROWS:]])[:, :3]
    vec = lax.dynamic_slice_in_dim(jnp.concatenate([vec, vec]), (4 - y) % 4, 4, 0)
    sent = jnp.concatenate([pair, vec.reshape(12, JC), query_w[0, :4]], 0)
    pair_w = exchange(jnp.broadcast_to(sent, (DP,) + sent.shape), "dp")
    vec = pair_w[:, ROWS : ROWS + 12].astype(f32).reshape(DP, 4, 3, 2, HEAD)[..., :40]
    vec = vec[:, :, 0] + vec[:, :, 1] + vec[:, :, 2]
    vec = vec.reshape(-1)

    gain_first, gain_second = vec[None, :D], vec[None, D : 2 * D]
    key_start = JC * KEY_AT + HEAD * (jnp.minimum(mp, KEY_AT - 1) // 3)
    starts = ((JC * mp, JC), (key_start, HEAD), (key_start + JC, HEAD))
    bias = jnp.concatenate(
        [lax.dynamic_slice_in_dim(vec, 2 * D + start, size, 0) for start, size in starts]
    )[None]

    cosine, sine = tables()
    back, back_t, back_part, tok_part, tok_half = whole(
        prepare,
        [
            ((T, D), bf16), ((D, T), bf16),
            ((PART, D), bf16), ((PART, D), bf16), ((HALF, D), bf16),
        ],
        [ids, cotangent[0], tok],
    )
    normed, heads, att_sent, lse, joint_w = whole(
        attend,
        [
            ((T, D), bf16), ((T, 2 * JC), bf16), ((MP, HALF, JC), bf16),
            ((T, JC), f32), ((D, 2 * JC), bf16),
        ],
        [ids, tok, gain_first, bias, cosine, sine, query_w, pair_w],
        after=[back],
    )
    att_near = exchange(att_sent, "mp")
    att_far = swap_core(att_near)
    mixer_near = gather(shift_y, query_w[:, ROWS:])
    mixer_far = [swap_core(v) for v in mixer_near]
    mixer, rows_w = whole(
        assemble, [((D, D), bf16), ((JC, D), bf16)], [ids] + mixer_near + mixer_far
    )

    def fixed(shape):
        return pl.BlockSpec(shape, lambda i: (0,) * len(shape))

    hidden_part, normed_near = pl.pallas_call(
        mix,
        grid=(4,),
        out_shape=[jax.ShapeDtypeStruct((PART, D), f32), jax.ShapeDtypeStruct((HALF, D), bf16)],
        in_specs=[
            SM,
            fixed((MP, HALF, JC)),
            pl.BlockSpec((D, 384), lambda i: (0, i)),
            pl.BlockSpec((HALF, 384), lambda i: (0, i)),
            fixed((1, D)),
        ],
        out_specs=[fixed((PART, D)), fixed((HALF, D))],
        scratch_shapes=[pltpu.VMEM((HALF, D), f32), pltpu.VMEM((HALF, D), bf16)],
        compiler_params=pltpu.CompilerParams(vmem_limit_bytes=60 * MiB),
        cost_estimate=SMALL,
    )(ids, att_near, mixer, tok_half, gain_second)
    normed_far = swap_core(normed_near)

    def columns(n):
        return pl.BlockSpec((n, 256), lambda i: (0, i))

    block = pl.BlockSpec((DP, 3, ROWS, 256), lambda i: (0, 0, 0, i))
    act, gate_grad, up_grad, ff_grads = pl.pallas_call(
        gated,
        grid=(pl.cdiv(FP, 256),),
        out_shape=[jax.ShapeDtypeStruct((T, FP), bf16)] * 3
        + [jax.ShapeDtypeStruct((DP, 3, ROWS, FP), bf16)],
        in_specs=[fixed((HALF, D)), fixed((HALF, D)), fixed((T, D)), fixed((D, T)), block],
        out_specs=[columns(T)] * 3 + [block],
        scratch_shapes=[pltpu.VMEM((D, T), bf16)],
        compiler_params=pltpu.CompilerParams(vmem_limit_bytes=60 * MiB),
        cost_estimate=SMALL,
    )(normed_near, normed_far, back, back_t, ff)
    ff_shard = lax.psum_scatter(ff_grads, "dp", scatter_dimension=0, tiled=False)

    near, far = pl.pallas_call(
        spread,
        grid=(2,),
        out_shape=[jax.ShapeDtypeStruct((HALF, D), bf16)] * 2,
        in_specs=[fixed((T, FP))] * 2
        + [pl.BlockSpec((DP // 2, 2, ROWS, FP), lambda i: (i, 0, 0, 0))],
        out_specs=[pl.BlockSpec((HALF, 768), lambda i: (0, i))] * 2,
        compiler_params=pltpu.CompilerParams(vmem_limit_bytes=60 * MiB),
        cost_estimate=SMALL,
    )(gate_grad, up_grad, ff)

    def half_sum(near, far, after=()):
        own, *parts = whole(
            halve,
            [((PART, D), f32)] + [((PART, D), bf16)] * 3,
            [ids, near, swap_core(far)],
            after=after,
            limit=8,
        )
        return [own] + [shift_y(v, k) for v, k in zip(parts, (1, -1, 2))]

    normed_second_parts = half_sum(near, far)
    out_near, out_far = pl.pallas_call(
        spread_out,
        grid=(2,),
        out_shape=[jax.ShapeDtypeStruct((HALF, D), bf16)] * 2,
        in_specs=[
            fixed((T, FP)),
            pl.BlockSpec((DP // 2, 1, ROWS, FP), lambda i: (i, 2, 0, 0)),
        ],
        out_specs=[pl.BlockSpec((HALF, 768), lambda i: (0, i))] * 2,
        compiler_params=pltpu.CompilerParams(vmem_limit_bytes=60 * MiB),
        cost_estimate=SMALL,
    )(act, ff)
    hidden_grad, low, gain_second_part = whole(
        hidden_back,
        [((PART, D), f32), ((PART, D), bf16), ((1, D), f32)],
        [ids] + normed_second_parts + [hidden_part, back_part, gain_second],
        after=[out_far],
        limit=8,
    )
    out_parts = half_sum(out_near, out_far)
    low_near = jnp.stack(gather(shift_y, low))
    low_far = swap_core(low_near)
    heads_grad, hidden_low, own_kind, other_kind, input_near, input_far, chunks = whole(
        back_to_input,
        [
            ((T, 2 * JC), bf16), ((T, 2 * MC), bf16), ((T, HEAD), bf16), ((T, HEAD), bf16),
            ((HALF, D), bf16), ((HALF, D), bf16), ((MP, 2 * DP, HEAD), bf16),
        ],
        [ids, low_near, low_far, rows_w, heads, lse, cosine, sine, joint_w, tok, gain_second_part],
        scratch=[
            pltpu.VMEM((T, D), bf16),
            pltpu.VMEM((T, JC), bf16),
            pltpu.VMEM((T, HEAD), f32),
            pltpu.VMEM((T, HEAD), f32),
            pltpu.VMEM((1, D), f32),
            pltpu.VMEM((1, DP * MP * 40), f32),
            pltpu.VMEM((DP, MP * 40), f32),
        ],
        after=[out_parts[0]],
    )
    (out_sum,) = whole(
        add_parts, [((PART, D), f32)], [ids] + out_parts, limit=8, after=[heads_grad]
    )
    both, left, right = whole(
        group_parts,
        [((T, JC), bf16), ((T, HEAD), bf16), ((T, HEAD), bf16)],
        [ids, own_kind, swap_core(other_kind)],
        limit=8,
        after=[out_sum],
    )
    left, right, both = to_last_chip(left, 0), to_last_chip(right, 2), to_last_chip(both, 1)
    moved = exchange(chunks, "mp")
    (mixer_parts,) = whole(
        weigh_mixer,
        [((DP, ROWS, MC), bf16)],
        [ids, att_near, att_far, hidden_low],
        after=[out_sum],
    )
    (joint_parts,) = whole(
        weigh_joint,
        [((DP, ROWS + 8, JC + MC), bf16)],
        [ids, normed, heads_grad, left, right, both, moved, mixer_parts],
    )
    joint_shard, mixer_shard, vector_shard, squares = whole(
        settle_grads,
        [((ROWS, JC), f32), ((ROWS, MC), f32), ((1, HEAD), f32), ((DP * MP, 1, HEAD), f32)],
        [ids, exchange(joint_parts, "dp"), ff_shard],
    )

    squares = exchange(squares, ("dp", "mp"))

    parts = half_sum(input_near, input_far, after=[joint_parts])
    (done,) = whole(
        finish,
        [((2, PART, D), bf16)],
        [ids, out_sum] + parts + [hidden_part, tok_part, hidden_grad, gain_first],
        limit=8,
    )
    done_parts = gather(shift_y, done)
    anywhere = pl.BlockSpec(memory_space=pl.ANY)
    results = [jax.ShapeDtypeStruct((1, T, D), f32)] * 2
    held = [pltpu.VMEM((2, HALF, D), f32), pltpu.SemaphoreType.DMA((2,))]
    *halves, token = pl.pallas_call(
        settle_near,
        out_shape=results + [jax.ShapeDtypeStruct((8, HEAD), f32)],
        in_specs=[SM] + [VM] * 4,
        out_specs=[anywhere] * 2 + [VM],
        scratch_shapes=held,
        compiler_params=pltpu.CompilerParams(vmem_limit_bytes=16 * MiB),
        cost_estimate=SMALL,
    )(ids, *done_parts)
    (done_near,) = whole(
        pile, [((4, 2, PART, D), bf16)], [ids] + done_parts, after=[squares, token], limit=8
    )
    output, input_grad = pl.pallas_call(
        settle_far,
        out_shape=results,
        in_specs=[SM, VM] + [anywhere] * 2,
        out_specs=[anywhere] * 2,
        input_output_aliases={2: 0, 3: 1},
        scratch_shapes=held,
        compiler_params=pltpu.CompilerParams(vmem_limit_bytes=16 * MiB),
        cost_estimate=SMALL,
    )(ids, swap_core(done_near), *halves)

    matrices = [joint_weight, joint_moment, joint_square]
    matrices += [mixer_weight, mixer_moment, mixer_square]
    matrices += [expand_weight, expand_moment, expand_square]
    matrices += [v.T for v in (shrink_weight, shrink_moment, shrink_square)]
    matrices += [v[None] for v in (vector_params, vector_moment, vector_square)]
    def third(shape):
        n = len(shape)
        if shape[-2] != ROWS:
            return pl.BlockSpec(shape, lambda i: (0,) * n)
        return pl.BlockSpec(
            shape[:-2] + (ROWS // 3, shape[-1]), lambda i: (0,) * (n - 2) + (i, 0)
        )

    given = [squares, joint_shard, mixer_shard, ff_shard, vector_shard] + matrices
    made = [(1, HEAD)] + [v.shape for v in matrices]
    norm, *new = pl.pallas_call(
        update,
        grid=(3,),
        out_shape=[jax.ShapeDtypeStruct(shape, f32) for shape in made],
        in_specs=[third(v.shape) for v in given],
        out_specs=[third(shape) for shape in made],
        compiler_params=pltpu.CompilerParams(vmem_limit_bytes=60 * MiB),
        cost_estimate=SMALL,
    )(*given)
    new[9:12] = [v.T for v in new[9:12]]
    new[12:] = [v[0] for v in new[12:]]
    return (output, input_grad, norm[0, 0], *new)


def solution(mesh):
    row = P("dp", None, None)
    matrix = [P("dp", "mp")] * 6 + [P(None, "dp", "mp")] * 3 + [P("mp", "dp")] * 3
    vector = [P(("dp", "mp"))] * 3
    return jax.shard_map(
        body,
        mesh=mesh,
        in_specs=tuple([row, P("dp"), row] + matrix + vector),
        out_specs=tuple([row, row, P()] + matrix + vector),
        check_vma=False,
    )
```

```python
import jax
import jax.numpy as jnp
import numpy as np
from jax import lax
from jax.experimental import pallas as pl
from jax.experimental.pallas import tpu as pltpu
from jax.sharding import PartitionSpec as P

QUERY_HEADS = 12
KEY_VALUE_HEADS = 2
HEAD = 128
STEP = 5
EPS_NORM = 1e-06
ROPE_BASE = 1000000.0
MAX_NORM = 1.0
BETA_ONE = 0.9
BETA_TWO = 0.95
ADAM_EPS = 1e-08
DECAY = 0.1
RATE_MATRIX = 0.06
RATE_VECTOR = 0.8
MASKED = -1e30

T = 512
HALF = 256
PART = 64
D = 1536
FF = 1120
FP = 1152
DP = 16
MP = 8
ROWS = D // DP
JC = 256
MC = 192
KEY_AT = 6
SCALE = HEAD ** (-0.5)

f32 = jnp.float32
bf16 = jnp.bfloat16
VM = pl.BlockSpec(memory_space=pltpu.VMEM)
SM = pl.BlockSpec(memory_space=pltpu.SMEM)
MiB = 1 << 20
SMALL = pl.CostEstimate(flops=1, bytes_accessed=1, transcendentals=0)


def shift_y(v, k):
    return lax.ppermute(v, "mp", [(i, (i + 2 * k) % MP) for i in range(MP)])


def from_last_chip(v, k):
    return lax.ppermute(v, "mp", [(i, (i + 2 * k) % MP) for i in (MP - 2, MP - 1)])


def to_last_chip(v, y):
    return lax.ppermute(v, "mp", [(2 * y + c, MP - 2 + c) for c in range(2)])


def swap_core(v):
    return lax.ppermute(v, "mp", [(i, i ^ 1) for i in range(MP)])


def exchange(v, axis):
    return lax.all_to_all(v, axis, split_axis=0, concat_axis=0, tiled=True)


RELATIVE = (0, -1, 1, 2)


def gather(shift, v):
    return [v, shift(v, 1), shift(v, -1), shift(v, 2)]


def nn(a, b):
    return lax.dot_general(a, b, (((1,), (0,)), ((), ())), preferred_element_type=f32)


def nt(a, b):
    return lax.dot_general(a, b, (((1,), (1,)), ((), ())), preferred_element_type=f32)


def tn(a, b):
    return lax.dot_general(a, b, (((0,), (0,)), ((), ())), preferred_element_type=f32)


def whole(body, outs, args, scratch=(), limit=60, after=()):
    n = len(args)

    def bare(*refs):
        body(*refs[:n], *refs[n + len(after) :])

    return pl.pallas_call(
        bare,
        out_shape=[jax.ShapeDtypeStruct(s, d) for s, d in outs],
        in_specs=[SM] + [VM] * (n - 1) + [pl.BlockSpec(memory_space=pl.ANY)] * len(after),
        out_specs=[VM] * len(outs),
        scratch_shapes=list(scratch),
        compiler_params=pltpu.CompilerParams(vmem_limit_bytes=limit * MiB),
        cost_estimate=SMALL,
    )(*args, *after)


def at(start, size, step):
    return pl.ds(pl.multiple_of(start, step), size)


def prepare(ids, cotangent, tok, back, back_t, back_part, tok_part, tok_half):
    length, y, c = ids[0], ids[3], ids[4]
    for h in range(2):
        start = HALF * ((c + h) % 2)
        t = lax.broadcasted_iota(jnp.int32, (HALF, 1), 0) + start
        v = cotangent[at(start, HALF, HALF), :]
        v = jnp.where(t < length, v, jnp.zeros_like(v))
        back[HALF * h : HALF * (h + 1), :] = v
        back_t[:, HALF * h : HALF * (h + 1)] = v.T
    back_part[...] = back[at(PART * y, PART, PART), :]
    tok_part[...] = tok[at(HALF * c + PART * y, PART, PART), :]
    tok_half[...] = tok[at(HALF * c, HALF, HALF), :]


def kept(i, n, length):
    t = lax.broadcasted_iota(jnp.int32, (128, n), 0) + 128 * i
    s = lax.broadcasted_iota(jnp.int32, (128, n), 1)
    return (s <= t) & (s < length)


def attend(
    ids, tok, gain, bias, cosine, sine, query_w, pair_w,
    normed, heads, out, lse, w,
):
    w[:, :JC] = query_w[:, :ROWS, :].reshape(D, JC)
    w[:, JC:] = pair_w[:, :ROWS, :].reshape(D, JC)

    @pl.loop(0, T // 128)
    def _(i):
        rows = at(i * 128, 128, 128)
        x = tok[rows, :].astype(f32)
        s = lax.rsqrt(jnp.mean(x * x, -1, keepdims=True) + EPS_NORM)
        n = (x * s * gain[...]).astype(bf16)
        normed[rows, :] = n
        j = nn(n, w[...]) + bias[...]
        for h in range(4):
            cols = slice(HEAD * h, HEAD * (h + 1))
            u = j[:, cols]
            if h < 3:
                u = u * cosine[rows, :] + pltpu.roll(u, HEAD // 2, 1) * sine[rows, :]
            heads[rows, cols] = u.astype(bf16)

    for h in range(2):
        for i in range(4):
            n = 128 * (i + 1)
            q = heads[128 * i : n, HEAD * h : HEAD * (h + 1)]
            k, v = heads[:n, 2 * HEAD : 3 * HEAD], heads[:n, 3 * HEAD :]
            s = jnp.where(kept(i, n, ids[0]), nt(q, k) * SCALE, MASKED)
            m = jnp.max(s, -1, keepdims=True)
            e = jnp.exp(s - m)
            total = jnp.sum(e, -1, keepdims=True)
            o = nn((e / total).astype(bf16), v).astype(bf16)
            lse[128 * i : n, HEAD * h : HEAD * (h + 1)] = jnp.broadcast_to(
                m + jnp.log(total), (128, HEAD)
            )
            at_row = 128 * (i % 2)
            for y in range(4):
                out[2 * y + i // 2, at_row : at_row + 128, HEAD * h : HEAD * (h + 1)] = o


def assemble(ids, a0, a1, a2, a3, b0, b1, b2, b3, mixer, rows_w):
    y, c = ids[3], ids[4]
    for e, a, b in zip(RELATIVE, (a0, a1, a2, a3), (b0, b1, b2, b3)):
        first = 384 * lax.rem(y + e + 4, 4)
        left, right = at(first, JC, 128), at(first + JC, HEAD, 128)
        for d in range(DP):
            for half, v in ((c, a), (1 - c, b)):
                row = ROWS * d + 48 * half
                mixer[at(row, 48, 16), left] = v[d, :48, :]
                mixer[at(row, 32, 16), right] = v[d, 48:80, :HEAD]
                mixer[at(row + 32, 16, 16), right] = v[d, 48:64, HEAD:]
    rows_w[...] = mixer[at(JC * jnp.minimum(ids[2], KEY_AT - 1), JC, JC), :]


def mix(ids, att, mixer, tok, gain, hidden_part, normed, hidden, side):
    i = pl.program_id(0)

    @pl.when(i == 0)
    def _():
        for j in range(KEY_AT):
            side[:, JC * j : JC * (j + 1)] = att[j]

    cols = at(384 * i, 384, 384)
    hidden[:, cols] = nn(side[...], mixer[...]) + tok[...].astype(f32)

    @pl.when(i == 3)
    def _():
        hidden_part[...] = hidden[at(PART * ids[3], PART, PART), :]
        for r in range(0, HALF, 64):
            v = hidden[r : r + 64, :]
            s = lax.rsqrt(jnp.mean(v * v, -1, keepdims=True) + EPS_NORM)
            normed[r : r + 64, :] = (v * s * gain[...]).astype(bf16)


def gated(near, far, back, back_t, w, act, gate_grad, up_grad, grads, near_t):
    @pl.when(pl.program_id(0) == 0)
    def _():
        near_t[:, :HALF] = near[...].T
        near_t[:, HALF:] = far[...].T

    gate_w, up_w, down_w = [w[:, m].reshape(D, 256) for m in range(3)]
    for r, normed in ((0, near), (HALF, far)):
        rows = slice(r, r + HALF)
        g = nn(normed[...], gate_w)
        u = nn(normed[...], up_w)
        a = nn(back[rows, :], down_w)
        sigma = 1.0 / (1.0 + jnp.exp(-g))
        swished = g * sigma
        act[rows, :] = (swished * u).astype(bf16)
        gate_grad[rows, :] = (a * u * sigma * (1.0 + g * (1.0 - sigma))).astype(bf16)
        up_grad[rows, :] = (a * swished).astype(bf16)
    for m, (left, right) in enumerate(((near_t, gate_grad), (near_t, up_grad), (back_t, act))):
        for r in range(4):
            part = nn(left[384 * r : 384 * (r + 1), :], right[...]).astype(bf16)
            grads[4 * r : 4 * (r + 1), m] = part.reshape(4, ROWS, 256)


def spread(gate_grad, up_grad, w, near, far):
    gate_w, up_w = [w[:, m].reshape(768, FP) for m in range(2)]
    for b in range(3):
        cols = slice(256 * b, 256 * (b + 1))
        part = nt(gate_grad[...], gate_w[cols]) + nt(up_grad[...], up_w[cols])
        near[:, cols] = part[:HALF].astype(bf16)
        far[:, cols] = part[HALF:].astype(bf16)


def spread_out(act, w, near, far):
    down_w = w[:, 0].reshape(768, FP)
    for b in range(3):
        cols = slice(256 * b, 256 * (b + 1))
        part = nt(act[...], down_w[cols])
        near[:, cols] = part[:HALF].astype(bf16)
        far[:, cols] = part[HALF:].astype(bf16)


def halve(ids, near, other, own, p1, p2, p3):
    y = ids[3]
    for k, out in ((0, own), (1, p1), (3, p2), (2, p3)):
        rows = at(PART * lax.rem(y + k, 4), PART, PART)
        out[...] = (near[rows, :].astype(f32) + other[rows, :].astype(f32)).astype(out.dtype)


def summed(own, parts):
    total = own[...]
    for part in parts:
        total += part[...].astype(f32)
    return total


def hidden_back(ids, own, a1, a2, a3, hidden, back, gain, grad, low, gain_part):
    h = hidden[...]
    g = summed(own, (a1, a2, a3))
    scale = lax.rsqrt(jnp.mean(h * h, -1, keepdims=True) + EPS_NORM)
    gain_part[...] = jnp.sum(g * h * scale, 0, keepdims=True)
    v = back[...].astype(f32) + norm_back(h, scale, gain[...], g)
    grad[...] = v
    low[...] = v.astype(bf16)


def add_parts(ids, own, a1, a2, a3, total):
    total[...] = summed(own, (a1, a2, a3))


def finish(ids, out_sum, own, a1, a2, a3, hidden, tok, grad, gain, done):
    length, y, c = ids[0], ids[3], ids[4]
    o, g = out_sum[...], summed(own, (a1, a2, a3))
    t = lax.broadcasted_iota(jnp.int32, (PART, 1), 0) + HALF * c + PART * y
    done[0] = jnp.where(t < length, o + hidden[...], 0.0).astype(bf16)
    x = tok[...].astype(f32)
    scale = lax.rsqrt(jnp.mean(x * x, -1, keepdims=True) + EPS_NORM)
    done[1] = (grad[...] + norm_back(x, scale, gain[...], g)).astype(bf16)


def attend_back(
    ids, near, far, rows_w, heads, lse, cosine, sine,
    grads, window, own_kind, other_kind, low, att_grad, key_grad, value_grad,
):
    length, y, c = ids[0], ids[3], ids[4]
    for k, e in enumerate(RELATIVE):
        place = PART * lax.rem(y + e + 4, 4)
        low[at(HALF * c + place, PART, PART), :] = near[k]
        low[at(HALF * (1 - c) + place, PART, PART), :] = far[k]
    window[...] = low[:, at(384 * y, 384, 384)]
    has_heads = (ids[2] < KEY_AT).astype(f32)
    att_grad[...] = (nt(low[...], rows_w[...]) * has_heads).astype(bf16)
    key_grad[...] = jnp.zeros_like(key_grad)
    value_grad[...] = jnp.zeros_like(value_grad)
    for h in range(2):
        cols = slice(HEAD * h, HEAD * (h + 1))
        for i in range(4):
            n = 128 * (i + 1)
            rows = slice(128 * i, n)
            q = heads[rows, cols]
            k, v = heads[:n, 2 * HEAD : 3 * HEAD], heads[:n, 3 * HEAD :]
            o = att_grad[rows, cols]
            s = nt(q, k) * SCALE
            p = jnp.where(kept(i, n, length), jnp.exp(s - lse[rows, HEAD * h : HEAD * h + 1]), 0.0)
            d = nt(o, v)
            g = (p * (d - jnp.sum(p * d, -1, keepdims=True))).astype(bf16)
            value_grad[:n, :] += tn(p.astype(bf16), o)
            key_grad[:n, :] += tn(g, q)
            dq = nn(g, k) * SCALE
            dq = dq * cosine[rows, :] - pltpu.roll(dq, HEAD // 2, 1) * sine[rows, :]
            grads[rows, cols] = dq.astype(bf16)
    dk = key_grad[...] * SCALE
    dk = dk * cosine[...] - pltpu.roll(dk, HEAD // 2, 1) * sine[...]
    grads[:, 2 * HEAD : 3 * HEAD] = dk.astype(bf16)
    grads[:, 3 * HEAD :] = value_grad[...].astype(bf16)
    k, v = grads[:, 2 * HEAD : 3 * HEAD], grads[:, 3 * HEAD :]

    @pl.when(c == 0)
    def _():
        own_kind[...] = k
        other_kind[...] = v

    @pl.when(c != 0)
    def _():
        own_kind[...] = v
        other_kind[...] = k


def joint_back(
    ids, grads, w, tok, second_part,
    near, far, chunks, gain_part, vec, blocks,
):
    g = grads[...]
    gain_part[...] = jnp.zeros_like(gain_part)
    for r in range(0, T, 128):
        rows = slice(r, r + 128)
        back = nt(g[rows], w[...])
        half, place = r // HALF, slice(r % HALF, r % HALF + 128)
        moves = back.astype(bf16)

        @pl.when(ids[4] == half)
        def _():
            near[place, :] = moves

        @pl.when(ids[4] != half)
        def _():
            far[place, :] = moves

        x = tok[rows, :].astype(f32)
        s = lax.rsqrt(jnp.mean(x * x, -1, keepdims=True) + EPS_NORM)
        gain_part[...] += jnp.sum(back * x * s, 0, keepdims=True)
    vec[...] = jnp.zeros_like(vec)
    vec[:, :D] = gain_part[...]
    vec[:, D : 2 * D] = second_part[...]
    bias = jnp.sum(g.astype(f32), 0, keepdims=True)
    head_at = jnp.minimum(ids[2], KEY_AT - 1)
    key_start = 2 * D + JC * KEY_AT + HEAD * lax.div(head_at, 3)
    vec[:, at(2 * D + JC * head_at, JC, JC)] = bias[:, :JC]
    vec[:, at(key_start, HEAD, HEAD)] = bias[:, JC : JC + HEAD]
    vec[:, at(key_start + JC, HEAD, HEAD)] = bias[:, JC + HEAD :]
    for d in range(DP):
        blocks[d : d + 1, :] = vec[:, 320 * d : 320 * (d + 1)]
    for m in range(MP):
        piece = blocks[:, 40 * m : 40 * (m + 1)]
        piece = jnp.concatenate([piece, jnp.zeros((DP, HEAD - 40), f32)], 1)
        high = piece.astype(bf16)
        chunks[m, :DP, :] = high
        chunks[m, DP:, :] = (piece - high.astype(f32)).astype(bf16)


def back_to_input(
    ids, near_low, far_low, rows_w, heads, lse, cosine, sine, w, tok, second_part,
    grads, window, own_kind, other_kind, near, far, chunks,
    low, att_grad, key_grad, value_grad, gain_part, vec, blocks,
):
    attend_back(
        ids, near_low, far_low, rows_w, heads, lse, cosine, sine,
        grads, window, own_kind, other_kind, low, att_grad, key_grad, value_grad,
    )
    joint_back(ids, grads, w, tok, second_part, near, far, chunks, gain_part, vec, blocks)


def group_parts(ids, own, other, both, left, right):
    own_group = lax.div(jnp.minimum(ids[2], KEY_AT - 1), 3)
    partner = ids[2] + 1 - 2 * ids[4]
    other_group = lax.div(jnp.minimum(partner, KEY_AT - 1), 3)
    a, b = own[...].astype(f32), other[...].astype(f32)
    for g, out in ((0, left), (1, right)):
        part = a * (own_group == g).astype(f32) + b * (other_group == g).astype(f32)
        out[...] = part.astype(bf16)
        both[:, HEAD * g : HEAD * (g + 1)] = part.astype(bf16)


def weigh_joint(ids, normed, grads, left, right, both, moved, mixer_parts, parts):
    pair = jnp.concatenate([left[...].astype(f32), right[...].astype(f32)], 1)
    pair = pair + both[...].astype(f32)
    own = grads[:, :JC].astype(f32)
    g = jnp.where(ids[2] < KEY_AT, own, pair).astype(bf16)
    for r in range(4):
        cols = slice(384 * r, 384 * (r + 1))
        part = tn(normed[:, cols], g).astype(bf16)
        parts[4 * r : 4 * (r + 1), :ROWS, :] = part.reshape(4, ROWS, JC)
    parts[:, ROWS : ROWS + 80, :] = mixer_parts[...]
    vec = moved[0].astype(f32)
    for j in range(1, MP):
        vec += moved[j].astype(f32)
    vec = vec[:DP] + vec[DP:]
    high = vec.astype(bf16).astype(f32)
    for d in range(DP):
        parts[d, ROWS + 80 :, :HEAD] = jnp.broadcast_to(high[d : d + 1], (8, HEAD)).astype(bf16)
        low = (vec - high)[d : d + 1]
        parts[d, ROWS + 80 :, HEAD:] = jnp.broadcast_to(low, (8, HEAD)).astype(bf16)


def weigh_mixer(ids, near, far, low, packed, parts):
    c = ids[4]

    def own_columns(half):
        v = low[at(HALF * half, HALF, HALF), :].astype(f32)
        return jnp.where(c == 0, v[:, :MC], v[:, MC:]).astype(bf16)

    mine, other = own_columns(c), own_columns(1 - c)
    for j in range(KEY_AT):
        part = tn(near[j], mine) + tn(far[j], other)
        start = JC * j
        while start < JC * (j + 1):
            stop = min((start // ROWS + 1) * ROWS, JC * (j + 1))
            first = start % ROWS
            parts[start // ROWS, first : first + stop - start, :] = part[
                start - JC * j : stop - JC * j
            ]
            start = stop
    for d in range(DP):
        left, right = parts[d, :, :HEAD], parts[d, :, HEAD:]
        packed[d, :48, :HEAD] = left[:48].astype(bf16)
        packed[d, :48, HEAD:] = left[48:].astype(bf16)
        packed[d, 48:, :HEAD] = jnp.concatenate([right[:32], right[32:64]], 1).astype(bf16)
        packed[d, 48:, HEAD:] = jnp.concatenate(
            [right[64:], jnp.zeros((32, JC - MC), f32)], 1
        ).astype(bf16)


def square_sums(ids, ff, sums):
    total = jnp.zeros((1, FP), f32)
    for m in range(3):
        v = ff[m].astype(f32)
        total += jnp.sum(v * v, 0, keepdims=True)
    sums[...] = jnp.full(sums.shape, jnp.sum(total), f32)


def settle_grads(ids, moved, sums, joint, mixer, vector, squares):
    total = moved[0].astype(f32)
    for d in range(1, DP):
        total += moved[d].astype(f32)
    joint[...] = total[:ROWS]
    left, right = total[ROWS : ROWS + 48], total[ROWS + 48 : ROWS + 80]
    mixer[:48, :HEAD] = left[:, :HEAD]
    mixer[48:, :HEAD] = left[:, HEAD:]
    mixer[:32, HEAD:] = right[:, : MC - HEAD]
    mixer[32:64, HEAD:] = right[:, MC - HEAD : HEAD]
    mixer[64:, HEAD:] = right[:, HEAD:MC]
    vec = total[ROWS + 80 : ROWS + 81, :HEAD] + total[ROWS + 80 : ROWS + 81, HEAD:]
    vector[...] = vec
    total = total[: ROWS + 80]
    total = jnp.sum(total * total) + jnp.sum(vec * vec)
    squares[...] = jnp.broadcast_to((sums[...] + total)[None], squares.shape)


def update(
    squares, joint_grad, mixer_grad, ff_grad, vector_grad,
    joint_w, joint_m, joint_v, mixer_w, mixer_m, mixer_v, expand_w, expand_m, expand_v,
    shrink_w, shrink_m, shrink_v, vector_w, vector_m, vector_v,
    norm_out, joint_wn, joint_mn, joint_vn, mixer_wn, mixer_mn, mixer_vn,
    expand_wn, expand_mn, expand_vn, shrink_wn, shrink_mn, shrink_vn,
    vector_wn, vector_mn, vector_vn,
):
    norm = jnp.sqrt(jnp.sum(squares[:, 0, :], 0, keepdims=True))
    norm_out[...] = norm
    clip = jnp.minimum(1.0, MAX_NORM / (norm[:, :1] + 1e-06))

    def step(grad, before, after, rate, decay, part=Ellipsis):
        w, m, v = [ref[part] for ref in before]
        results = adam_step(w, clip * grad, m, v, rate, decay)
        for ref, new in zip(after, results):
            ref[part] = new

    step(
        joint_grad[...], (joint_w, joint_m, joint_v), (joint_wn, joint_mn, joint_vn),
        RATE_MATRIX, DECAY,
    )
    step(
        mixer_grad[...], (mixer_w, mixer_m, mixer_v), (mixer_wn, mixer_mn, mixer_vn),
        RATE_MATRIX, DECAY,
    )
    for m in range(2):
        step(
            ff_grad[m, :, :FF].astype(f32),
            (expand_w, expand_m, expand_v), (expand_wn, expand_mn, expand_vn),
            RATE_MATRIX, DECAY, m,
        )
    step(
        ff_grad[2, :, :FF].astype(f32),
        (shrink_w, shrink_m, shrink_v), (shrink_wn, shrink_mn, shrink_vn),
        RATE_MATRIX, DECAY,
    )
    step(
        vector_grad[:, :40], (vector_w, vector_m, vector_v), (vector_wn, vector_mn, vector_vn),
        RATE_VECTOR, 0.0,
    )


def write_half(ids, half, pieces, outs, rows, sems):
    for k, e in enumerate(RELATIVE):
        place = at(PART * lax.rem(ids[3] + e + 4, 4), PART, PART)
        for n in range(2):
            rows[n, place, :] = pieces[k][n].astype(f32)
    copies = [
        pltpu.make_async_copy(rows.at[n], out.at[0, at(HALF * half, HALF, HALF)], sems.at[n])
        for n, out in enumerate(outs)
    ]
    for copy in copies:
        copy.start()
    for copy in copies:
        copy.wait()


def settle_near(ids, p0, p1, p2, p3, output, input_grad, token, rows, sems):
    token[...] = jnp.zeros_like(token)
    write_half(ids, ids[4], (p0, p1, p2, p3), (output, input_grad), rows, sems)


def settle_far(ids, far, _a, _b, output, input_grad, rows, sems):
    pieces = [far.at[k] for k in range(4)]
    write_half(ids, 1 - ids[4], pieces, (output, input_grad), rows, sems)


def pile(ids, p0, p1, p2, p3, out):
    for k, p in enumerate((p0, p1, p2, p3)):
        out[k] = p[...]


def norm_back(v, scale, gain, grad):
    scaled = gain * grad
    return scale * scaled - v * scale * scale * scale * jnp.mean(scaled * v, -1, keepdims=True)


def adam_step(weight, grad, moment, square, rate, decay):
    moment_next = BETA_ONE * moment + (1.0 - BETA_ONE) * grad
    square_next = BETA_TWO * square + (1.0 - BETA_TWO) * grad * grad
    first_hat = moment_next * (1.0 / (1.0 - BETA_ONE**STEP))
    second_hat = square_next * (1.0 / (1.0 - BETA_TWO**STEP))
    weight_next = weight - rate * (first_hat / (jnp.sqrt(second_hat) + ADAM_EPS) + decay * weight)
    return (weight_next, moment_next, square_next)


def tables():
    freq = np.float32(ROPE_BASE) ** (-np.arange(0, HEAD, 2, dtype=np.float32) / np.float32(HEAD))
    angle = np.arange(T, dtype=np.float32)[:, None] * freq.astype(np.float32)[None, :]
    cosine, sine = np.cos(angle), np.sin(angle)
    return (
        np.concatenate([cosine, cosine], -1).astype(np.float32),
        np.concatenate([-sine, sine], -1).astype(np.float32),
    )


def split_low(v):
    high = lax.reduce_precision(v, 8, 7)
    middle = lax.reduce_precision(v - high, 8, 7)
    return [part.astype(bf16) for part in (high, middle, v - high - middle)]


def body(
    tokens, lengths, cotangent,
    joint_weight, joint_moment, joint_square,
    mixer_weight, mixer_moment, mixer_square,
    expand_weight, expand_moment, expand_square,
    shrink_weight, shrink_moment, shrink_square,
    vector_params, vector_moment, vector_square,
):
    dp, mp = lax.axis_index("dp"), lax.axis_index("mp")
    y, c = mp // 2, mp % 2
    tok, length = tokens[0], lengths[0]
    ids = jnp.stack([length, dp, mp, y, c]).astype(jnp.int32)

    stack = jnp.concatenate(
        [expand_weight.astype(bf16), shrink_weight.T.astype(bf16)[None]], 0
    )
    stack = jnp.pad(stack, ((0, 0), (0, 0), (0, FP - FF)))
    ff = lax.all_gather(stack, "dp", axis=0, tiled=False)

    low = jnp.concatenate([joint_weight.astype(bf16), mixer_weight.astype(bf16)], 1)
    vec = jnp.pad(jnp.stack(split_low(vector_params)), ((0, 13), (0, JC + MC - 40)))
    low = jnp.concatenate([low, vec], 0)
    other = swap_core(low)
    first, second = jnp.where(c == 0, low, other), jnp.where(c == 0, other, low)
    pairs = [
        jnp.concatenate([first[:ROWS, cols], second[:ROWS, cols]], 1)
        for cols in (slice(0, HEAD), slice(HEAD, JC))
    ]
    chip = jnp.concatenate([first[:ROWS, JC:], second[:ROWS, JC:]], 1)
    chip = lax.dynamic_slice_in_dim(chip, 48 * c, 48, 0)
    rest = jnp.concatenate([chip[:32, JC:], jnp.pad(chip[32:, JC:], ((0, 16), (0, 0)))], 1)
    sent = jnp.concatenate([low[:ROWS, :JC], chip[:, :JC], rest], 0)
    query_w = exchange(jnp.broadcast_to(sent, (DP,) + sent.shape), "dp")
    vec = jnp.concatenate([first[ROWS:, :HEAD], second[ROWS:, :HEAD]], 1)
    sends = [pairs[0], pairs[1], jnp.where(c == 0, pairs[0], pairs[1])]
    sends = [jnp.concatenate([v, vec], 0) for v in sends]
    a1, a2, a3 = [shift_y(v, k) for v, k in zip(sends, (1, -1, 2))]
    pair = jnp.where(y == 0, a1[:ROWS], jnp.where(y == 2, a2[:ROWS], a3[:ROWS]))
    vec = jnp.stack([vec, a2[ROWS:], a3[ROWS:], a1[ROWS:]])[:, :3]
    vec = lax.dynamic_slice_in_dim(jnp.concatenate([vec, vec]), (4 - y) % 4, 4, 0)
    sent = jnp.concatenate([pair, vec.reshape(12, JC), query_w[0, :4]], 0)
    pair_w = exchange(jnp.broadcast_to(sent, (DP,) + sent.shape), "dp")
    vec = pair_w[:, ROWS : ROWS + 12].astype(f32).reshape(DP, 4, 3, 2, HEAD)[..., :40]
    vec = vec[:, :, 0] + vec[:, :, 1] + vec[:, :, 2]
    vec = vec.reshape(-1)

    gain_first, gain_second = vec[None, :D], vec[None, D : 2 * D]
    key_start = JC * KEY_AT + HEAD * (jnp.minimum(mp, KEY_AT - 1) // 3)
    starts = ((JC * mp, JC), (key_start, HEAD), (key_start + JC, HEAD))
    bias = jnp.concatenate(
        [lax.dynamic_slice_in_dim(vec, 2 * D + start, size, 0) for start, size in starts]
    )[None]

    cosine, sine = tables()
    back, back_t, back_part, tok_part, tok_half = whole(
        prepare,
        [
            ((T, D), bf16), ((D, T), bf16),
            ((PART, D), bf16), ((PART, D), bf16), ((HALF, D), bf16),
        ],
        [ids, cotangent[0], tok],
    )
    normed, heads, att_sent, lse, joint_w = whole(
        attend,
        [
            ((T, D), bf16), ((T, 2 * JC), bf16), ((MP, HALF, JC), bf16),
            ((T, JC), f32), ((D, 2 * JC), bf16),
        ],
        [ids, tok, gain_first, bias, cosine, sine, query_w, pair_w],
        after=[back],
    )
    att_near = exchange(att_sent, "mp")
    att_far = swap_core(att_near)
    mixer_near = gather(shift_y, query_w[:, ROWS:])
    mixer_far = [swap_core(v) for v in mixer_near]
    mixer, rows_w = whole(
        assemble, [((D, D), bf16), ((JC, D), bf16)], [ids] + mixer_near + mixer_far
    )

    def fixed(shape):
        return pl.BlockSpec(shape, lambda i: (0,) * len(shape))

    hidden_part, normed_near = pl.pallas_call(
        mix,
        grid=(4,),
        out_shape=[jax.ShapeDtypeStruct((PART, D), f32), jax.ShapeDtypeStruct((HALF, D), bf16)],
        in_specs=[
            SM,
            fixed((MP, HALF, JC)),
            pl.BlockSpec((D, 384), lambda i: (0, i)),
            pl.BlockSpec((HALF, 384), lambda i: (0, i)),
            fixed((1, D)),
        ],
        out_specs=[fixed((PART, D)), fixed((HALF, D))],
        scratch_shapes=[pltpu.VMEM((HALF, D), f32), pltpu.VMEM((HALF, D), bf16)],
        compiler_params=pltpu.CompilerParams(vmem_limit_bytes=60 * MiB),
        cost_estimate=SMALL,
    )(ids, att_near, mixer, tok_half, gain_second)
    normed_far = swap_core(normed_near)

    def columns(n):
        return pl.BlockSpec((n, 256), lambda i: (0, i))

    block = pl.BlockSpec((DP, 3, ROWS, 256), lambda i: (0, 0, 0, i))
    act, gate_grad, up_grad, ff_grads = pl.pallas_call(
        gated,
        grid=(pl.cdiv(FP, 256),),
        out_shape=[jax.ShapeDtypeStruct((T, FP), bf16)] * 3
        + [jax.ShapeDtypeStruct((DP, 3, ROWS, FP), bf16)],
        in_specs=[fixed((HALF, D)), fixed((HALF, D)), fixed((T, D)), fixed((D, T)), block],
        out_specs=[columns(T)] * 3 + [block],
        scratch_shapes=[pltpu.VMEM((D, T), bf16)],
        compiler_params=pltpu.CompilerParams(vmem_limit_bytes=60 * MiB),
        cost_estimate=SMALL,
    )(normed_near, normed_far, back, back_t, ff)
    ff_shard = lax.psum_scatter(ff_grads, "dp", scatter_dimension=0, tiled=False)

    near, far = pl.pallas_call(
        spread,
        grid=(2,),
        out_shape=[jax.ShapeDtypeStruct((HALF, D), bf16)] * 2,
        in_specs=[fixed((T, FP))] * 2
        + [pl.BlockSpec((DP // 2, 2, ROWS, FP), lambda i: (i, 0, 0, 0))],
        out_specs=[pl.BlockSpec((HALF, 768), lambda i: (0, i))] * 2,
        compiler_params=pltpu.CompilerParams(vmem_limit_bytes=60 * MiB),
        cost_estimate=SMALL,
    )(gate_grad, up_grad, ff)

    def half_sum(near, far, after=()):
        own, *parts = whole(
            halve,
            [((PART, D), f32)] + [((PART, D), bf16)] * 3,
            [ids, near, swap_core(far)],
            after=after,
            limit=8,
        )
        return [own] + [shift_y(v, k) for v, k in zip(parts, (1, -1, 2))]

    normed_second_parts = half_sum(near, far)
    out_near, out_far = pl.pallas_call(
        spread_out,
        grid=(2,),
        out_shape=[jax.ShapeDtypeStruct((HALF, D), bf16)] * 2,
        in_specs=[
            fixed((T, FP)),
            pl.BlockSpec((DP // 2, 1, ROWS, FP), lambda i: (i, 2, 0, 0)),
        ],
        out_specs=[pl.BlockSpec((HALF, 768), lambda i: (0, i))] * 2,
        compiler_params=pltpu.CompilerParams(vmem_limit_bytes=60 * MiB),
        cost_estimate=SMALL,
    )(act, ff)
    hidden_grad, low, gain_second_part = whole(
        hidden_back,
        [((PART, D), f32), ((PART, D), bf16), ((1, D), f32)],
        [ids] + normed_second_parts + [hidden_part, back_part, gain_second],
        after=[out_far],
        limit=8,
    )
    out_parts = half_sum(out_near, out_far)
    low_near = jnp.stack(gather(shift_y, low))
    low_far = swap_core(low_near)
    heads_grad, hidden_low, own_kind, other_kind, input_near, input_far, chunks = whole(
        back_to_input,
        [
            ((T, 2 * JC), bf16), ((T, 2 * MC), bf16), ((T, HEAD), bf16), ((T, HEAD), bf16),
            ((HALF, D), bf16), ((HALF, D), bf16), ((MP, 2 * DP, HEAD), bf16),
        ],
        [ids, low_near, low_far, rows_w, heads, lse, cosine, sine, joint_w, tok, gain_second_part],
        scratch=[
            pltpu.VMEM((T, D), bf16),
            pltpu.VMEM((T, JC), bf16),
            pltpu.VMEM((T, HEAD), f32),
            pltpu.VMEM((T, HEAD), f32),
            pltpu.VMEM((1, D), f32),
            pltpu.VMEM((1, DP * MP * 40), f32),
            pltpu.VMEM((DP, MP * 40), f32),
        ],
        after=[out_parts[0]],
    )
    (out_sum,) = whole(
        add_parts, [((PART, D), f32)], [ids] + out_parts, limit=8, after=[heads_grad]
    )
    both, left, right = whole(
        group_parts,
        [((T, JC), bf16), ((T, HEAD), bf16), ((T, HEAD), bf16)],
        [ids, own_kind, swap_core(other_kind)],
        limit=8,
        after=[out_sum],
    )
    left, right, both = to_last_chip(left, 0), to_last_chip(right, 2), to_last_chip(both, 1)
    moved = exchange(chunks, "mp")
    (mixer_parts,) = whole(
        weigh_mixer,
        [((DP, 80, JC), bf16)],
        [ids, att_near, att_far, hidden_low],
        scratch=[pltpu.VMEM((DP, ROWS, MC), f32)],
        after=[out_sum],
    )
    (joint_parts,) = whole(
        weigh_joint,
        [((DP, ROWS + 88, JC), bf16)],
        [ids, normed, heads_grad, left, right, both, moved, mixer_parts],
    )
    (ff_sums,) = whole(square_sums, [((1, HEAD), f32)], [ids, ff_shard])
    joint_shard, mixer_shard, vector_shard, squares = whole(
        settle_grads,
        [((ROWS, JC), f32), ((ROWS, MC), f32), ((1, HEAD), f32), ((DP * MP, 1, HEAD), f32)],
        [ids, exchange(joint_parts, "dp"), ff_sums],
    )

    squares = exchange(squares, ("dp", "mp"))

    parts = half_sum(input_near, input_far, after=[joint_parts])
    (done,) = whole(
        finish,
        [((2, PART, D), bf16)],
        [ids, out_sum] + parts + [hidden_part, tok_part, hidden_grad, gain_first],
        limit=8,
        after=[ff_sums],
    )
    done_parts = gather(shift_y, done)
    anywhere = pl.BlockSpec(memory_space=pl.ANY)
    results = [jax.ShapeDtypeStruct((1, T, D), f32)] * 2
    held = [pltpu.VMEM((2, HALF, D), f32), pltpu.SemaphoreType.DMA((2,))]
    *halves, token = pl.pallas_call(
        settle_near,
        out_shape=results + [jax.ShapeDtypeStruct((8, HEAD), f32)],
        in_specs=[SM] + [VM] * 4,
        out_specs=[anywhere] * 2 + [VM],
        scratch_shapes=held,
        compiler_params=pltpu.CompilerParams(vmem_limit_bytes=16 * MiB),
        cost_estimate=SMALL,
    )(ids, *done_parts)
    (done_near,) = whole(
        pile, [((4, 2, PART, D), bf16)], [ids] + done_parts, after=[squares, token], limit=8
    )
    output, input_grad = pl.pallas_call(
        settle_far,
        out_shape=results,
        in_specs=[SM, VM] + [anywhere] * 2,
        out_specs=[anywhere] * 2,
        input_output_aliases={2: 0, 3: 1},
        scratch_shapes=held,
        compiler_params=pltpu.CompilerParams(vmem_limit_bytes=16 * MiB),
        cost_estimate=SMALL,
    )(ids, swap_core(done_near), *halves)

    matrices = [joint_weight, joint_moment, joint_square]
    matrices += [mixer_weight, mixer_moment, mixer_square]
    matrices += [expand_weight, expand_moment, expand_square]
    matrices += [v.T for v in (shrink_weight, shrink_moment, shrink_square)]
    matrices += [v[None] for v in (vector_params, vector_moment, vector_square)]
    def third(shape):
        n = len(shape)
        if shape[-2] != ROWS:
            return pl.BlockSpec(shape, lambda i: (0,) * n)
        return pl.BlockSpec(
            shape[:-2] + (ROWS // 3, shape[-1]), lambda i: (0,) * (n - 2) + (i, 0)
        )

    given = [squares, joint_shard, mixer_shard, ff_shard, vector_shard] + matrices
    made = [(1, HEAD)] + [v.shape for v in matrices]
    norm, *new = pl.pallas_call(
        update,
        grid=(3,),
        out_shape=[jax.ShapeDtypeStruct(shape, f32) for shape in made],
        in_specs=[third(v.shape) for v in given],
        out_specs=[third(shape) for shape in made],
        compiler_params=pltpu.CompilerParams(vmem_limit_bytes=60 * MiB),
        cost_estimate=SMALL,
    )(*given)
    new[9:12] = [v.T for v in new[9:12]]
    new[12:] = [v[0] for v in new[12:]]
    return (output, input_grad, norm[0, 0], *new)


def solution(mesh):
    row = P("dp", None, None)
    matrix = [P("dp", "mp")] * 6 + [P(None, "dp", "mp")] * 3 + [P("mp", "dp")] * 3
    vector = [P(("dp", "mp"))] * 3
    return jax.shard_map(
        body,
        mesh=mesh,
        in_specs=tuple([row, P("dp"), row] + matrix + vector),
        out_specs=tuple([row, row, P()] + matrix + vector),
        check_vma=False,
    )
```

```python
import jax
import jax.numpy as jnp
import numpy as np
from jax import lax
from jax.experimental import pallas as pl
from jax.experimental.pallas import tpu as pltpu
from jax.sharding import PartitionSpec as P

QUERY_HEADS = 12
KEY_VALUE_HEADS = 2
HEAD = 128
STEP = 5
EPS_NORM = 1e-06
ROPE_BASE = 1000000.0
MAX_NORM = 1.0
BETA_ONE = 0.9
BETA_TWO = 0.95
ADAM_EPS = 1e-08
DECAY = 0.1
RATE_MATRIX = 0.06
RATE_VECTOR = 0.8
MASKED = -1e30

T = 512
HALF = 256
PART = 64
D = 1536
FF = 1120
FP = 1152
DP = 16
MP = 8
ROWS = D // DP
JC = 256
MC = 192
KEY_AT = 6
SCALE = HEAD ** (-0.5)

f32 = jnp.float32
bf16 = jnp.bfloat16
VM = pl.BlockSpec(memory_space=pltpu.VMEM)
SM = pl.BlockSpec(memory_space=pltpu.SMEM)
MiB = 1 << 20
SMALL = pl.CostEstimate(flops=1, bytes_accessed=1, transcendentals=0)


def shift_y(v, k):
    return lax.ppermute(v, "mp", [(i, (i + 2 * k) % MP) for i in range(MP)])


def from_last_chip(v, k):
    return lax.ppermute(v, "mp", [(i, (i + 2 * k) % MP) for i in (MP - 2, MP - 1)])


def to_last_chip(v, y):
    return lax.ppermute(v, "mp", [(2 * y + c, MP - 2 + c) for c in range(2)])


def swap_core(v):
    return lax.ppermute(v, "mp", [(i, i ^ 1) for i in range(MP)])


def exchange(v, axis):
    return lax.all_to_all(v, axis, split_axis=0, concat_axis=0, tiled=True)


RELATIVE = (0, -1, 1, 2)


def gather(shift, v):
    return [v, shift(v, 1), shift(v, -1), shift(v, 2)]


def nn(a, b):
    return lax.dot_general(a, b, (((1,), (0,)), ((), ())), preferred_element_type=f32)


def nt(a, b):
    return lax.dot_general(a, b, (((1,), (1,)), ((), ())), preferred_element_type=f32)


def tn(a, b):
    return lax.dot_general(a, b, (((0,), (0,)), ((), ())), preferred_element_type=f32)


def whole(body, outs, args, scratch=(), limit=60, after=(), loose=()):
    n = len(args)

    def bare(*refs):
        body(*refs[:n], *refs[n + len(after) :])

    return pl.pallas_call(
        bare,
        out_shape=[jax.ShapeDtypeStruct(s, d) for s, d in outs],
        in_specs=[SM]
        + [pl.BlockSpec(memory_space=pl.ANY) if k in loose else VM for k in range(1, n)]
        + [pl.BlockSpec(memory_space=pl.ANY)] * len(after),
        out_specs=[VM] * len(outs),
        scratch_shapes=list(scratch),
        compiler_params=pltpu.CompilerParams(vmem_limit_bytes=limit * MiB),
        cost_estimate=SMALL,
    )(*args, *after)


def at(start, size, step):
    return pl.ds(pl.multiple_of(start, step), size)


def prepare(ids, cotangent, tok, back, back_t, back_part, tok_part, tok_half):
    length, y, c = ids[0], ids[3], ids[4]
    for h in range(2):
        start = HALF * ((c + h) % 2)
        t = lax.broadcasted_iota(jnp.int32, (HALF, 1), 0) + start
        v = cotangent[at(start, HALF, HALF), :]
        v = jnp.where(t < length, v, jnp.zeros_like(v))
        back[HALF * h : HALF * (h + 1), :] = v
        back_t[:, HALF * h : HALF * (h + 1)] = v.T
    back_part[...] = back[at(PART * y, PART, PART), :]
    tok_part[...] = tok[at(HALF * c + PART * y, PART, PART), :]
    tok_half[...] = tok[at(HALF * c, HALF, HALF), :]


def kept(i, n, length):
    t = lax.broadcasted_iota(jnp.int32, (128, n), 0) + 128 * i
    s = lax.broadcasted_iota(jnp.int32, (128, n), 1)
    return (s <= t) & (s < length)


def attend(
    ids, tok, gain, bias, cosine, sine, query_w, pair_w,
    normed, heads, out, lse, w,
):
    w[:, :JC] = query_w[:, :ROWS, :].reshape(D, JC)
    w[:, JC:] = pair_w[:, :ROWS, :].reshape(D, JC)

    @pl.loop(0, T // 128)
    def _(i):
        rows = at(i * 128, 128, 128)
        x = tok[rows, :].astype(f32)
        s = lax.rsqrt(jnp.mean(x * x, -1, keepdims=True) + EPS_NORM)
        n = (x * s * gain[...]).astype(bf16)
        normed[rows, :] = n
        j = nn(n, w[...]) + bias[...]
        for h in range(4):
            cols = slice(HEAD * h, HEAD * (h + 1))
            u = j[:, cols]
            if h < 3:
                u = u * cosine[rows, :] + pltpu.roll(u, HEAD // 2, 1) * sine[rows, :]
            heads[rows, cols] = u.astype(bf16)

    for h in range(2):
        for i in range(4):
            n = 128 * (i + 1)
            q = heads[128 * i : n, HEAD * h : HEAD * (h + 1)]
            k, v = heads[:n, 2 * HEAD : 3 * HEAD], heads[:n, 3 * HEAD :]
            s = jnp.where(kept(i, n, ids[0]), nt(q, k) * SCALE, MASKED)
            m = jnp.max(s, -1, keepdims=True)
            e = jnp.exp(s - m)
            total = jnp.sum(e, -1, keepdims=True)
            o = nn((e / total).astype(bf16), v).astype(bf16)
            lse[128 * i : n, HEAD * h : HEAD * (h + 1)] = jnp.broadcast_to(
                m + jnp.log(total), (128, HEAD)
            )
            at_row = 128 * (i % 2)
            for y in range(4):
                out[2 * y + i // 2, at_row : at_row + 128, HEAD * h : HEAD * (h + 1)] = o


def assemble(ids, a0, a1, a2, a3, b0, b1, b2, b3, mixer, rows_w):
    y, c = ids[3], ids[4]
    for e, a, b in zip(RELATIVE, (a0, a1, a2, a3), (b0, b1, b2, b3)):
        first = 384 * lax.rem(y + e + 4, 4)
        left, right = at(first, JC, 128), at(first + JC, HEAD, 128)
        for d in range(DP):
            for half, v in ((c, a), (1 - c, b)):
                row = ROWS * d + 48 * half
                mixer[at(row, 48, 16), left] = v[d, :48, :]
                mixer[at(row, 32, 16), right] = v[d, 48:80, :HEAD]
                mixer[at(row + 32, 16, 16), right] = v[d, 48:64, HEAD:]
    rows_w[...] = mixer[at(JC * jnp.minimum(ids[2], KEY_AT - 1), JC, JC), :]


def mix(ids, att, mixer, tok, gain, hidden_part, normed, hidden, side):
    i = pl.program_id(0)

    @pl.when(i == 0)
    def _():
        for j in range(KEY_AT):
            side[:, JC * j : JC * (j + 1)] = att[j]

    cols = at(384 * i, 384, 384)
    hidden[:, cols] = nn(side[...], mixer[...]) + tok[...].astype(f32)

    @pl.when(i == 3)
    def _():
        hidden_part[...] = hidden[at(PART * ids[3], PART, PART), :]
        for r in range(0, HALF, 64):
            v = hidden[r : r + 64, :]
            s = lax.rsqrt(jnp.mean(v * v, -1, keepdims=True) + EPS_NORM)
            normed[r : r + 64, :] = (v * s * gain[...]).astype(bf16)


def gated(near, far, back, back_t, w, act, gate_grad, up_grad, grads, near_t):
    @pl.when(pl.program_id(0) == 0)
    def _():
        near_t[:, :HALF] = near[...].T
        near_t[:, HALF:] = far[...].T

    gate_w, up_w, down_w = [w[:, m].reshape(D, 256) for m in range(3)]
    for r, normed in ((0, near), (HALF, far)):
        rows = slice(r, r + HALF)
        g = nn(normed[...], gate_w)
        u = nn(normed[...], up_w)
        a = nn(back[rows, :], down_w)
        sigma = 1.0 / (1.0 + jnp.exp(-g))
        swished = g * sigma
        act[rows, :] = (swished * u).astype(bf16)
        gate_grad[rows, :] = (a * u * sigma * (1.0 + g * (1.0 - sigma))).astype(bf16)
        up_grad[rows, :] = (a * swished).astype(bf16)
    for m, (left, right) in enumerate(((near_t, gate_grad), (near_t, up_grad), (back_t, act))):
        for r in range(4):
            part = nn(left[384 * r : 384 * (r + 1), :], right[...]).astype(bf16)
            grads[4 * r : 4 * (r + 1), m] = part.reshape(4, ROWS, 256)


def spread(gate_grad, up_grad, w, near, far):
    gate_w, up_w = [w[:, m].reshape(768, FP) for m in range(2)]
    for b in range(3):
        cols = slice(256 * b, 256 * (b + 1))
        part = nt(gate_grad[...], gate_w[cols]) + nt(up_grad[...], up_w[cols])
        near[:, cols] = part[:HALF].astype(bf16)
        far[:, cols] = part[HALF:].astype(bf16)


def spread_out(act, w, near, far):
    down_w = w[:, 0].reshape(768, FP)
    for b in range(3):
        cols = slice(256 * b, 256 * (b + 1))
        part = nt(act[...], down_w[cols])
        near[:, cols] = part[:HALF].astype(bf16)
        far[:, cols] = part[HALF:].astype(bf16)


def halve(ids, near, other, own, p1, p2, p3):
    y = ids[3]
    for k, out in ((0, own), (1, p1), (3, p2), (2, p3)):
        rows = at(PART * lax.rem(y + k, 4), PART, PART)
        out[...] = (near[rows, :].astype(f32) + other[rows, :].astype(f32)).astype(out.dtype)


def summed(own, parts):
    total = own[...]
    for part in parts:
        total += part[...].astype(f32)
    return total


def hidden_back(ids, own, a1, a2, a3, hidden, back, gain, grad, low, gain_part):
    h = hidden[...]
    g = summed(own, (a1, a2, a3))
    scale = lax.rsqrt(jnp.mean(h * h, -1, keepdims=True) + EPS_NORM)
    gain_part[...] = jnp.sum(g * h * scale, 0, keepdims=True)
    v = back[...].astype(f32) + norm_back(h, scale, gain[...], g)
    grad[...] = v
    low[...] = v.astype(bf16)


def finish(ids, out_sum, own, a1, a2, a3, hidden, tok, grad, gain, done):
    length, y, c = ids[0], ids[3], ids[4]
    o, g = out_sum[...], summed(own, (a1, a2, a3))
    t = lax.broadcasted_iota(jnp.int32, (PART, 1), 0) + HALF * c + PART * y
    done[0] = jnp.where(t < length, o + hidden[...], 0.0).astype(bf16)
    x = tok[...].astype(f32)
    scale = lax.rsqrt(jnp.mean(x * x, -1, keepdims=True) + EPS_NORM)
    done[1] = (grad[...] + norm_back(x, scale, gain[...], g)).astype(bf16)


def attend_back(
    ids, near, far, rows_w, heads, lse, cosine, sine,
    grads, window, own_kind, other_kind, low, att_grad, key_grad, value_grad,
):
    length, y, c = ids[0], ids[3], ids[4]
    for k, e in enumerate(RELATIVE):
        place = PART * lax.rem(y + e + 4, 4)
        low[at(HALF * c + place, PART, PART), :] = near[k]
        low[at(HALF * (1 - c) + place, PART, PART), :] = far[k]
    window[...] = low[:, at(384 * y, 384, 384)]
    has_heads = (ids[2] < KEY_AT).astype(f32)
    att_grad[...] = (nt(low[...], rows_w[...]) * has_heads).astype(bf16)
    key_grad[...] = jnp.zeros_like(key_grad)
    value_grad[...] = jnp.zeros_like(value_grad)
    for h in range(2):
        cols = slice(HEAD * h, HEAD * (h + 1))
        for i in range(4):
            n = 128 * (i + 1)
            rows = slice(128 * i, n)
            q = heads[rows, cols]
            k, v = heads[:n, 2 * HEAD : 3 * HEAD], heads[:n, 3 * HEAD :]
            o = att_grad[rows, cols]
            s = nt(q, k) * SCALE
            p = jnp.where(kept(i, n, length), jnp.exp(s - lse[rows, HEAD * h : HEAD * h + 1]), 0.0)
            d = nt(o, v)
            g = (p * (d - jnp.sum(p * d, -1, keepdims=True))).astype(bf16)
            value_grad[:n, :] += tn(p.astype(bf16), o)
            key_grad[:n, :] += tn(g, q)
            dq = nn(g, k) * SCALE
            dq = dq * cosine[rows, :] - pltpu.roll(dq, HEAD // 2, 1) * sine[rows, :]
            grads[rows, cols] = dq.astype(bf16)
    dk = key_grad[...] * SCALE
    dk = dk * cosine[...] - pltpu.roll(dk, HEAD // 2, 1) * sine[...]
    grads[:, 2 * HEAD : 3 * HEAD] = dk.astype(bf16)
    grads[:, 3 * HEAD :] = value_grad[...].astype(bf16)
    k, v = grads[:, 2 * HEAD : 3 * HEAD], grads[:, 3 * HEAD :]

    @pl.when(c == 0)
    def _():
        own_kind[...] = k
        other_kind[...] = v

    @pl.when(c != 0)
    def _():
        own_kind[...] = v
        other_kind[...] = k


def joint_back(
    ids, grads, w, tok, second_part,
    near, far, chunks, gain_part, vec, blocks,
):
    g = grads[...]
    gain_part[...] = jnp.zeros_like(gain_part)
    for r in range(0, T, 128):
        rows = slice(r, r + 128)
        back = nt(g[rows], w[...])
        half, place = r // HALF, slice(r % HALF, r % HALF + 128)
        moves = back.astype(bf16)

        @pl.when(ids[4] == half)
        def _():
            near[place, :] = moves

        @pl.when(ids[4] != half)
        def _():
            far[place, :] = moves

        x = tok[rows, :].astype(f32)
        s = lax.rsqrt(jnp.mean(x * x, -1, keepdims=True) + EPS_NORM)
        gain_part[...] += jnp.sum(back * x * s, 0, keepdims=True)
    vec[...] = jnp.zeros_like(vec)
    vec[:, :D] = gain_part[...]
    vec[:, D : 2 * D] = second_part[...]
    bias = jnp.sum(g.astype(f32), 0, keepdims=True)
    head_at = jnp.minimum(ids[2], KEY_AT - 1)
    key_start = 2 * D + JC * KEY_AT + HEAD * lax.div(head_at, 3)
    vec[:, at(2 * D + JC * head_at, JC, JC)] = bias[:, :JC]
    vec[:, at(key_start, HEAD, HEAD)] = bias[:, JC : JC + HEAD]
    vec[:, at(key_start + JC, HEAD, HEAD)] = bias[:, JC + HEAD :]
    for d in range(DP):
        blocks[d : d + 1, :] = vec[:, 320 * d : 320 * (d + 1)]
    for m in range(MP):
        piece = blocks[:, 40 * m : 40 * (m + 1)]
        piece = jnp.concatenate([piece, jnp.zeros((DP, HEAD - 40), f32)], 1)
        high = piece.astype(bf16)
        chunks[m, :DP, :] = high
        chunks[m, DP:, :] = (piece - high.astype(f32)).astype(bf16)


def back_to_input(
    ids, near_low, far_low, rows_w, heads, lse, cosine, sine, w, tok, second_part,
    grads, window, own_kind, other_kind, near, far, chunks,
    low, att_grad, key_grad, value_grad, gain_part, vec, blocks, w_held, tok_held, sems,
):
    copies = [
        pltpu.make_async_copy(w, w_held, sems.at[0]),
        pltpu.make_async_copy(tok, tok_held, sems.at[1]),
    ]
    for copy in copies:
        copy.start()
    attend_back(
        ids, near_low, far_low, rows_w, heads, lse, cosine, sine,
        grads, window, own_kind, other_kind, low, att_grad, key_grad, value_grad,
    )
    for copy in copies:
        copy.wait()
    joint_back(ids, grads, w_held, tok_held, second_part, near, far, chunks, gain_part, vec, blocks)


def group_parts(ids, own, other, o0, o1, o2, o3, both, left, right, out_sum):
    out_sum[...] = summed(o0, (o1, o2, o3))
    own_group = lax.div(jnp.minimum(ids[2], KEY_AT - 1), 3)
    partner = ids[2] + 1 - 2 * ids[4]
    other_group = lax.div(jnp.minimum(partner, KEY_AT - 1), 3)
    a, b = own[...].astype(f32), other[...].astype(f32)
    for g, out in ((0, left), (1, right)):
        part = a * (own_group == g).astype(f32) + b * (other_group == g).astype(f32)
        out[...] = part.astype(bf16)
        both[:, HEAD * g : HEAD * (g + 1)] = part.astype(bf16)


def weigh_joint(ids, normed, grads, left, right, both, moved, mixer_parts, parts):
    pair = jnp.concatenate([left[...].astype(f32), right[...].astype(f32)], 1)
    pair = pair + both[...].astype(f32)
    own = grads[:, :JC].astype(f32)
    g = jnp.where(ids[2] < KEY_AT, own, pair).astype(bf16)
    for r in range(4):
        cols = slice(384 * r, 384 * (r + 1))
        part = tn(normed[:, cols], g).astype(bf16)
        parts[4 * r : 4 * (r + 1), :ROWS, :] = part.reshape(4, ROWS, JC)
    parts[:, ROWS : ROWS + 80, :] = mixer_parts[...]
    vec = moved[0].astype(f32)
    for j in range(1, MP):
        vec += moved[j].astype(f32)
    vec = vec[:DP] + vec[DP:]
    high = vec.astype(bf16).astype(f32)
    for d in range(DP):
        parts[d, ROWS + 80 :, :HEAD] = jnp.broadcast_to(high[d : d + 1], (8, HEAD)).astype(bf16)
        low = (vec - high)[d : d + 1]
        parts[d, ROWS + 80 :, HEAD:] = jnp.broadcast_to(low, (8, HEAD)).astype(bf16)


def weigh_mixer(ids, near, far, low, packed, parts):
    c = ids[4]

    def own_columns(half):
        v = low[at(HALF * half, HALF, HALF), :].astype(f32)
        return jnp.where(c == 0, v[:, :MC], v[:, MC:]).astype(bf16)

    mine, other = own_columns(c), own_columns(1 - c)
    for j in range(KEY_AT):
        part = tn(near[j], mine) + tn(far[j], other)
        start = JC * j
        while start < JC * (j + 1):
            stop = min((start // ROWS + 1) * ROWS, JC * (j + 1))
            first = start % ROWS
            parts[start // ROWS, first : first + stop - start, :] = part[
                start - JC * j : stop - JC * j
            ]
            start = stop
    for d in range(DP):
        left, right = parts[d, :, :HEAD], parts[d, :, HEAD:]
        packed[d, :48, :HEAD] = left[:48].astype(bf16)
        packed[d, :48, HEAD:] = left[48:].astype(bf16)
        packed[d, 48:, :HEAD] = jnp.concatenate([right[:32], right[32:64]], 1).astype(bf16)
        packed[d, 48:, HEAD:] = jnp.concatenate(
            [right[64:], jnp.zeros((32, JC - MC), f32)], 1
        ).astype(bf16)


def settle_grads(ids, moved, ff, joint, mixer, vector, squares):
    total = moved[0].astype(f32)
    for d in range(1, DP):
        total += moved[d].astype(f32)
    joint[...] = total[:ROWS]
    left, right = total[ROWS : ROWS + 48], total[ROWS + 48 : ROWS + 80]
    mixer[:48, :HEAD] = left[:, :HEAD]
    mixer[48:, :HEAD] = left[:, HEAD:]
    mixer[:32, HEAD:] = right[:, : MC - HEAD]
    mixer[32:64, HEAD:] = right[:, MC - HEAD : HEAD]
    mixer[64:, HEAD:] = right[:, HEAD:MC]
    vec = total[ROWS + 80 : ROWS + 81, :HEAD] + total[ROWS + 80 : ROWS + 81, HEAD:]
    vector[...] = vec
    total = total[: ROWS + 80]
    total = jnp.sum(total * total) + jnp.sum(vec * vec)
    for m in range(3):
        v = ff[m].astype(f32)
        total += jnp.sum(v * v)
    squares[...] = jnp.full(squares.shape, total, f32)


def update(
    squares, joint_grad, mixer_grad, ff_grad, vector_grad,
    joint_w, joint_m, joint_v, mixer_w, mixer_m, mixer_v, expand_w, expand_m, expand_v,
    shrink_w, shrink_m, shrink_v, vector_w, vector_m, vector_v,
    norm_out, joint_wn, joint_mn, joint_vn, mixer_wn, mixer_mn, mixer_vn,
    expand_wn, expand_mn, expand_vn, shrink_wn, shrink_mn, shrink_vn,
    vector_wn, vector_mn, vector_vn,
):
    norm = jnp.sqrt(jnp.sum(squares[:, 0, :], 0, keepdims=True))
    norm_out[...] = norm
    clip = jnp.minimum(1.0, MAX_NORM / (norm[:, :1] + 1e-06))

    def step(grad, before, after, rate, decay, part=Ellipsis):
        w, m, v = [ref[part] for ref in before]
        results = adam_step(w, clip * grad, m, v, rate, decay)
        for ref, new in zip(after, results):
            ref[part] = new

    step(
        joint_grad[...], (joint_w, joint_m, joint_v), (joint_wn, joint_mn, joint_vn),
        RATE_MATRIX, DECAY,
    )
    step(
        mixer_grad[...], (mixer_w, mixer_m, mixer_v), (mixer_wn, mixer_mn, mixer_vn),
        RATE_MATRIX, DECAY,
    )
    for m in range(2):
        step(
            ff_grad[m, :, :FF].astype(f32),
            (expand_w, expand_m, expand_v), (expand_wn, expand_mn, expand_vn),
            RATE_MATRIX, DECAY, m,
        )
    step(
        ff_grad[2, :, :FF].astype(f32),
        (shrink_w, shrink_m, shrink_v), (shrink_wn, shrink_mn, shrink_vn),
        RATE_MATRIX, DECAY,
    )
    step(
        vector_grad[:, :40], (vector_w, vector_m, vector_v), (vector_wn, vector_mn, vector_vn),
        RATE_VECTOR, 0.0,
    )


def write_half(ids, half, pieces, outs, rows, sems):
    for k, e in enumerate(RELATIVE):
        place = at(PART * lax.rem(ids[3] + e + 4, 4), PART, PART)
        for n in range(2):
            rows[n, place, :] = pieces[k][n].astype(f32)
    copies = [
        pltpu.make_async_copy(rows.at[n], out.at[0, at(HALF * half, HALF, HALF)], sems.at[n])
        for n, out in enumerate(outs)
    ]
    for copy in copies:
        copy.start()
    for copy in copies:
        copy.wait()


def settle_near(ids, p0, p1, p2, p3, output, input_grad, token, rows, sems):
    token[...] = jnp.zeros_like(token)
    write_half(ids, ids[4], (p0, p1, p2, p3), (output, input_grad), rows, sems)


def settle_far(ids, far, _a, _b, output, input_grad, rows, sems):
    pieces = [far.at[k] for k in range(4)]
    write_half(ids, 1 - ids[4], pieces, (output, input_grad), rows, sems)


def pile(ids, p0, p1, p2, p3, out):
    for k, p in enumerate((p0, p1, p2, p3)):
        out[k] = p[...]


def norm_back(v, scale, gain, grad):
    scaled = gain * grad
    return scale * scaled - v * scale * scale * scale * jnp.mean(scaled * v, -1, keepdims=True)


def adam_step(weight, grad, moment, square, rate, decay):
    moment_next = BETA_ONE * moment + (1.0 - BETA_ONE) * grad
    square_next = BETA_TWO * square + (1.0 - BETA_TWO) * grad * grad
    first_hat = moment_next * (1.0 / (1.0 - BETA_ONE**STEP))
    second_hat = square_next * (1.0 / (1.0 - BETA_TWO**STEP))
    weight_next = weight - rate * (first_hat / (jnp.sqrt(second_hat) + ADAM_EPS) + decay * weight)
    return (weight_next, moment_next, square_next)


def tables():
    freq = np.float32(ROPE_BASE) ** (-np.arange(0, HEAD, 2, dtype=np.float32) / np.float32(HEAD))
    angle = np.arange(T, dtype=np.float32)[:, None] * freq.astype(np.float32)[None, :]
    cosine, sine = np.cos(angle), np.sin(angle)
    return (
        np.concatenate([cosine, cosine], -1).astype(np.float32),
        np.concatenate([-sine, sine], -1).astype(np.float32),
    )


def split_low(v):
    high = lax.reduce_precision(v, 8, 7)
    middle = lax.reduce_precision(v - high, 8, 7)
    return [part.astype(bf16) for part in (high, middle, v - high - middle)]


def body(
    tokens, lengths, cotangent,
    joint_weight, joint_moment, joint_square,
    mixer_weight, mixer_moment, mixer_square,
    expand_weight, expand_moment, expand_square,
    shrink_weight, shrink_moment, shrink_square,
    vector_params, vector_moment, vector_square,
):
    dp, mp = lax.axis_index("dp"), lax.axis_index("mp")
    y, c = mp // 2, mp % 2
    tok, length = tokens[0], lengths[0]
    ids = jnp.stack([length, dp, mp, y, c]).astype(jnp.int32)

    stack = jnp.concatenate(
        [expand_weight.astype(bf16), shrink_weight.T.astype(bf16)[None]], 0
    )
    stack = jnp.pad(stack, ((0, 0), (0, 0), (0, FP - FF)))
    ff = lax.all_gather(stack, "dp", axis=0, tiled=False)

    low = jnp.concatenate([joint_weight.astype(bf16), mixer_weight.astype(bf16)], 1)
    vec = jnp.pad(jnp.stack(split_low(vector_params)), ((0, 13), (0, JC + MC - 40)))
    low = jnp.concatenate([low, vec], 0)
    other = swap_core(low)
    first, second = jnp.where(c == 0, low, other), jnp.where(c == 0, other, low)
    pairs = [
        jnp.concatenate([first[:ROWS, cols], second[:ROWS, cols]], 1)
        for cols in (slice(0, HEAD), slice(HEAD, JC))
    ]
    chip = jnp.concatenate([first[:ROWS, JC:], second[:ROWS, JC:]], 1)
    chip = lax.dynamic_slice_in_dim(chip, 48 * c, 48, 0)
    rest = jnp.concatenate([chip[:32, JC:], jnp.pad(chip[32:, JC:], ((0, 16), (0, 0)))], 1)
    sent = jnp.concatenate([low[:ROWS, :JC], chip[:, :JC], rest], 0)
    query_w = exchange(jnp.broadcast_to(sent, (DP,) + sent.shape), "dp")
    vec = jnp.concatenate([first[ROWS:, :HEAD], second[ROWS:, :HEAD]], 1)
    sends = [pairs[0], pairs[1], jnp.where(c == 0, pairs[0], pairs[1])]
    sends = [jnp.concatenate([v, vec], 0) for v in sends]
    a1, a2, a3 = [shift_y(v, k) for v, k in zip(sends, (1, -1, 2))]
    pair = jnp.where(y == 0, a1[:ROWS], jnp.where(y == 2, a2[:ROWS], a3[:ROWS]))
    vec = jnp.stack([vec, a2[ROWS:], a3[ROWS:], a1[ROWS:]])[:, :3]
    vec = lax.dynamic_slice_in_dim(jnp.concatenate([vec, vec]), (4 - y) % 4, 4, 0)
    sent = jnp.concatenate([pair, vec.reshape(12, JC), query_w[0, :4]], 0)
    pair_w = exchange(jnp.broadcast_to(sent, (DP,) + sent.shape), "dp")
    vec = pair_w[:, ROWS : ROWS + 12].astype(f32).reshape(DP, 4, 3, 2, HEAD)[..., :40]
    vec = vec[:, :, 0] + vec[:, :, 1] + vec[:, :, 2]
    vec = vec.reshape(-1)

    gain_first, gain_second = vec[None, :D], vec[None, D : 2 * D]
    key_start = JC * KEY_AT + HEAD * (jnp.minimum(mp, KEY_AT - 1) // 3)
    starts = ((JC * mp, JC), (key_start, HEAD), (key_start + JC, HEAD))
    bias = jnp.concatenate(
        [lax.dynamic_slice_in_dim(vec, 2 * D + start, size, 0) for start, size in starts]
    )[None]

    cosine, sine = tables()
    back, back_t, back_part, tok_part, tok_half = whole(
        prepare,
        [
            ((T, D), bf16), ((D, T), bf16),
            ((PART, D), bf16), ((PART, D), bf16), ((HALF, D), bf16),
        ],
        [ids, cotangent[0], tok],
    )
    normed, heads, att_sent, lse, joint_w = whole(
        attend,
        [
            ((T, D), bf16), ((T, 2 * JC), bf16), ((MP, HALF, JC), bf16),
            ((T, JC), f32), ((D, 2 * JC), bf16),
        ],
        [ids, tok, gain_first, bias, cosine, sine, query_w, pair_w],
        after=[back],
    )
    att_near = exchange(att_sent, "mp")
    att_far = swap_core(att_near)
    mixer_near = gather(shift_y, query_w[:, ROWS:])
    mixer_far = [swap_core(v) for v in mixer_near]
    mixer, rows_w = whole(
        assemble, [((D, D), bf16), ((JC, D), bf16)], [ids] + mixer_near + mixer_far
    )

    def fixed(shape):
        return pl.BlockSpec(shape, lambda i: (0,) * len(shape))

    hidden_part, normed_near = pl.pallas_call(
        mix,
        grid=(4,),
        out_shape=[jax.ShapeDtypeStruct((PART, D), f32), jax.ShapeDtypeStruct((HALF, D), bf16)],
        in_specs=[
            SM,
            fixed((MP, HALF, JC)),
            pl.BlockSpec((D, 384), lambda i: (0, i)),
            pl.BlockSpec((HALF, 384), lambda i: (0, i)),
            fixed((1, D)),
        ],
        out_specs=[fixed((PART, D)), fixed((HALF, D))],
        scratch_shapes=[pltpu.VMEM((HALF, D), f32), pltpu.VMEM((HALF, D), bf16)],
        compiler_params=pltpu.CompilerParams(vmem_limit_bytes=60 * MiB),
        cost_estimate=SMALL,
    )(ids, att_near, mixer, tok_half, gain_second)
    normed_far = swap_core(normed_near)

    def columns(n):
        return pl.BlockSpec((n, 256), lambda i: (0, i))

    block = pl.BlockSpec((DP, 3, ROWS, 256), lambda i: (0, 0, 0, i))
    act, gate_grad, up_grad, ff_grads = pl.pallas_call(
        gated,
        grid=(pl.cdiv(FP, 256),),
        out_shape=[jax.ShapeDtypeStruct((T, FP), bf16)] * 3
        + [jax.ShapeDtypeStruct((DP, 3, ROWS, FP), bf16)],
        in_specs=[fixed((HALF, D)), fixed((HALF, D)), fixed((T, D)), fixed((D, T)), block],
        out_specs=[columns(T)] * 3 + [block],
        scratch_shapes=[pltpu.VMEM((D, T), bf16)],
        compiler_params=pltpu.CompilerParams(vmem_limit_bytes=60 * MiB),
        cost_estimate=SMALL,
    )(normed_near, normed_far, back, back_t, ff)
    ff_shard = lax.psum_scatter(ff_grads, "dp", scatter_dimension=0, tiled=False)

    near, far = pl.pallas_call(
        spread,
        grid=(2,),
        out_shape=[jax.ShapeDtypeStruct((HALF, D), bf16)] * 2,
        in_specs=[fixed((T, FP))] * 2
        + [pl.BlockSpec((DP // 2, 2, ROWS, FP), lambda i: (i, 0, 0, 0))],
        out_specs=[pl.BlockSpec((HALF, 768), lambda i: (0, i))] * 2,
        compiler_params=pltpu.CompilerParams(vmem_limit_bytes=60 * MiB),
        cost_estimate=SMALL,
    )(gate_grad, up_grad, ff)

    def half_sum(near, far, after=()):
        own, *parts = whole(
            halve,
            [((PART, D), f32)] + [((PART, D), bf16)] * 3,
            [ids, near, swap_core(far)],
            after=after,
            limit=8,
        )
        return [own] + [shift_y(v, k) for v, k in zip(parts, (1, -1, 2))]

    normed_second_parts = half_sum(near, far)
    out_near, out_far = pl.pallas_call(
        spread_out,
        grid=(2,),
        out_shape=[jax.ShapeDtypeStruct((HALF, D), bf16)] * 2,
        in_specs=[
            fixed((T, FP)),
            pl.BlockSpec((DP // 2, 1, ROWS, FP), lambda i: (i, 2, 0, 0)),
        ],
        out_specs=[pl.BlockSpec((HALF, 768), lambda i: (0, i))] * 2,
        compiler_params=pltpu.CompilerParams(vmem_limit_bytes=60 * MiB),
        cost_estimate=SMALL,
    )(act, ff)
    hidden_grad, low, gain_second_part = whole(
        hidden_back,
        [((PART, D), f32), ((PART, D), bf16), ((1, D), f32)],
        [ids] + normed_second_parts + [hidden_part, back_part, gain_second],
        after=[out_far],
        limit=8,
    )
    out_parts = half_sum(out_near, out_far)
    low_near = jnp.stack(gather(shift_y, low))
    low_far = swap_core(low_near)
    heads_grad, hidden_low, own_kind, other_kind, input_near, input_far, chunks = whole(
        back_to_input,
        [
            ((T, 2 * JC), bf16), ((T, 2 * MC), bf16), ((T, HEAD), bf16), ((T, HEAD), bf16),
            ((HALF, D), bf16), ((HALF, D), bf16), ((MP, 2 * DP, HEAD), bf16),
        ],
        [ids, low_near, low_far, rows_w, heads, lse, cosine, sine, joint_w, tok, gain_second_part],
        scratch=[
            pltpu.VMEM((T, D), bf16),
            pltpu.VMEM((T, JC), bf16),
            pltpu.VMEM((T, HEAD), f32),
            pltpu.VMEM((T, HEAD), f32),
            pltpu.VMEM((1, D), f32),
            pltpu.VMEM((1, DP * MP * 40), f32),
            pltpu.VMEM((DP, MP * 40), f32),
            pltpu.VMEM((D, 2 * JC), bf16),
            pltpu.VMEM((T, D), bf16),
            pltpu.SemaphoreType.DMA((2,)),
        ],
        after=[out_parts[0]],
        loose=(8, 9),
    )
    both, left, right, out_sum = whole(
        group_parts,
        [((T, JC), bf16), ((T, HEAD), bf16), ((T, HEAD), bf16), ((PART, D), f32)],
        [ids, own_kind, swap_core(other_kind)] + out_parts,
        limit=8,
    )
    left, right, both = to_last_chip(left, 0), to_last_chip(right, 2), to_last_chip(both, 1)
    moved = exchange(chunks, "mp")
    (mixer_parts,) = whole(
        weigh_mixer,
        [((DP, 80, JC), bf16)],
        [ids, att_near, att_far, hidden_low],
        scratch=[pltpu.VMEM((DP, ROWS, MC), f32)],
        after=[out_sum],
    )
    (joint_parts,) = whole(
        weigh_joint,
        [((DP, ROWS + 88, JC), bf16)],
        [ids, normed, heads_grad, left, right, both, moved, mixer_parts],
    )
    joint_shard, mixer_shard, vector_shard, squares = whole(
        settle_grads,
        [((ROWS, JC), f32), ((ROWS, MC), f32), ((1, HEAD), f32), ((DP * MP, 1, HEAD), f32)],
        [ids, exchange(joint_parts, "dp"), ff_shard],
    )

    squares = exchange(squares, ("dp", "mp"))

    parts = half_sum(input_near, input_far, after=[joint_parts])
    (done,) = whole(
        finish,
        [((2, PART, D), bf16)],
        [ids, out_sum] + parts + [hidden_part, tok_part, hidden_grad, gain_first],
        limit=8,
    )
    done_parts = gather(shift_y, done)
    anywhere = pl.BlockSpec(memory_space=pl.ANY)
    results = [jax.ShapeDtypeStruct((1, T, D), f32)] * 2
    held = [pltpu.VMEM((2, HALF, D), f32), pltpu.SemaphoreType.DMA((2,))]
    *halves, token = pl.pallas_call(
        settle_near,
        out_shape=results + [jax.ShapeDtypeStruct((8, HEAD), f32)],
        in_specs=[SM] + [VM] * 4,
        out_specs=[anywhere] * 2 + [VM],
        scratch_shapes=held,
        compiler_params=pltpu.CompilerParams(vmem_limit_bytes=16 * MiB),
        cost_estimate=SMALL,
    )(ids, *done_parts)
    (done_near,) = whole(
        pile, [((4, 2, PART, D), bf16)], [ids] + done_parts, after=[squares, token], limit=8
    )
    output, input_grad = pl.pallas_call(
        settle_far,
        out_shape=results,
        in_specs=[SM, VM] + [anywhere] * 2,
        out_specs=[anywhere] * 2,
        input_output_aliases={2: 0, 3: 1},
        scratch_shapes=held,
        compiler_params=pltpu.CompilerParams(vmem_limit_bytes=16 * MiB),
        cost_estimate=SMALL,
    )(ids, swap_core(done_near), *halves)

    matrices = [joint_weight, joint_moment, joint_square]
    matrices += [mixer_weight, mixer_moment, mixer_square]
    matrices += [expand_weight, expand_moment, expand_square]
    matrices += [v.T for v in (shrink_weight, shrink_moment, shrink_square)]
    matrices += [v[None] for v in (vector_params, vector_moment, vector_square)]
    def third(shape):
        n = len(shape)
        if shape[-2] != ROWS:
            return pl.BlockSpec(shape, lambda i: (0,) * n)
        return pl.BlockSpec(
            shape[:-2] + (ROWS // 3, shape[-1]), lambda i: (0,) * (n - 2) + (i, 0)
        )

    given = [squares, joint_shard, mixer_shard, ff_shard, vector_shard] + matrices
    made = [(1, HEAD)] + [v.shape for v in matrices]
    norm, *new = pl.pallas_call(
        update,
        grid=(3,),
        out_shape=[jax.ShapeDtypeStruct(shape, f32) for shape in made],
        in_specs=[third(v.shape) for v in given],
        out_specs=[third(shape) for shape in made],
        compiler_params=pltpu.CompilerParams(vmem_limit_bytes=60 * MiB),
        cost_estimate=SMALL,
    )(*given)
    new[9:12] = [v.T for v in new[9:12]]
    new[12:] = [v[0] for v in new[12:]]
    return (output, input_grad, norm[0, 0], *new)


def solution(mesh):
    row = P("dp", None, None)
    matrix = [P("dp", "mp")] * 6 + [P(None, "dp", "mp")] * 3 + [P("mp", "dp")] * 3
    vector = [P(("dp", "mp"))] * 3
    return jax.shard_map(
        body,
        mesh=mesh,
        in_specs=tuple([row, P("dp"), row] + matrix + vector),
        out_specs=tuple([row, row, P()] + matrix + vector),
        check_vma=False,
    )
```

```python
import jax
import jax.numpy as jnp
import numpy as np
from jax import lax
from jax.experimental import pallas as pl
from jax.experimental.pallas import tpu as pltpu
from jax.sharding import PartitionSpec as P

QUERY_HEADS = 12
KEY_VALUE_HEADS = 2
HEAD = 128
STEP = 5
EPS_NORM = 1e-06
ROPE_BASE = 1000000.0
MAX_NORM = 1.0
BETA_ONE = 0.9
BETA_TWO = 0.95
ADAM_EPS = 1e-08
DECAY = 0.1
RATE_MATRIX = 0.06
RATE_VECTOR = 0.8
MASKED = -1e30

T = 512
HALF = 256
PART = 64
D = 1536
FF = 1120
FP = 1152
DP = 16
MP = 8
VEC = 5120
ROWS = D // DP
JC = 256
MC = 192
KEY_AT = 6
SCALE = HEAD ** (-0.5)

f32 = jnp.float32
bf16 = jnp.bfloat16
VM = pl.BlockSpec(memory_space=pltpu.VMEM)
SM = pl.BlockSpec(memory_space=pltpu.SMEM)
MiB = 1 << 20
SMALL = pl.CostEstimate(flops=1, bytes_accessed=1, transcendentals=0)


def shift_y(v, k):
    return lax.ppermute(v, "mp", [(i, (i + 2 * k) % MP) for i in range(MP)])


def from_last_chip(v, k):
    return lax.ppermute(v, "mp", [(i, (i + 2 * k) % MP) for i in (MP - 2, MP - 1)])


def to_last_chip(v, y):
    return lax.ppermute(v, "mp", [(2 * y + c, MP - 2 + c) for c in range(2)])


def swap_core(v):
    return lax.ppermute(v, "mp", [(i, i ^ 1) for i in range(MP)])


def exchange(v, axis):
    return lax.all_to_all(v, axis, split_axis=0, concat_axis=0, tiled=True)


RELATIVE = (0, -1, 1, 2)


def gather(shift, v):
    return [v, shift(v, 1), shift(v, -1), shift(v, 2)]


def nn(a, b):
    return lax.dot_general(a, b, (((1,), (0,)), ((), ())), preferred_element_type=f32)


def nt(a, b):
    return lax.dot_general(a, b, (((1,), (1,)), ((), ())), preferred_element_type=f32)


def tn(a, b):
    return lax.dot_general(a, b, (((0,), (0,)), ((), ())), preferred_element_type=f32)


def whole(body, outs, args, scratch=(), limit=60, after=(), loose=()):
    n = len(args)

    def bare(*refs):
        body(*refs[:n], *refs[n + len(after) :])

    return pl.pallas_call(
        bare,
        out_shape=[jax.ShapeDtypeStruct(s, d) for s, d in outs],
        in_specs=[SM]
        + [pl.BlockSpec(memory_space=pl.ANY) if k in loose else VM for k in range(1, n)]
        + [pl.BlockSpec(memory_space=pl.ANY)] * len(after),
        out_specs=[VM] * len(outs),
        scratch_shapes=list(scratch),
        compiler_params=pltpu.CompilerParams(vmem_limit_bytes=limit * MiB),
        cost_estimate=SMALL,
    )(*args, *after)


def at(start, size, step):
    return pl.ds(pl.multiple_of(start, step), size)


def prepare(ids, cotangent, tok, back, back_t, back_part, tok_part, tok_half):
    length, y, c = ids[0], ids[3], ids[4]
    for h in range(2):
        start = HALF * ((c + h) % 2)
        t = lax.broadcasted_iota(jnp.int32, (HALF, 1), 0) + start
        v = cotangent[at(start, HALF, HALF), :]
        v = jnp.where(t < length, v, jnp.zeros_like(v))
        back[HALF * h : HALF * (h + 1), :] = v
        back_t[:, HALF * h : HALF * (h + 1)] = v.T
    back_part[...] = back[at(PART * y, PART, PART), :]
    tok_part[...] = tok[at(HALF * c + PART * y, PART, PART), :]
    tok_half[...] = tok[at(HALF * c, HALF, HALF), :]


def kept(i, n, length):
    t = lax.broadcasted_iota(jnp.int32, (128, n), 0) + 128 * i
    s = lax.broadcasted_iota(jnp.int32, (128, n), 1)
    return (s <= t) & (s < length)


def attend(
    ids, tok, cosine, sine, query_w, pair_w,
    normed, heads, out, lse, w, vec,
):
    for d in range(DP):
        rows = pair_w[d, ROWS:, :].astype(f32)
        pieces = []
        for y in range(4):
            v = rows[3 * y : 3 * y + 1] + rows[3 * y + 1 : 3 * y + 2] + rows[3 * y + 2 : 3 * y + 3]
            pieces += [v[:, :40], v[:, HEAD : HEAD + 40]]
        vec[:, 320 * d : 320 * (d + 1)] = jnp.concatenate(pieces, 1)
    key_start = 2 * D + JC * KEY_AT + HEAD * lax.div(jnp.minimum(ids[2], KEY_AT - 1), 3)
    bias = jnp.concatenate(
        [
            vec[:, at(2 * D + JC * ids[2], JC, JC)],
            vec[:, at(key_start, HEAD, HEAD)],
            vec[:, at(key_start + JC, HEAD, HEAD)],
        ],
        1,
    )
    w[:, :JC] = query_w[:, :ROWS, :].reshape(D, JC)
    w[:, JC:] = pair_w[:, :ROWS, :].reshape(D, JC)

    gain = vec[:, :D]

    @pl.loop(0, T // 128)
    def _(i):
        rows = at(i * 128, 128, 128)
        x = tok[rows, :].astype(f32)
        s = lax.rsqrt(jnp.mean(x * x, -1, keepdims=True) + EPS_NORM)
        n = (x * s * gain).astype(bf16)
        normed[rows, :] = n
        j = nn(n, w[...]) + bias
        for h in range(4):
            cols = slice(HEAD * h, HEAD * (h + 1))
            u = j[:, cols]
            if h < 3:
                u = u * cosine[rows, :] + pltpu.roll(u, HEAD // 2, 1) * sine[rows, :]
            heads[rows, cols] = u.astype(bf16)

    for h in range(2):
        for i in range(4):
            n = 128 * (i + 1)
            q = heads[128 * i : n, HEAD * h : HEAD * (h + 1)]
            k, v = heads[:n, 2 * HEAD : 3 * HEAD], heads[:n, 3 * HEAD :]
            s = jnp.where(kept(i, n, ids[0]), nt(q, k) * SCALE, MASKED)
            m = jnp.max(s, -1, keepdims=True)
            e = jnp.exp(s - m)
            total = jnp.sum(e, -1, keepdims=True)
            o = nn((e / total).astype(bf16), v).astype(bf16)
            lse[128 * i : n, HEAD * h : HEAD * (h + 1)] = jnp.broadcast_to(
                m + jnp.log(total), (128, HEAD)
            )
            at_row = 128 * (i % 2)
            for y in range(4):
                out[2 * y + i // 2, at_row : at_row + 128, HEAD * h : HEAD * (h + 1)] = o


def assemble(ids, a0, a1, a2, a3, b0, b1, b2, b3, mixer, rows_w):
    y, c = ids[3], ids[4]
    for e, a, b in zip(RELATIVE, (a0, a1, a2, a3), (b0, b1, b2, b3)):
        first = 384 * lax.rem(y + e + 4, 4)
        left, right = at(first, JC, 128), at(first + JC, HEAD, 128)
        for d in range(DP):
            for half, v in ((c, a), (1 - c, b)):
                row = ROWS * d + 48 * half
                mixer[at(row, 48, 16), left] = v[d, :48, :]
                mixer[at(row, 32, 16), right] = v[d, 48:80, :HEAD]
                mixer[at(row + 32, 16, 16), right] = v[d, 48:64, HEAD:]
    rows_w[...] = mixer[at(JC * jnp.minimum(ids[2], KEY_AT - 1), JC, JC), :]


def mix(ids, att, mixer, tok, vec, hidden_part, normed, hidden, side):
    i = pl.program_id(0)

    @pl.when(i == 0)
    def _():
        for j in range(KEY_AT):
            side[:, JC * j : JC * (j + 1)] = att[j]

    cols = at(384 * i, 384, 384)
    hidden[:, cols] = nn(side[...], mixer[...]) + tok[...].astype(f32)

    @pl.when(i == 3)
    def _():
        hidden_part[...] = hidden[at(PART * ids[3], PART, PART), :]
        for r in range(0, HALF, 64):
            v = hidden[r : r + 64, :]
            s = lax.rsqrt(jnp.mean(v * v, -1, keepdims=True) + EPS_NORM)
            normed[r : r + 64, :] = (v * s * vec[:, D : 2 * D]).astype(bf16)


def gated(near, far, back, back_t, w, act, gate_grad, up_grad, grads, near_t):
    @pl.when(pl.program_id(0) == 0)
    def _():
        near_t[:, :HALF] = near[...].T
        near_t[:, HALF:] = far[...].T

    gate_w, up_w, down_w = [w[:, m].reshape(D, 256) for m in range(3)]
    for r, normed in ((0, near), (HALF, far)):
        rows = slice(r, r + HALF)
        g = nn(normed[...], gate_w)
        u = nn(normed[...], up_w)
        a = nn(back[rows, :], down_w)
        sigma = 1.0 / (1.0 + jnp.exp(-g))
        swished = g * sigma
        act[rows, :] = (swished * u).astype(bf16)
        gate_grad[rows, :] = (a * u * sigma * (1.0 + g * (1.0 - sigma))).astype(bf16)
        up_grad[rows, :] = (a * swished).astype(bf16)
    for m, (left, right) in enumerate(((near_t, gate_grad), (near_t, up_grad), (back_t, act))):
        for r in range(4):
            part = nn(left[384 * r : 384 * (r + 1), :], right[...]).astype(bf16)
            grads[4 * r : 4 * (r + 1), m] = part.reshape(4, ROWS, 256)


def spread(gate_grad, up_grad, w, near, far):
    gate_w, up_w = [w[:, m].reshape(768, FP) for m in range(2)]
    for b in range(3):
        cols = slice(256 * b, 256 * (b + 1))
        part = nt(gate_grad[...], gate_w[cols]) + nt(up_grad[...], up_w[cols])
        near[:, cols] = part[:HALF].astype(bf16)
        far[:, cols] = part[HALF:].astype(bf16)


def spread_out(act, w, near, far):
    down_w = w[:, 0].reshape(768, FP)
    for b in range(3):
        cols = slice(256 * b, 256 * (b + 1))
        part = nt(act[...], down_w[cols])
        near[:, cols] = part[:HALF].astype(bf16)
        far[:, cols] = part[HALF:].astype(bf16)


def halve(ids, near, other, own, p1, p2, p3):
    y = ids[3]
    for k, out in ((0, own), (1, p1), (3, p2), (2, p3)):
        rows = at(PART * lax.rem(y + k, 4), PART, PART)
        out[...] = (near[rows, :].astype(f32) + other[rows, :].astype(f32)).astype(out.dtype)


def summed(own, parts):
    total = own[...]
    for part in parts:
        total += part[...].astype(f32)
    return total


def hidden_back(ids, own, a1, a2, a3, hidden, back, gain, grad, low, gain_part):
    h = hidden[...]
    g = summed(own, (a1, a2, a3))
    scale = lax.rsqrt(jnp.mean(h * h, -1, keepdims=True) + EPS_NORM)
    gain_part[...] = jnp.sum(g * h * scale, 0, keepdims=True)
    v = back[...].astype(f32) + norm_back(h, scale, gain[...], g)
    grad[...] = v
    low[...] = v.astype(bf16)


def finish(ids, out_sum, own, a1, a2, a3, hidden, tok, grad, gain, done):
    length, y, c = ids[0], ids[3], ids[4]
    o, g = out_sum[...], summed(own, (a1, a2, a3))
    t = lax.broadcasted_iota(jnp.int32, (PART, 1), 0) + HALF * c + PART * y
    done[0] = jnp.where(t < length, o + hidden[...], 0.0).astype(bf16)
    x = tok[...].astype(f32)
    scale = lax.rsqrt(jnp.mean(x * x, -1, keepdims=True) + EPS_NORM)
    done[1] = (grad[...] + norm_back(x, scale, gain[...], g)).astype(bf16)


def attend_back(
    ids, near, far, rows_w, heads, lse, cosine, sine,
    grads, window, own_kind, other_kind, low, att_grad, key_grad, value_grad,
):
    length, y, c = ids[0], ids[3], ids[4]
    for k, e in enumerate(RELATIVE):
        place = PART * lax.rem(y + e + 4, 4)
        low[at(HALF * c + place, PART, PART), :] = near[k]
        low[at(HALF * (1 - c) + place, PART, PART), :] = far[k]
    window[...] = low[:, at(384 * y, 384, 384)]
    has_heads = (ids[2] < KEY_AT).astype(f32)
    att_grad[...] = (nt(low[...], rows_w[...]) * has_heads).astype(bf16)
    key_grad[...] = jnp.zeros_like(key_grad)
    value_grad[...] = jnp.zeros_like(value_grad)
    for h in range(2):
        cols = slice(HEAD * h, HEAD * (h + 1))
        for i in range(4):
            n = 128 * (i + 1)
            rows = slice(128 * i, n)
            q = heads[rows, cols]
            k, v = heads[:n, 2 * HEAD : 3 * HEAD], heads[:n, 3 * HEAD :]
            o = att_grad[rows, cols]
            s = nt(q, k) * SCALE
            p = jnp.where(kept(i, n, length), jnp.exp(s - lse[rows, HEAD * h : HEAD * h + 1]), 0.0)
            d = nt(o, v)
            g = (p * (d - jnp.sum(p * d, -1, keepdims=True))).astype(bf16)
            value_grad[:n, :] += tn(p.astype(bf16), o)
            key_grad[:n, :] += tn(g, q)
            dq = nn(g, k) * SCALE
            dq = dq * cosine[rows, :] - pltpu.roll(dq, HEAD // 2, 1) * sine[rows, :]
            grads[rows, cols] = dq.astype(bf16)
    dk = key_grad[...] * SCALE
    dk = dk * cosine[...] - pltpu.roll(dk, HEAD // 2, 1) * sine[...]
    grads[:, 2 * HEAD : 3 * HEAD] = dk.astype(bf16)
    grads[:, 3 * HEAD :] = value_grad[...].astype(bf16)
    k, v = grads[:, 2 * HEAD : 3 * HEAD], grads[:, 3 * HEAD :]

    @pl.when(c == 0)
    def _():
        own_kind[...] = k
        other_kind[...] = v

    @pl.when(c != 0)
    def _():
        own_kind[...] = v
        other_kind[...] = k


def joint_back(
    ids, grads, w, tok, second_part,
    near, far, chunks, gain_part, vec, blocks,
):
    g = grads[...]
    gain_part[...] = jnp.zeros_like(gain_part)
    for r in range(0, T, 128):
        rows = slice(r, r + 128)
        back = nt(g[rows], w[...])
        half, place = r // HALF, slice(r % HALF, r % HALF + 128)
        moves = back.astype(bf16)

        @pl.when(ids[4] == half)
        def _():
            near[place, :] = moves

        @pl.when(ids[4] != half)
        def _():
            far[place, :] = moves

        x = tok[rows, :].astype(f32)
        s = lax.rsqrt(jnp.mean(x * x, -1, keepdims=True) + EPS_NORM)
        gain_part[...] += jnp.sum(back * x * s, 0, keepdims=True)
    vec[...] = jnp.zeros_like(vec)
    vec[:, :D] = gain_part[...]
    vec[:, D : 2 * D] = second_part[...]
    bias = jnp.sum(g.astype(f32), 0, keepdims=True)
    head_at = jnp.minimum(ids[2], KEY_AT - 1)
    key_start = 2 * D + JC * KEY_AT + HEAD * lax.div(head_at, 3)
    vec[:, at(2 * D + JC * head_at, JC, JC)] = bias[:, :JC]
    vec[:, at(key_start, HEAD, HEAD)] = bias[:, JC : JC + HEAD]
    vec[:, at(key_start + JC, HEAD, HEAD)] = bias[:, JC + HEAD :]
    for d in range(DP):
        blocks[d : d + 1, :] = vec[:, 320 * d : 320 * (d + 1)]
    for m in range(MP):
        piece = blocks[:, 40 * m : 40 * (m + 1)]
        piece = jnp.concatenate([piece, jnp.zeros((DP, HEAD - 40), f32)], 1)
        high = piece.astype(bf16)
        chunks[m, :DP, :] = high
        chunks[m, DP:, :] = (piece - high.astype(f32)).astype(bf16)


def back_to_input(
    ids, near_low, far_low, rows_w, heads, lse, cosine, sine, w, tok, second_part,
    grads, window, own_kind, other_kind, near, far, chunks,
    low, att_grad, key_grad, value_grad, gain_part, vec, blocks, w_held, tok_held, sems,
):
    copies = [
        pltpu.make_async_copy(w, w_held, sems.at[0]),
        pltpu.make_async_copy(tok, tok_held, sems.at[1]),
    ]
    for copy in copies:
        copy.start()
    attend_back(
        ids, near_low, far_low, rows_w, heads, lse, cosine, sine,
        grads, window, own_kind, other_kind, low, att_grad, key_grad, value_grad,
    )
    for copy in copies:
        copy.wait()
    joint_back(ids, grads, w_held, tok_held, second_part, near, far, chunks, gain_part, vec, blocks)


def group_parts(ids, own, other, o0, o1, o2, o3, both, left, right, out_sum):
    out_sum[...] = summed(o0, (o1, o2, o3))
    own_group = lax.div(jnp.minimum(ids[2], KEY_AT - 1), 3)
    partner = ids[2] + 1 - 2 * ids[4]
    other_group = lax.div(jnp.minimum(partner, KEY_AT - 1), 3)
    a, b = own[...].astype(f32), other[...].astype(f32)
    for g, out in ((0, left), (1, right)):
        part = a * (own_group == g).astype(f32) + b * (other_group == g).astype(f32)
        out[...] = part.astype(bf16)
        both[:, HEAD * g : HEAD * (g + 1)] = part.astype(bf16)


def weigh_joint(ids, normed, grads, left, right, both, moved, mixer_parts, parts):
    pair = jnp.concatenate([left[...].astype(f32), right[...].astype(f32)], 1)
    pair = pair + both[...].astype(f32)
    own = grads[:, :JC].astype(f32)
    g = jnp.where(ids[2] < KEY_AT, own, pair).astype(bf16)
    for r in range(4):
        cols = slice(384 * r, 384 * (r + 1))
        part = tn(normed[:, cols], g).astype(bf16)
        parts[4 * r : 4 * (r + 1), :ROWS, :] = part.reshape(4, ROWS, JC)
    parts[:, ROWS : ROWS + 80, :] = mixer_parts[...]
    vec = moved[0].astype(f32)
    for j in range(1, MP):
        vec += moved[j].astype(f32)
    vec = vec[:DP] + vec[DP:]
    high = vec.astype(bf16).astype(f32)
    for d in range(DP):
        parts[d, ROWS + 80 :, :HEAD] = jnp.broadcast_to(high[d : d + 1], (8, HEAD)).astype(bf16)
        low = (vec - high)[d : d + 1]
        parts[d, ROWS + 80 :, HEAD:] = jnp.broadcast_to(low, (8, HEAD)).astype(bf16)


def weigh_mixer(ids, near, far, low, packed, parts):
    c = ids[4]

    def own_columns(half):
        v = low[at(HALF * half, HALF, HALF), :].astype(f32)
        return jnp.where(c == 0, v[:, :MC], v[:, MC:]).astype(bf16)

    mine, other = own_columns(c), own_columns(1 - c)
    for j in range(KEY_AT):
        part = tn(near[j], mine) + tn(far[j], other)
        start = JC * j
        while start < JC * (j + 1):
            stop = min((start // ROWS + 1) * ROWS, JC * (j + 1))
            first = start % ROWS
            parts[start // ROWS, first : first + stop - start, :] = part[
                start - JC * j : stop - JC * j
            ]
            start = stop
    for d in range(DP):
        left, right = parts[d, :, :HEAD], parts[d, :, HEAD:]
        packed[d, :48, :HEAD] = left[:48].astype(bf16)
        packed[d, :48, HEAD:] = left[48:].astype(bf16)
        packed[d, 48:, :HEAD] = jnp.concatenate([right[:32], right[32:64]], 1).astype(bf16)
        packed[d, 48:, HEAD:] = jnp.concatenate(
            [right[64:], jnp.zeros((32, JC - MC), f32)], 1
        ).astype(bf16)


def settle_grads(ids, moved, ff, joint, mixer, vector, squares):
    total = moved[0].astype(f32)
    for d in range(1, DP):
        total += moved[d].astype(f32)
    joint[...] = total[:ROWS]
    left, right = total[ROWS : ROWS + 48], total[ROWS + 48 : ROWS + 80]
    mixer[:48, :HEAD] = left[:, :HEAD]
    mixer[48:, :HEAD] = left[:, HEAD:]
    mixer[:32, HEAD:] = right[:, : MC - HEAD]
    mixer[32:64, HEAD:] = right[:, MC - HEAD : HEAD]
    mixer[64:, HEAD:] = right[:, HEAD:MC]
    vec = total[ROWS + 80 : ROWS + 81, :HEAD] + total[ROWS + 80 : ROWS + 81, HEAD:]
    vector[...] = vec
    total = total[: ROWS + 80]
    total = jnp.sum(total * total) + jnp.sum(vec * vec)
    for m in range(3):
        v = ff[m].astype(f32)
        total += jnp.sum(v * v)
    squares[...] = jnp.full(squares.shape, total, f32)


def update(
    squares, joint_grad, mixer_grad, ff_grad, vector_grad,
    joint_w, joint_m, joint_v, mixer_w, mixer_m, mixer_v, expand_w, expand_m, expand_v,
    shrink_w, shrink_m, shrink_v, vector_w, vector_m, vector_v,
    norm_out, joint_wn, joint_mn, joint_vn, mixer_wn, mixer_mn, mixer_vn,
    expand_wn, expand_mn, expand_vn, shrink_wn, shrink_mn, shrink_vn,
    vector_wn, vector_mn, vector_vn,
):
    norm = jnp.sqrt(jnp.sum(squares[:, 0, :], 0, keepdims=True))
    norm_out[...] = norm
    clip = jnp.minimum(1.0, MAX_NORM / (norm[:, :1] + 1e-06))

    def step(grad, before, after, rate, decay, part=Ellipsis):
        w, m, v = [ref[part] for ref in before]
        results = adam_step(w, clip * grad, m, v, rate, decay)
        for ref, new in zip(after, results):
            ref[part] = new

    step(
        joint_grad[...], (joint_w, joint_m, joint_v), (joint_wn, joint_mn, joint_vn),
        RATE_MATRIX, DECAY,
    )
    step(
        mixer_grad[...], (mixer_w, mixer_m, mixer_v), (mixer_wn, mixer_mn, mixer_vn),
        RATE_MATRIX, DECAY,
    )
    for m in range(2):
        step(
            ff_grad[m, :, :FF].astype(f32),
            (expand_w, expand_m, expand_v), (expand_wn, expand_mn, expand_vn),
            RATE_MATRIX, DECAY, m,
        )
    step(
        ff_grad[2, :, :FF].astype(f32),
        (shrink_w, shrink_m, shrink_v), (shrink_wn, shrink_mn, shrink_vn),
        RATE_MATRIX, DECAY,
    )
    step(
        vector_grad[:, :40], (vector_w, vector_m, vector_v), (vector_wn, vector_mn, vector_vn),
        RATE_VECTOR, 0.0,
    )


def write_half(ids, half, pieces, outs, rows, sems):
    for k, e in enumerate(RELATIVE):
        place = at(PART * lax.rem(ids[3] + e + 4, 4), PART, PART)
        for n in range(2):
            rows[n, place, :] = pieces[k][n].astype(f32)
    copies = [
        pltpu.make_async_copy(rows.at[n], out.at[0, at(HALF * half, HALF, HALF)], sems.at[n])
        for n, out in enumerate(outs)
    ]
    for copy in copies:
        copy.start()
    for copy in copies:
        copy.wait()


def settle_near(ids, p0, p1, p2, p3, output, input_grad, token, rows, sems):
    token[...] = jnp.zeros_like(token)
    write_half(ids, ids[4], (p0, p1, p2, p3), (output, input_grad), rows, sems)


def settle_far(ids, far, _a, _b, output, input_grad, rows, sems):
    pieces = [far.at[k] for k in range(4)]
    write_half(ids, 1 - ids[4], pieces, (output, input_grad), rows, sems)


def pile(ids, p0, p1, p2, p3, out):
    for k, p in enumerate((p0, p1, p2, p3)):
        out[k] = p[...]


def norm_back(v, scale, gain, grad):
    scaled = gain * grad
    return scale * scaled - v * scale * scale * scale * jnp.mean(scaled * v, -1, keepdims=True)


def adam_step(weight, grad, moment, square, rate, decay):
    moment_next = BETA_ONE * moment + (1.0 - BETA_ONE) * grad
    square_next = BETA_TWO * square + (1.0 - BETA_TWO) * grad * grad
    first_hat = moment_next * (1.0 / (1.0 - BETA_ONE**STEP))
    second_hat = square_next * (1.0 / (1.0 - BETA_TWO**STEP))
    weight_next = weight - rate * (first_hat / (jnp.sqrt(second_hat) + ADAM_EPS) + decay * weight)
    return (weight_next, moment_next, square_next)


def tables():
    freq = np.float32(ROPE_BASE) ** (-np.arange(0, HEAD, 2, dtype=np.float32) / np.float32(HEAD))
    angle = np.arange(T, dtype=np.float32)[:, None] * freq.astype(np.float32)[None, :]
    cosine, sine = np.cos(angle), np.sin(angle)
    return (
        np.concatenate([cosine, cosine], -1).astype(np.float32),
        np.concatenate([-sine, sine], -1).astype(np.float32),
    )


def split_low(v):
    high = lax.reduce_precision(v, 8, 7)
    middle = lax.reduce_precision(v - high, 8, 7)
    return [part.astype(bf16) for part in (high, middle, v - high - middle)]


def body(
    tokens, lengths, cotangent,
    joint_weight, joint_moment, joint_square,
    mixer_weight, mixer_moment, mixer_square,
    expand_weight, expand_moment, expand_square,
    shrink_weight, shrink_moment, shrink_square,
    vector_params, vector_moment, vector_square,
):
    dp, mp = lax.axis_index("dp"), lax.axis_index("mp")
    y, c = mp // 2, mp % 2
    tok, length = tokens[0], lengths[0]
    ids = jnp.stack([length, dp, mp, y, c]).astype(jnp.int32)

    stack = jnp.concatenate(
        [expand_weight.astype(bf16), shrink_weight.T.astype(bf16)[None]], 0
    )
    stack = jnp.pad(stack, ((0, 0), (0, 0), (0, FP - FF)))
    ff = lax.all_gather(stack, "dp", axis=0, tiled=False)

    low = jnp.concatenate([joint_weight.astype(bf16), mixer_weight.astype(bf16)], 1)
    vec = jnp.pad(jnp.stack(split_low(vector_params)), ((0, 13), (0, JC + MC - 40)))
    low = jnp.concatenate([low, vec], 0)
    other = swap_core(low)
    first, second = jnp.where(c == 0, low, other), jnp.where(c == 0, other, low)
    pairs = [
        jnp.concatenate([first[:ROWS, cols], second[:ROWS, cols]], 1)
        for cols in (slice(0, HEAD), slice(HEAD, JC))
    ]
    chip = jnp.concatenate([first[:ROWS, JC:], second[:ROWS, JC:]], 1)
    chip = lax.dynamic_slice_in_dim(chip, 48 * c, 48, 0)
    rest = jnp.concatenate([chip[:32, JC:], jnp.pad(chip[32:, JC:], ((0, 16), (0, 0)))], 1)
    sent = jnp.concatenate([low[:ROWS, :JC], chip[:, :JC], rest], 0)
    query_w = exchange(jnp.broadcast_to(sent, (DP,) + sent.shape), "dp")
    vec = jnp.concatenate([first[ROWS:, :HEAD], second[ROWS:, :HEAD]], 1)
    sends = [pairs[0], pairs[1], jnp.where(c == 0, pairs[0], pairs[1])]
    sends = [jnp.concatenate([v, vec], 0) for v in sends]
    a1, a2, a3 = [shift_y(v, k) for v, k in zip(sends, (1, -1, 2))]
    pair = jnp.where(y == 0, a1[:ROWS], jnp.where(y == 2, a2[:ROWS], a3[:ROWS]))
    vec = jnp.stack([vec, a2[ROWS:], a3[ROWS:], a1[ROWS:]])[:, :3]
    vec = lax.dynamic_slice_in_dim(jnp.concatenate([vec, vec]), (4 - y) % 4, 4, 0)
    sent = jnp.concatenate([pair, vec.reshape(12, JC), query_w[0, :4]], 0)
    pair_w = exchange(jnp.broadcast_to(sent, (DP,) + sent.shape), "dp")
    cosine, sine = tables()
    back, back_t, back_part, tok_part, tok_half = whole(
        prepare,
        [
            ((T, D), bf16), ((D, T), bf16),
            ((PART, D), bf16), ((PART, D), bf16), ((HALF, D), bf16),
        ],
        [ids, cotangent[0], tok],
    )
    normed, heads, att_sent, lse, joint_w, vec = whole(
        attend,
        [
            ((T, D), bf16), ((T, 2 * JC), bf16), ((MP, HALF, JC), bf16),
            ((T, JC), f32), ((D, 2 * JC), bf16), ((1, VEC), f32),
        ],
        [ids, tok, cosine, sine, query_w, pair_w],
        after=[back],
    )
    gain_first, gain_second = vec[:, :D], vec[:, D : 2 * D]
    att_near = exchange(att_sent, "mp")
    att_far = swap_core(att_near)
    mixer_near = gather(shift_y, query_w[:, ROWS:])
    mixer_far = [swap_core(v) for v in mixer_near]
    mixer, rows_w = whole(
        assemble, [((D, D), bf16), ((JC, D), bf16)], [ids] + mixer_near + mixer_far
    )

    def fixed(shape):
        return pl.BlockSpec(shape, lambda i: (0,) * len(shape))

    hidden_part, normed_near = pl.pallas_call(
        mix,
        grid=(4,),
        out_shape=[jax.ShapeDtypeStruct((PART, D), f32), jax.ShapeDtypeStruct((HALF, D), bf16)],
        in_specs=[
            SM,
            fixed((MP, HALF, JC)),
            pl.BlockSpec((D, 384), lambda i: (0, i)),
            pl.BlockSpec((HALF, 384), lambda i: (0, i)),
            fixed((1, VEC)),
        ],
        out_specs=[fixed((PART, D)), fixed((HALF, D))],
        scratch_shapes=[pltpu.VMEM((HALF, D), f32), pltpu.VMEM((HALF, D), bf16)],
        compiler_params=pltpu.CompilerParams(vmem_limit_bytes=60 * MiB),
        cost_estimate=SMALL,
    )(ids, att_near, mixer, tok_half, vec)
    normed_far = swap_core(normed_near)

    def columns(n):
        return pl.BlockSpec((n, 256), lambda i: (0, i))

    block = pl.BlockSpec((DP, 3, ROWS, 256), lambda i: (0, 0, 0, i))
    act, gate_grad, up_grad, ff_grads = pl.pallas_call(
        gated,
        grid=(pl.cdiv(FP, 256),),
        out_shape=[jax.ShapeDtypeStruct((T, FP), bf16)] * 3
        + [jax.ShapeDtypeStruct((DP, 3, ROWS, FP), bf16)],
        in_specs=[fixed((HALF, D)), fixed((HALF, D)), fixed((T, D)), fixed((D, T)), block],
        out_specs=[columns(T)] * 3 + [block],
        scratch_shapes=[pltpu.VMEM((D, T), bf16)],
        compiler_params=pltpu.CompilerParams(vmem_limit_bytes=60 * MiB),
        cost_estimate=SMALL,
    )(normed_near, normed_far, back, back_t, ff)
    ff_shard = lax.psum_scatter(ff_grads, "dp", scatter_dimension=0, tiled=False)

    near, far = pl.pallas_call(
        spread,
        grid=(2,),
        out_shape=[jax.ShapeDtypeStruct((HALF, D), bf16)] * 2,
        in_specs=[fixed((T, FP))] * 2
        + [pl.BlockSpec((DP // 2, 2, ROWS, FP), lambda i: (i, 0, 0, 0))],
        out_specs=[pl.BlockSpec((HALF, 768), lambda i: (0, i))] * 2,
        compiler_params=pltpu.CompilerParams(vmem_limit_bytes=60 * MiB),
        cost_estimate=SMALL,
    )(gate_grad, up_grad, ff)

    def half_sum(near, far, after=()):
        own, *parts = whole(
            halve,
            [((PART, D), f32)] + [((PART, D), bf16)] * 3,
            [ids, near, swap_core(far)],
            after=after,
            limit=8,
        )
        return [own] + [shift_y(v, k) for v, k in zip(parts, (1, -1, 2))]

    normed_second_parts = half_sum(near, far)
    out_near, out_far = pl.pallas_call(
        spread_out,
        grid=(2,),
        out_shape=[jax.ShapeDtypeStruct((HALF, D), bf16)] * 2,
        in_specs=[
            fixed((T, FP)),
            pl.BlockSpec((DP // 2, 1, ROWS, FP), lambda i: (i, 2, 0, 0)),
        ],
        out_specs=[pl.BlockSpec((HALF, 768), lambda i: (0, i))] * 2,
        compiler_params=pltpu.CompilerParams(vmem_limit_bytes=60 * MiB),
        cost_estimate=SMALL,
    )(act, ff)
    hidden_grad, low, gain_second_part = whole(
        hidden_back,
        [((PART, D), f32), ((PART, D), bf16), ((1, D), f32)],
        [ids] + normed_second_parts + [hidden_part, back_part, gain_second],
        after=[out_far],
        limit=8,
    )
    out_parts = half_sum(out_near, out_far)
    low_near = jnp.stack(gather(shift_y, low))
    low_far = swap_core(low_near)
    heads_grad, hidden_low, own_kind, other_kind, input_near, input_far, chunks = whole(
        back_to_input,
        [
            ((T, 2 * JC), bf16), ((T, 2 * MC), bf16), ((T, HEAD), bf16), ((T, HEAD), bf16),
            ((HALF, D), bf16), ((HALF, D), bf16), ((MP, 2 * DP, HEAD), bf16),
        ],
        [ids, low_near, low_far, rows_w, heads, lse, cosine, sine, joint_w, tok, gain_second_part],
        scratch=[
            pltpu.VMEM((T, D), bf16),
            pltpu.VMEM((T, JC), bf16),
            pltpu.VMEM((T, HEAD), f32),
            pltpu.VMEM((T, HEAD), f32),
            pltpu.VMEM((1, D), f32),
            pltpu.VMEM((1, DP * MP * 40), f32),
            pltpu.VMEM((DP, MP * 40), f32),
            pltpu.VMEM((D, 2 * JC), bf16),
            pltpu.VMEM((T, D), bf16),
            pltpu.SemaphoreType.DMA((2,)),
        ],
        after=[out_parts[0]],
        loose=(8, 9),
    )
    both, left, right, out_sum = whole(
        group_parts,
        [((T, JC), bf16), ((T, HEAD), bf16), ((T, HEAD), bf16), ((PART, D), f32)],
        [ids, own_kind, swap_core(other_kind)] + out_parts,
        limit=8,
    )
    left, right, both = to_last_chip(left, 0), to_last_chip(right, 2), to_last_chip(both, 1)
    moved = exchange(chunks, "mp")
    (mixer_parts,) = whole(
        weigh_mixer,
        [((DP, 80, JC), bf16)],
        [ids, att_near, att_far, hidden_low],
        scratch=[pltpu.VMEM((DP, ROWS, MC), f32)],
        after=[out_sum],
    )
    (joint_parts,) = whole(
        weigh_joint,
        [((DP, ROWS + 88, JC), bf16)],
        [ids, normed, heads_grad, left, right, both, moved, mixer_parts],
    )
    joint_shard, mixer_shard, vector_shard, squares = whole(
        settle_grads,
        [((ROWS, JC), f32), ((ROWS, MC), f32), ((1, HEAD), f32), ((DP * MP, 1, HEAD), f32)],
        [ids, exchange(joint_parts, "dp"), ff_shard],
    )

    squares = exchange(squares, ("dp", "mp"))

    parts = half_sum(input_near, input_far, after=[joint_parts])
    (done,) = whole(
        finish,
        [((2, PART, D), bf16)],
        [ids, out_sum] + parts + [hidden_part, tok_part, hidden_grad, gain_first],
        limit=8,
    )
    done_parts = gather(shift_y, done)
    anywhere = pl.BlockSpec(memory_space=pl.ANY)
    results = [jax.ShapeDtypeStruct((1, T, D), f32)] * 2
    held = [pltpu.VMEM((2, HALF, D), f32), pltpu.SemaphoreType.DMA((2,))]
    *halves, token = pl.pallas_call(
        settle_near,
        out_shape=results + [jax.ShapeDtypeStruct((8, HEAD), f32)],
        in_specs=[SM] + [VM] * 4,
        out_specs=[anywhere] * 2 + [VM],
        scratch_shapes=held,
        compiler_params=pltpu.CompilerParams(vmem_limit_bytes=16 * MiB),
        cost_estimate=SMALL,
    )(ids, *done_parts)
    (done_near,) = whole(
        pile, [((4, 2, PART, D), bf16)], [ids] + done_parts, after=[squares, token], limit=8
    )
    output, input_grad = pl.pallas_call(
        settle_far,
        out_shape=results,
        in_specs=[SM, VM] + [anywhere] * 2,
        out_specs=[anywhere] * 2,
        input_output_aliases={2: 0, 3: 1},
        scratch_shapes=held,
        compiler_params=pltpu.CompilerParams(vmem_limit_bytes=16 * MiB),
        cost_estimate=SMALL,
    )(ids, swap_core(done_near), *halves)

    matrices = [joint_weight, joint_moment, joint_square]
    matrices += [mixer_weight, mixer_moment, mixer_square]
    matrices += [expand_weight, expand_moment, expand_square]
    matrices += [v.T for v in (shrink_weight, shrink_moment, shrink_square)]
    matrices += [v[None] for v in (vector_params, vector_moment, vector_square)]
    def third(shape):
        n = len(shape)
        if shape[-2] != ROWS:
            return pl.BlockSpec(shape, lambda i: (0,) * n)
        return pl.BlockSpec(
            shape[:-2] + (ROWS // 3, shape[-1]), lambda i: (0,) * (n - 2) + (i, 0)
        )

    given = [squares, joint_shard, mixer_shard, ff_shard, vector_shard] + matrices
    made = [(1, HEAD)] + [v.shape for v in matrices]
    norm, *new = pl.pallas_call(
        update,
        grid=(3,),
        out_shape=[jax.ShapeDtypeStruct(shape, f32) for shape in made],
        in_specs=[third(v.shape) for v in given],
        out_specs=[third(shape) for shape in made],
        compiler_params=pltpu.CompilerParams(vmem_limit_bytes=60 * MiB),
        cost_estimate=SMALL,
    )(*given)
    new[9:12] = [v.T for v in new[9:12]]
    new[12:] = [v[0] for v in new[12:]]
    return (output, input_grad, norm[0, 0], *new)


def solution(mesh):
    row = P("dp", None, None)
    matrix = [P("dp", "mp")] * 6 + [P(None, "dp", "mp")] * 3 + [P("mp", "dp")] * 3
    vector = [P(("dp", "mp"))] * 3
    return jax.shard_map(
        body,
        mesh=mesh,
        in_specs=tuple([row, P("dp"), row] + matrix + vector),
        out_specs=tuple([row, row, P()] + matrix + vector),
        check_vma=False,
    )
```

```python
import jax
import jax.numpy as jnp
import numpy as np
from jax import lax
from jax.experimental import pallas as pl
from jax.experimental.pallas import tpu as pltpu
from jax.sharding import PartitionSpec as P

QUERY_HEADS = 12
KEY_VALUE_HEADS = 2
HEAD = 128
STEP = 5
EPS_NORM = 1e-06
ROPE_BASE = 1000000.0
MAX_NORM = 1.0
BETA_ONE = 0.9
BETA_TWO = 0.95
ADAM_EPS = 1e-08
DECAY = 0.1
RATE_MATRIX = 0.06
RATE_VECTOR = 0.8
MASKED = -1e30

T = 512
HALF = 256
PART = 64
D = 1536
FF = 1120
FP = 1152
DP = 16
MP = 8
VEC = 5120
ROWS = D // DP
JC = 256
MC = 192
KEY_AT = 6
SCALE = HEAD ** (-0.5)

f32 = jnp.float32
bf16 = jnp.bfloat16
VM = pl.BlockSpec(memory_space=pltpu.VMEM)
SM = pl.BlockSpec(memory_space=pltpu.SMEM)
MiB = 1 << 20
SMALL = pl.CostEstimate(flops=1, bytes_accessed=1, transcendentals=0)


def shift_y(v, k):
    return lax.ppermute(v, "mp", [(i, (i + 2 * k) % MP) for i in range(MP)])


def from_last_chip(v, k):
    return lax.ppermute(v, "mp", [(i, (i + 2 * k) % MP) for i in (MP - 2, MP - 1)])


def to_last_chip(v, y):
    return lax.ppermute(v, "mp", [(2 * y + c, MP - 2 + c) for c in range(2)])


def swap_core(v):
    return lax.ppermute(v, "mp", [(i, i ^ 1) for i in range(MP)])


def exchange(v, axis):
    return lax.all_to_all(v, axis, split_axis=0, concat_axis=0, tiled=True)


RELATIVE = (0, -1, 1, 2)


def gather(shift, v):
    return [v, shift(v, 1), shift(v, -1), shift(v, 2)]


def nn(a, b):
    return lax.dot_general(a, b, (((1,), (0,)), ((), ())), preferred_element_type=f32)


def nt(a, b):
    return lax.dot_general(a, b, (((1,), (1,)), ((), ())), preferred_element_type=f32)


def tn(a, b):
    return lax.dot_general(a, b, (((0,), (0,)), ((), ())), preferred_element_type=f32)


def whole(body, outs, args, scratch=(), limit=60, after=(), loose=()):
    n = len(args)

    def bare(*refs):
        body(*refs[:n], *refs[n + len(after) :])

    return pl.pallas_call(
        bare,
        out_shape=[jax.ShapeDtypeStruct(s, d) for s, d in outs],
        in_specs=[SM]
        + [pl.BlockSpec(memory_space=pl.ANY) if k in loose else VM for k in range(1, n)]
        + [pl.BlockSpec(memory_space=pl.ANY)] * len(after),
        out_specs=[VM] * len(outs),
        scratch_shapes=list(scratch),
        compiler_params=pltpu.CompilerParams(vmem_limit_bytes=limit * MiB),
        cost_estimate=SMALL,
    )(*args, *after)


def at(start, size, step):
    return pl.ds(pl.multiple_of(start, step), size)


def prepare(ids, cotangent, tok, back, back_t, back_part, tok_part, tok_half):
    length, y, c = ids[0], ids[3], ids[4]
    for h in range(2):
        start = HALF * ((c + h) % 2)
        t = lax.broadcasted_iota(jnp.int32, (HALF, 1), 0) + start
        v = cotangent[at(start, HALF, HALF), :]
        v = jnp.where(t < length, v, jnp.zeros_like(v))
        back[HALF * h : HALF * (h + 1), :] = v
        back_t[:, HALF * h : HALF * (h + 1)] = v.T
    back_part[...] = back[at(PART * y, PART, PART), :]
    tok_part[...] = tok[at(HALF * c + PART * y, PART, PART), :]
    tok_half[...] = tok[at(HALF * c, HALF, HALF), :]


def kept(i, n, length):
    t = lax.broadcasted_iota(jnp.int32, (128, n), 0) + 128 * i
    s = lax.broadcasted_iota(jnp.int32, (128, n), 1)
    return (s <= t) & (s < length)


def attend(
    ids, tok, cosine, sine, query_w, pair_w,
    normed, heads, out, lse, w, vec,
):
    for d in range(DP):
        rows = pair_w[d, ROWS:, :].astype(f32)
        pieces = []
        for y in range(4):
            v = rows[3 * y : 3 * y + 1] + rows[3 * y + 1 : 3 * y + 2] + rows[3 * y + 2 : 3 * y + 3]
            pieces += [v[:, :40], v[:, HEAD : HEAD + 40]]
        vec[:, 320 * d : 320 * (d + 1)] = jnp.concatenate(pieces, 1)
    key_start = 2 * D + JC * KEY_AT + HEAD * lax.div(jnp.minimum(ids[2], KEY_AT - 1), 3)
    bias = jnp.concatenate(
        [
            vec[:, at(2 * D + JC * ids[2], JC, JC)],
            vec[:, at(key_start, HEAD, HEAD)],
            vec[:, at(key_start + JC, HEAD, HEAD)],
        ],
        1,
    )
    w[:, :JC] = query_w[:, :ROWS, :].reshape(D, JC)
    w[:, JC:] = pair_w[:, :ROWS, :].reshape(D, JC)

    gain = vec[:, :D]

    @pl.loop(0, T // 128)
    def _(i):
        rows = at(i * 128, 128, 128)
        x = tok[rows, :].astype(f32)
        s = lax.rsqrt(jnp.mean(x * x, -1, keepdims=True) + EPS_NORM)
        n = (x * s * gain).astype(bf16)
        normed[rows, :] = n
        j = nn(n, w[...]) + bias
        for h in range(4):
            cols = slice(HEAD * h, HEAD * (h + 1))
            u = j[:, cols]
            if h < 3:
                u = u * cosine[rows, :] + pltpu.roll(u, HEAD // 2, 1) * sine[rows, :]
            heads[rows, cols] = u.astype(bf16)

    for h in range(2):
        for i in range(4):
            n = 128 * (i + 1)
            q = heads[128 * i : n, HEAD * h : HEAD * (h + 1)]
            k, v = heads[:n, 2 * HEAD : 3 * HEAD], heads[:n, 3 * HEAD :]
            s = jnp.where(kept(i, n, ids[0]), nt(q, k) * SCALE, MASKED)
            m = jnp.max(s, -1, keepdims=True)
            e = jnp.exp(s - m)
            total = jnp.sum(e, -1, keepdims=True)
            o = nn((e / total).astype(bf16), v).astype(bf16)
            lse[128 * i : n, HEAD * h : HEAD * (h + 1)] = jnp.broadcast_to(
                m + jnp.log(total), (128, HEAD)
            )
            at_row = 128 * (i % 2)
            for y in range(4):
                out[2 * y + i // 2, at_row : at_row + 128, HEAD * h : HEAD * (h + 1)] = o


def assemble(ids, a0, a1, a2, a3, b0, b1, b2, b3, mixer, rows_w):
    y, c = ids[3], ids[4]
    for e, a, b in zip(RELATIVE, (a0, a1, a2, a3), (b0, b1, b2, b3)):
        first = 384 * lax.rem(y + e + 4, 4)
        left, right = at(first, JC, 128), at(first + JC, HEAD, 128)
        for d in range(DP):
            for half, v in ((c, a), (1 - c, b)):
                row = ROWS * d + 48 * half
                mixer[at(row, 48, 16), left] = v[d, :48, :]
                mixer[at(row, 32, 16), right] = v[d, 48:80, :HEAD]
                mixer[at(row + 32, 16, 16), right] = v[d, 48:64, HEAD:]
    rows_w[...] = mixer[at(JC * jnp.minimum(ids[2], KEY_AT - 1), JC, JC), :]


def mix(ids, att, mixer, tok, vec, hidden_part, normed, hidden, side):
    i = pl.program_id(0)

    @pl.when(i == 0)
    def _():
        for j in range(KEY_AT):
            side[:, JC * j : JC * (j + 1)] = att[j]

    cols = at(384 * i, 384, 384)
    hidden[:, cols] = nn(side[...], mixer[...]) + tok[...].astype(f32)

    @pl.when(i == 3)
    def _():
        hidden_part[...] = hidden[at(PART * ids[3], PART, PART), :]
        for r in range(0, HALF, 64):
            v = hidden[r : r + 64, :]
            s = lax.rsqrt(jnp.mean(v * v, -1, keepdims=True) + EPS_NORM)
            normed[r : r + 64, :] = (v * s * vec[:, D : 2 * D]).astype(bf16)


def gated(near, far, back, back_t, w, act, gate_grad, up_grad, grads, near_t):
    @pl.when(pl.program_id(0) == 0)
    def _():
        near_t[:, :HALF] = near[...].T
        near_t[:, HALF:] = far[...].T

    gate_w, up_w, down_w = [w[:, m].reshape(D, 256) for m in range(3)]
    for r, normed in ((0, near), (HALF, far)):
        rows = slice(r, r + HALF)
        g = nn(normed[...], gate_w)
        u = nn(normed[...], up_w)
        a = nn(back[rows, :], down_w)
        sigma = 1.0 / (1.0 + jnp.exp(-g))
        swished = g * sigma
        act[rows, :] = (swished * u).astype(bf16)
        gate_grad[rows, :] = (a * u * sigma * (1.0 + g * (1.0 - sigma))).astype(bf16)
        up_grad[rows, :] = (a * swished).astype(bf16)
    for m, (left, right) in enumerate(((near_t, gate_grad), (near_t, up_grad), (back_t, act))):
        for r in range(4):
            part = nn(left[384 * r : 384 * (r + 1), :], right[...]).astype(bf16)
            grads[4 * r : 4 * (r + 1), m] = part.reshape(4, ROWS, 256)


def spread(gate_grad, up_grad, w, near, far):
    gate_w, up_w = [w[:, m].reshape(768, FP) for m in range(2)]
    for b in range(3):
        cols = slice(256 * b, 256 * (b + 1))
        part = nt(gate_grad[...], gate_w[cols]) + nt(up_grad[...], up_w[cols])
        near[:, cols] = part[:HALF].astype(bf16)
        far[:, cols] = part[HALF:].astype(bf16)


def spread_out(act, w, near, far):
    down_w = w[:, 0].reshape(768, FP)
    for b in range(3):
        cols = slice(256 * b, 256 * (b + 1))
        part = nt(act[...], down_w[cols])
        near[:, cols] = part[:HALF].astype(bf16)
        far[:, cols] = part[HALF:].astype(bf16)


def halve(ids, near, other, own, p1, p2, p3):
    y = ids[3]
    for k, out in ((0, own), (1, p1), (3, p2), (2, p3)):
        rows = at(PART * lax.rem(y + k, 4), PART, PART)
        out[...] = (near[rows, :].astype(f32) + other[rows, :].astype(f32)).astype(out.dtype)


def summed(own, parts):
    total = own[...]
    for part in parts:
        total += part[...].astype(f32)
    return total


def hidden_back(ids, own, a1, a2, a3, hidden, back, gain, grad, low, gain_part):
    h = hidden[...]
    g = summed(own, (a1, a2, a3))
    scale = lax.rsqrt(jnp.mean(h * h, -1, keepdims=True) + EPS_NORM)
    gain_part[...] = jnp.sum(g * h * scale, 0, keepdims=True)
    v = back[...].astype(f32) + norm_back(h, scale, gain[...], g)
    grad[...] = v
    low[...] = v.astype(bf16)


def finish_out(ids, total, hidden, done):
    length, y, c = ids[0], ids[3], ids[4]
    t = lax.broadcasted_iota(jnp.int32, (PART, 1), 0) + HALF * c + PART * y
    done[...] = jnp.where(t < length, total[...] + hidden[...], 0.0).astype(bf16)


def finish_in(ids, own, a1, a2, a3, tok, grad, gain, done):
    x = tok[...].astype(f32)
    scale = lax.rsqrt(jnp.mean(x * x, -1, keepdims=True) + EPS_NORM)
    g = summed(own, (a1, a2, a3))
    done[...] = (grad[...] + norm_back(x, scale, gain[...], g)).astype(bf16)


def attend_back(
    ids, near, far, rows_w, heads, lse, cosine, sine,
    grads, window, own_kind, other_kind, low, att_grad, key_grad, value_grad,
):
    length, y, c = ids[0], ids[3], ids[4]
    for k, e in enumerate(RELATIVE):
        place = PART * lax.rem(y + e + 4, 4)
        low[at(HALF * c + place, PART, PART), :] = near[k]
        low[at(HALF * (1 - c) + place, PART, PART), :] = far[k]
    window[...] = low[:, at(384 * y, 384, 384)]
    has_heads = (ids[2] < KEY_AT).astype(f32)
    att_grad[...] = (nt(low[...], rows_w[...]) * has_heads).astype(bf16)
    key_grad[...] = jnp.zeros_like(key_grad)
    value_grad[...] = jnp.zeros_like(value_grad)
    for h in range(2):
        cols = slice(HEAD * h, HEAD * (h + 1))
        for i in range(4):
            n = 128 * (i + 1)
            rows = slice(128 * i, n)
            q = heads[rows, cols]
            k, v = heads[:n, 2 * HEAD : 3 * HEAD], heads[:n, 3 * HEAD :]
            o = att_grad[rows, cols]
            s = nt(q, k) * SCALE
            p = jnp.where(kept(i, n, length), jnp.exp(s - lse[rows, HEAD * h : HEAD * h + 1]), 0.0)
            d = nt(o, v)
            g = (p * (d - jnp.sum(p * d, -1, keepdims=True))).astype(bf16)
            value_grad[:n, :] += tn(p.astype(bf16), o)
            key_grad[:n, :] += tn(g, q)
            dq = nn(g, k) * SCALE
            dq = dq * cosine[rows, :] - pltpu.roll(dq, HEAD // 2, 1) * sine[rows, :]
            grads[rows, cols] = dq.astype(bf16)
    dk = key_grad[...] * SCALE
    dk = dk * cosine[...] - pltpu.roll(dk, HEAD // 2, 1) * sine[...]
    grads[:, 2 * HEAD : 3 * HEAD] = dk.astype(bf16)
    grads[:, 3 * HEAD :] = value_grad[...].astype(bf16)
    k, v = grads[:, 2 * HEAD : 3 * HEAD], grads[:, 3 * HEAD :]

    @pl.when(c == 0)
    def _():
        own_kind[...] = k
        other_kind[...] = v

    @pl.when(c != 0)
    def _():
        own_kind[...] = v
        other_kind[...] = k


def joint_back(
    ids, grads, w, tok, second_part,
    near, far, chunks, gain_part, vec, blocks,
):
    g = grads[...]
    gain_part[...] = jnp.zeros_like(gain_part)
    for r in range(0, T, 128):
        rows = slice(r, r + 128)
        back = nt(g[rows], w[...])
        half, place = r // HALF, slice(r % HALF, r % HALF + 128)
        moves = back.astype(bf16)

        @pl.when(ids[4] == half)
        def _():
            near[place, :] = moves

        @pl.when(ids[4] != half)
        def _():
            far[place, :] = moves

        x = tok[rows, :].astype(f32)
        s = lax.rsqrt(jnp.mean(x * x, -1, keepdims=True) + EPS_NORM)
        gain_part[...] += jnp.sum(back * x * s, 0, keepdims=True)
    vec[...] = jnp.zeros_like(vec)
    vec[:, :D] = gain_part[...]
    vec[:, D : 2 * D] = second_part[...]
    bias = jnp.sum(g.astype(f32), 0, keepdims=True)
    head_at = jnp.minimum(ids[2], KEY_AT - 1)
    key_start = 2 * D + JC * KEY_AT + HEAD * lax.div(head_at, 3)
    vec[:, at(2 * D + JC * head_at, JC, JC)] = bias[:, :JC]
    vec[:, at(key_start, HEAD, HEAD)] = bias[:, JC : JC + HEAD]
    vec[:, at(key_start + JC, HEAD, HEAD)] = bias[:, JC + HEAD :]
    for d in range(DP):
        blocks[d : d + 1, :] = vec[:, 320 * d : 320 * (d + 1)]
    for m in range(MP):
        piece = blocks[:, 40 * m : 40 * (m + 1)]
        piece = jnp.concatenate([piece, jnp.zeros((DP, HEAD - 40), f32)], 1)
        high = piece.astype(bf16)
        chunks[m, :DP, :] = high
        chunks[m, DP:, :] = (piece - high.astype(f32)).astype(bf16)


def back_to_input(
    ids, near_low, far_low, rows_w, heads, lse, cosine, sine, w, tok, second_part,
    grads, window, own_kind, other_kind, near, far, chunks,
    low, att_grad, key_grad, value_grad, gain_part, vec, blocks, w_held, tok_held, sems,
):
    copies = [
        pltpu.make_async_copy(w, w_held, sems.at[0]),
        pltpu.make_async_copy(tok, tok_held, sems.at[1]),
    ]
    for copy in copies:
        copy.start()
    attend_back(
        ids, near_low, far_low, rows_w, heads, lse, cosine, sine,
        grads, window, own_kind, other_kind, low, att_grad, key_grad, value_grad,
    )
    for copy in copies:
        copy.wait()
    joint_back(ids, grads, w_held, tok_held, second_part, near, far, chunks, gain_part, vec, blocks)


def group_parts(ids, own, other, o0, o1, o2, o3, both, left, right, out_sum):
    out_sum[...] = summed(o0, (o1, o2, o3))
    own_group = lax.div(jnp.minimum(ids[2], KEY_AT - 1), 3)
    partner = ids[2] + 1 - 2 * ids[4]
    other_group = lax.div(jnp.minimum(partner, KEY_AT - 1), 3)
    a, b = own[...].astype(f32), other[...].astype(f32)
    for g, out in ((0, left), (1, right)):
        part = a * (own_group == g).astype(f32) + b * (other_group == g).astype(f32)
        out[...] = part.astype(bf16)
        both[:, HEAD * g : HEAD * (g + 1)] = part.astype(bf16)


def weigh_joint(ids, normed, grads, left, right, both, moved, mixer_parts, parts):
    pair = jnp.concatenate([left[...].astype(f32), right[...].astype(f32)], 1)
    pair = pair + both[...].astype(f32)
    own = grads[:, :JC].astype(f32)
    g = jnp.where(ids[2] < KEY_AT, own, pair).astype(bf16)
    for r in range(4):
        cols = slice(384 * r, 384 * (r + 1))
        part = tn(normed[:, cols], g).astype(bf16)
        parts[4 * r : 4 * (r + 1), :ROWS, :] = part.reshape(4, ROWS, JC)
    parts[:, ROWS : ROWS + 80, :] = mixer_parts[...]
    vec = moved[0].astype(f32)
    for j in range(1, MP):
        vec += moved[j].astype(f32)
    vec = vec[:DP] + vec[DP:]
    high = vec.astype(bf16).astype(f32)
    for d in range(DP):
        parts[d, ROWS + 80 :, :HEAD] = jnp.broadcast_to(high[d : d + 1], (8, HEAD)).astype(bf16)
        low = (vec - high)[d : d + 1]
        parts[d, ROWS + 80 :, HEAD:] = jnp.broadcast_to(low, (8, HEAD)).astype(bf16)


def weigh_mixer(ids, near, far, low, packed, parts):
    c = ids[4]

    def own_columns(half):
        v = low[at(HALF * half, HALF, HALF), :].astype(f32)
        return jnp.where(c == 0, v[:, :MC], v[:, MC:]).astype(bf16)

    mine, other = own_columns(c), own_columns(1 - c)
    for j in range(KEY_AT):
        part = tn(near[j], mine) + tn(far[j], other)
        start = JC * j
        while start < JC * (j + 1):
            stop = min((start // ROWS + 1) * ROWS, JC * (j + 1))
            first = start % ROWS
            parts[start // ROWS, first : first + stop - start, :] = part[
                start - JC * j : stop - JC * j
            ]
            start = stop
    for d in range(DP):
        left, right = parts[d, :, :HEAD], parts[d, :, HEAD:]
        packed[d, :48, :HEAD] = left[:48].astype(bf16)
        packed[d, :48, HEAD:] = left[48:].astype(bf16)
        packed[d, 48:, :HEAD] = jnp.concatenate([right[:32], right[32:64]], 1).astype(bf16)
        packed[d, 48:, HEAD:] = jnp.concatenate(
            [right[64:], jnp.zeros((32, JC - MC), f32)], 1
        ).astype(bf16)


def settle_grads(ids, moved, ff, joint, mixer, vector, squares):
    total = moved[0].astype(f32)
    for d in range(1, DP):
        total += moved[d].astype(f32)
    joint[...] = total[:ROWS]
    left, right = total[ROWS : ROWS + 48], total[ROWS + 48 : ROWS + 80]
    mixer[:48, :HEAD] = left[:, :HEAD]
    mixer[48:, :HEAD] = left[:, HEAD:]
    mixer[:32, HEAD:] = right[:, : MC - HEAD]
    mixer[32:64, HEAD:] = right[:, MC - HEAD : HEAD]
    mixer[64:, HEAD:] = right[:, HEAD:MC]
    vec = total[ROWS + 80 : ROWS + 81, :HEAD] + total[ROWS + 80 : ROWS + 81, HEAD:]
    vector[...] = vec
    total = total[: ROWS + 80]
    total = jnp.sum(total * total) + jnp.sum(vec * vec)
    for m in range(3):
        v = ff[m].astype(f32)
        total += jnp.sum(v * v)
    squares[...] = jnp.full(squares.shape, total, f32)


def update(
    squares, joint_grad, mixer_grad, ff_grad, vector_grad,
    joint_w, joint_m, joint_v, mixer_w, mixer_m, mixer_v, expand_w, expand_m, expand_v,
    shrink_w, shrink_m, shrink_v, vector_w, vector_m, vector_v,
    norm_out, joint_wn, joint_mn, joint_vn, mixer_wn, mixer_mn, mixer_vn,
    expand_wn, expand_mn, expand_vn, shrink_wn, shrink_mn, shrink_vn,
    vector_wn, vector_mn, vector_vn,
):
    norm = jnp.sqrt(jnp.sum(squares[:, 0, :], 0, keepdims=True))
    norm_out[...] = norm
    clip = jnp.minimum(1.0, MAX_NORM / (norm[:, :1] + 1e-06))

    def step(grad, before, after, rate, decay, part=Ellipsis):
        w, m, v = [ref[part] for ref in before]
        results = adam_step(w, clip * grad, m, v, rate, decay)
        for ref, new in zip(after, results):
            ref[part] = new

    step(
        joint_grad[...], (joint_w, joint_m, joint_v), (joint_wn, joint_mn, joint_vn),
        RATE_MATRIX, DECAY,
    )
    step(
        mixer_grad[...], (mixer_w, mixer_m, mixer_v), (mixer_wn, mixer_mn, mixer_vn),
        RATE_MATRIX, DECAY,
    )
    for m in range(2):
        step(
            ff_grad[m, :, :FF].astype(f32),
            (expand_w, expand_m, expand_v), (expand_wn, expand_mn, expand_vn),
            RATE_MATRIX, DECAY, m,
        )
    step(
        ff_grad[2, :, :FF].astype(f32),
        (shrink_w, shrink_m, shrink_v), (shrink_wn, shrink_mn, shrink_vn),
        RATE_MATRIX, DECAY,
    )
    step(
        vector_grad[:, :40], (vector_w, vector_m, vector_v), (vector_wn, vector_mn, vector_vn),
        RATE_VECTOR, 0.0,
    )


def write_half(ids, half, pieces, outs, rows, sems):
    for k, e in enumerate(RELATIVE):
        place = at(PART * lax.rem(ids[3] + e + 4, 4), PART, PART)
        for n in range(2):
            rows[n, place, :] = pieces[n][k][...].astype(f32)
    copies = [
        pltpu.make_async_copy(rows.at[n], out.at[0, at(HALF * half, HALF, HALF)], sems.at[n])
        for n, out in enumerate(outs)
    ]
    for copy in copies:
        copy.start()
    for copy in copies:
        copy.wait()


def settle_near(
    ids, a0, a1, a2, a3, b0, b1, b2, b3, output, input_grad, token, rows, sems
):
    token[...] = jnp.zeros_like(token)
    pieces = (a0, a1, a2, a3), (b0, b1, b2, b3)
    write_half(ids, ids[4], pieces, (output, input_grad), rows, sems)


def settle_far(ids, far, _a, _b, output, input_grad, rows, sems):
    pieces = [[far.at[4 * n + k] for k in range(4)] for n in range(2)]
    write_half(ids, 1 - ids[4], pieces, (output, input_grad), rows, sems)


def pile(ids, *refs):
    for k, p in enumerate(refs[:-1]):
        refs[-1][k] = p[...]


def norm_back(v, scale, gain, grad):
    scaled = gain * grad
    return scale * scaled - v * scale * scale * scale * jnp.mean(scaled * v, -1, keepdims=True)


def adam_step(weight, grad, moment, square, rate, decay):
    moment_next = BETA_ONE * moment + (1.0 - BETA_ONE) * grad
    square_next = BETA_TWO * square + (1.0 - BETA_TWO) * grad * grad
    first_hat = moment_next * (1.0 / (1.0 - BETA_ONE**STEP))
    second_hat = square_next * (1.0 / (1.0 - BETA_TWO**STEP))
    weight_next = weight - rate * (first_hat / (jnp.sqrt(second_hat) + ADAM_EPS) + decay * weight)
    return (weight_next, moment_next, square_next)


def tables():
    freq = np.float32(ROPE_BASE) ** (-np.arange(0, HEAD, 2, dtype=np.float32) / np.float32(HEAD))
    angle = np.arange(T, dtype=np.float32)[:, None] * freq.astype(np.float32)[None, :]
    cosine, sine = np.cos(angle), np.sin(angle)
    return (
        np.concatenate([cosine, cosine], -1).astype(np.float32),
        np.concatenate([-sine, sine], -1).astype(np.float32),
    )


def split_low(v):
    high = lax.reduce_precision(v, 8, 7)
    middle = lax.reduce_precision(v - high, 8, 7)
    return [part.astype(bf16) for part in (high, middle, v - high - middle)]


def body(
    tokens, lengths, cotangent,
    joint_weight, joint_moment, joint_square,
    mixer_weight, mixer_moment, mixer_square,
    expand_weight, expand_moment, expand_square,
    shrink_weight, shrink_moment, shrink_square,
    vector_params, vector_moment, vector_square,
):
    dp, mp = lax.axis_index("dp"), lax.axis_index("mp")
    y, c = mp // 2, mp % 2
    tok, length = tokens[0], lengths[0]
    ids = jnp.stack([length, dp, mp, y, c]).astype(jnp.int32)

    stack = jnp.concatenate(
        [expand_weight.astype(bf16), shrink_weight.T.astype(bf16)[None]], 0
    )
    stack = jnp.pad(stack, ((0, 0), (0, 0), (0, FP - FF)))
    ff = lax.all_gather(stack, "dp", axis=0, tiled=False)

    low = jnp.concatenate([joint_weight.astype(bf16), mixer_weight.astype(bf16)], 1)
    vec = jnp.pad(jnp.stack(split_low(vector_params)), ((0, 13), (0, JC + MC - 40)))
    low = jnp.concatenate([low, vec], 0)
    other = swap_core(low)
    first, second = jnp.where(c == 0, low, other), jnp.where(c == 0, other, low)
    pairs = [
        jnp.concatenate([first[:ROWS, cols], second[:ROWS, cols]], 1)
        for cols in (slice(0, HEAD), slice(HEAD, JC))
    ]
    chip = jnp.concatenate([first[:ROWS, JC:], second[:ROWS, JC:]], 1)
    chip = lax.dynamic_slice_in_dim(chip, 48 * c, 48, 0)
    rest = jnp.concatenate([chip[:32, JC:], jnp.pad(chip[32:, JC:], ((0, 16), (0, 0)))], 1)
    sent = jnp.concatenate([low[:ROWS, :JC], chip[:, :JC], rest], 0)
    query_w = exchange(jnp.broadcast_to(sent, (DP,) + sent.shape), "dp")
    vec = jnp.concatenate([first[ROWS:, :HEAD], second[ROWS:, :HEAD]], 1)
    sends = [pairs[0], pairs[1], jnp.where(c == 0, pairs[0], pairs[1])]
    sends = [jnp.concatenate([v, vec], 0) for v in sends]
    a1, a2, a3 = [shift_y(v, k) for v, k in zip(sends, (1, -1, 2))]
    pair = jnp.where(y == 0, a1[:ROWS], jnp.where(y == 2, a2[:ROWS], a3[:ROWS]))
    vec = jnp.stack([vec, a2[ROWS:], a3[ROWS:], a1[ROWS:]])[:, :3]
    vec = lax.dynamic_slice_in_dim(jnp.concatenate([vec, vec]), (4 - y) % 4, 4, 0)
    sent = jnp.concatenate([pair, vec.reshape(12, JC), query_w[0, :4]], 0)
    pair_w = exchange(jnp.broadcast_to(sent, (DP,) + sent.shape), "dp")
    cosine, sine = tables()
    back, back_t, back_part, tok_part, tok_half = whole(
        prepare,
        [
            ((T, D), bf16), ((D, T), bf16),
            ((PART, D), bf16), ((PART, D), bf16), ((HALF, D), bf16),
        ],
        [ids, cotangent[0], tok],
    )
    normed, heads, att_sent, lse, joint_w, vec = whole(
        attend,
        [
            ((T, D), bf16), ((T, 2 * JC), bf16), ((MP, HALF, JC), bf16),
            ((T, JC), f32), ((D, 2 * JC), bf16), ((1, VEC), f32),
        ],
        [ids, tok, cosine, sine, query_w, pair_w],
        after=[back],
    )
    gain_first, gain_second = vec[:, :D], vec[:, D : 2 * D]
    att_near = exchange(att_sent, "mp")
    att_far = swap_core(att_near)
    mixer_near = gather(shift_y, query_w[:, ROWS:])
    mixer_far = [swap_core(v) for v in mixer_near]
    mixer, rows_w = whole(
        assemble, [((D, D), bf16), ((JC, D), bf16)], [ids] + mixer_near + mixer_far
    )

    def fixed(shape):
        return pl.BlockSpec(shape, lambda i: (0,) * len(shape))

    hidden_part, normed_near = pl.pallas_call(
        mix,
        grid=(4,),
        out_shape=[jax.ShapeDtypeStruct((PART, D), f32), jax.ShapeDtypeStruct((HALF, D), bf16)],
        in_specs=[
            SM,
            fixed((MP, HALF, JC)),
            pl.BlockSpec((D, 384), lambda i: (0, i)),
            pl.BlockSpec((HALF, 384), lambda i: (0, i)),
            fixed((1, VEC)),
        ],
        out_specs=[fixed((PART, D)), fixed((HALF, D))],
        scratch_shapes=[pltpu.VMEM((HALF, D), f32), pltpu.VMEM((HALF, D), bf16)],
        compiler_params=pltpu.CompilerParams(vmem_limit_bytes=60 * MiB),
        cost_estimate=SMALL,
    )(ids, att_near, mixer, tok_half, vec)
    normed_far = swap_core(normed_near)

    def columns(n):
        return pl.BlockSpec((n, 256), lambda i: (0, i))

    block = pl.BlockSpec((DP, 3, ROWS, 256), lambda i: (0, 0, 0, i))
    act, gate_grad, up_grad, ff_grads = pl.pallas_call(
        gated,
        grid=(pl.cdiv(FP, 256),),
        out_shape=[jax.ShapeDtypeStruct((T, FP), bf16)] * 3
        + [jax.ShapeDtypeStruct((DP, 3, ROWS, FP), bf16)],
        in_specs=[fixed((HALF, D)), fixed((HALF, D)), fixed((T, D)), fixed((D, T)), block],
        out_specs=[columns(T)] * 3 + [block],
        scratch_shapes=[pltpu.VMEM((D, T), bf16)],
        compiler_params=pltpu.CompilerParams(vmem_limit_bytes=60 * MiB),
        cost_estimate=SMALL,
    )(normed_near, normed_far, back, back_t, ff)
    ff_shard = lax.psum_scatter(ff_grads, "dp", scatter_dimension=0, tiled=False)

    near, far = pl.pallas_call(
        spread,
        grid=(2,),
        out_shape=[jax.ShapeDtypeStruct((HALF, D), bf16)] * 2,
        in_specs=[fixed((T, FP))] * 2
        + [pl.BlockSpec((DP // 2, 2, ROWS, FP), lambda i: (i, 0, 0, 0))],
        out_specs=[pl.BlockSpec((HALF, 768), lambda i: (0, i))] * 2,
        compiler_params=pltpu.CompilerParams(vmem_limit_bytes=60 * MiB),
        cost_estimate=SMALL,
    )(gate_grad, up_grad, ff)

    def half_sum(near, far, after=()):
        own, *parts = whole(
            halve,
            [((PART, D), f32)] + [((PART, D), bf16)] * 3,
            [ids, near, swap_core(far)],
            after=after,
            limit=8,
        )
        return [own] + [shift_y(v, k) for v, k in zip(parts, (1, -1, 2))]

    normed_second_parts = half_sum(near, far)
    out_near, out_far = pl.pallas_call(
        spread_out,
        grid=(2,),
        out_shape=[jax.ShapeDtypeStruct((HALF, D), bf16)] * 2,
        in_specs=[
            fixed((T, FP)),
            pl.BlockSpec((DP // 2, 1, ROWS, FP), lambda i: (i, 2, 0, 0)),
        ],
        out_specs=[pl.BlockSpec((HALF, 768), lambda i: (0, i))] * 2,
        compiler_params=pltpu.CompilerParams(vmem_limit_bytes=60 * MiB),
        cost_estimate=SMALL,
    )(act, ff)
    hidden_grad, low, gain_second_part = whole(
        hidden_back,
        [((PART, D), f32), ((PART, D), bf16), ((1, D), f32)],
        [ids] + normed_second_parts + [hidden_part, back_part, gain_second],
        after=[out_far],
        limit=8,
    )
    out_parts = half_sum(out_near, out_far)
    low_near = jnp.stack(gather(shift_y, low))
    low_far = swap_core(low_near)
    heads_grad, hidden_low, own_kind, other_kind, input_near, input_far, chunks = whole(
        back_to_input,
        [
            ((T, 2 * JC), bf16), ((T, 2 * MC), bf16), ((T, HEAD), bf16), ((T, HEAD), bf16),
            ((HALF, D), bf16), ((HALF, D), bf16), ((MP, 2 * DP, HEAD), bf16),
        ],
        [ids, low_near, low_far, rows_w, heads, lse, cosine, sine, joint_w, tok, gain_second_part],
        scratch=[
            pltpu.VMEM((T, D), bf16),
            pltpu.VMEM((T, JC), bf16),
            pltpu.VMEM((T, HEAD), f32),
            pltpu.VMEM((T, HEAD), f32),
            pltpu.VMEM((1, D), f32),
            pltpu.VMEM((1, DP * MP * 40), f32),
            pltpu.VMEM((DP, MP * 40), f32),
            pltpu.VMEM((D, 2 * JC), bf16),
            pltpu.VMEM((T, D), bf16),
            pltpu.SemaphoreType.DMA((2,)),
        ],
        after=[out_parts[0]],
        loose=(8, 9),
    )
    both, left, right, out_sum = whole(
        group_parts,
        [((T, JC), bf16), ((T, HEAD), bf16), ((T, HEAD), bf16), ((PART, D), f32)],
        [ids, own_kind, swap_core(other_kind)] + out_parts,
        limit=8,
    )
    left, right, both = to_last_chip(left, 0), to_last_chip(right, 2), to_last_chip(both, 1)
    moved = exchange(chunks, "mp")
    (mixer_parts,) = whole(
        weigh_mixer,
        [((DP, 80, JC), bf16)],
        [ids, att_near, att_far, hidden_low],
        scratch=[pltpu.VMEM((DP, ROWS, MC), f32)],
        after=[out_sum],
    )
    (joint_parts,) = whole(
        weigh_joint,
        [((DP, ROWS + 88, JC), bf16)],
        [ids, normed, heads_grad, left, right, both, moved, mixer_parts],
    )
    joint_shard, mixer_shard, vector_shard, squares = whole(
        settle_grads,
        [((ROWS, JC), f32), ((ROWS, MC), f32), ((1, HEAD), f32), ((DP * MP, 1, HEAD), f32)],
        [ids, exchange(joint_parts, "dp"), ff_shard],
    )

    squares = exchange(squares, ("dp", "mp"))

    parts = half_sum(input_near, input_far, after=[joint_parts])
    (done,) = whole(
        finish_out, [((PART, D), bf16)], [ids, out_sum, hidden_part], limit=8, after=[joint_parts]
    )
    done_parts = gather(shift_y, done)
    (done,) = whole(
        finish_in,
        [((PART, D), bf16)],
        [ids] + parts + [tok_part, hidden_grad, gain_first],
        limit=8,
        after=done_parts[1:],
    )
    done_parts += gather(shift_y, done)
    anywhere = pl.BlockSpec(memory_space=pl.ANY)
    results = [jax.ShapeDtypeStruct((1, T, D), f32)] * 2
    held = [pltpu.VMEM((2, HALF, D), f32), pltpu.SemaphoreType.DMA((2,))]
    *halves, token = pl.pallas_call(
        settle_near,
        out_shape=results + [jax.ShapeDtypeStruct((8, HEAD), f32)],
        in_specs=[SM] + [VM] * 8,
        out_specs=[anywhere] * 2 + [VM],
        scratch_shapes=held,
        compiler_params=pltpu.CompilerParams(vmem_limit_bytes=16 * MiB),
        cost_estimate=SMALL,
    )(ids, *done_parts)
    (done_near,) = whole(
        pile, [((8, PART, D), bf16)], [ids] + done_parts, after=[squares, token], limit=8
    )
    output, input_grad = pl.pallas_call(
        settle_far,
        out_shape=results,
        in_specs=[SM, VM] + [anywhere] * 2,
        out_specs=[anywhere] * 2,
        input_output_aliases={2: 0, 3: 1},
        scratch_shapes=held,
        compiler_params=pltpu.CompilerParams(vmem_limit_bytes=16 * MiB),
        cost_estimate=SMALL,
    )(ids, swap_core(done_near), *halves)

    matrices = [joint_weight, joint_moment, joint_square]
    matrices += [mixer_weight, mixer_moment, mixer_square]
    matrices += [expand_weight, expand_moment, expand_square]
    matrices += [v.T for v in (shrink_weight, shrink_moment, shrink_square)]
    matrices += [v[None] for v in (vector_params, vector_moment, vector_square)]
    def third(shape):
        n = len(shape)
        if shape[-2] != ROWS:
            return pl.BlockSpec(shape, lambda i: (0,) * n)
        return pl.BlockSpec(
            shape[:-2] + (ROWS // 3, shape[-1]), lambda i: (0,) * (n - 2) + (i, 0)
        )

    given = [squares, joint_shard, mixer_shard, ff_shard, vector_shard] + matrices
    made = [(1, HEAD)] + [v.shape for v in matrices]
    norm, *new = pl.pallas_call(
        update,
        grid=(3,),
        out_shape=[jax.ShapeDtypeStruct(shape, f32) for shape in made],
        in_specs=[third(v.shape) for v in given],
        out_specs=[third(shape) for shape in made],
        compiler_params=pltpu.CompilerParams(vmem_limit_bytes=60 * MiB),
        cost_estimate=SMALL,
    )(*given)
    new[9:12] = [v.T for v in new[9:12]]
    new[12:] = [v[0] for v in new[12:]]
    return (output, input_grad, norm[0, 0], *new)


def solution(mesh):
    row = P("dp", None, None)
    matrix = [P("dp", "mp")] * 6 + [P(None, "dp", "mp")] * 3 + [P("mp", "dp")] * 3
    vector = [P(("dp", "mp"))] * 3
    return jax.shard_map(
        body,
        mesh=mesh,
        in_specs=tuple([row, P("dp"), row] + matrix + vector),
        out_specs=tuple([row, row, P()] + matrix + vector),
        check_vma=False,
    )
```

```python
import jax
import jax.numpy as jnp
import numpy as np
from jax import lax
from jax.experimental import pallas as pl
from jax.experimental.pallas import tpu as pltpu
from jax.sharding import PartitionSpec as P

QUERY_HEADS = 12
KEY_VALUE_HEADS = 2
HEAD = 128
STEP = 5
EPS_NORM = 1e-06
ROPE_BASE = 1000000.0
MAX_NORM = 1.0
BETA_ONE = 0.9
BETA_TWO = 0.95
ADAM_EPS = 1e-08
DECAY = 0.1
RATE_MATRIX = 0.06
RATE_VECTOR = 0.8
MASKED = -1e30

T = 512
HALF = 256
PART = 64
D = 1536
FF = 1120
FP = 1152
DP = 16
MP = 8
VEC = 5120
ROWS = D // DP
JC = 256
MC = 192
KEY_AT = 6
SCALE = HEAD ** (-0.5)

f32 = jnp.float32
bf16 = jnp.bfloat16
VM = pl.BlockSpec(memory_space=pltpu.VMEM)
SM = pl.BlockSpec(memory_space=pltpu.SMEM)
MiB = 1 << 20
SMALL = pl.CostEstimate(flops=1, bytes_accessed=1, transcendentals=0)


def shift_y(v, k):
    return lax.ppermute(v, "mp", [(i, (i + 2 * k) % MP) for i in range(MP)])


def from_last_chip(v, k):
    return lax.ppermute(v, "mp", [(i, (i + 2 * k) % MP) for i in (MP - 2, MP - 1)])


def to_last_chip(v, y):
    return lax.ppermute(v, "mp", [(2 * y + c, MP - 2 + c) for c in range(2)])


def swap_core(v):
    return lax.ppermute(v, "mp", [(i, i ^ 1) for i in range(MP)])


def exchange(v, axis):
    return lax.all_to_all(v, axis, split_axis=0, concat_axis=0, tiled=True)


RELATIVE = (0, 2, -1, 1)


def gather(shift, v):
    return [v, shift(v, 2), shift(v, 1), shift(v, -1)]


def nn(a, b):
    return lax.dot_general(a, b, (((1,), (0,)), ((), ())), preferred_element_type=f32)


def nt(a, b):
    return lax.dot_general(a, b, (((1,), (1,)), ((), ())), preferred_element_type=f32)


def tn(a, b):
    return lax.dot_general(a, b, (((0,), (0,)), ((), ())), preferred_element_type=f32)


def whole(body, outs, args, scratch=(), limit=60, after=(), loose=()):
    n = len(args)

    def bare(*refs):
        body(*refs[:n], *refs[n + len(after) :])

    return pl.pallas_call(
        bare,
        out_shape=[jax.ShapeDtypeStruct(s, d) for s, d in outs],
        in_specs=[SM]
        + [pl.BlockSpec(memory_space=pl.ANY) if k in loose else VM for k in range(1, n)]
        + [pl.BlockSpec(memory_space=pl.ANY)] * len(after),
        out_specs=[VM] * len(outs),
        scratch_shapes=list(scratch),
        compiler_params=pltpu.CompilerParams(vmem_limit_bytes=limit * MiB),
        cost_estimate=SMALL,
    )(*args, *after)


def at(start, size, step):
    return pl.ds(pl.multiple_of(start, step), size)


def prepare(ids, cotangent, tok, back, back_t, back_part, tok_part, tok_half):
    length, y, c = ids[0], ids[3], ids[4]
    for h in range(2):
        start = HALF * ((c + h) % 2)
        t = lax.broadcasted_iota(jnp.int32, (HALF, 1), 0) + start
        v = cotangent[at(start, HALF, HALF), :]
        v = jnp.where(t < length, v, jnp.zeros_like(v))
        back[HALF * h : HALF * (h + 1), :] = v
        back_t[:, HALF * h : HALF * (h + 1)] = v.T
    back_part[...] = back[at(PART * y, PART, PART), :]
    tok_part[...] = tok[at(HALF * c + PART * y, PART, PART), :]
    tok_half[...] = tok[at(HALF * c, HALF, HALF), :]


def kept(i, n, length):
    t = lax.broadcasted_iota(jnp.int32, (128, n), 0) + 128 * i
    s = lax.broadcasted_iota(jnp.int32, (128, n), 1)
    return (s <= t) & (s < length)


def attend(
    ids, tok, cosine, sine, query_w, pair_w,
    normed, heads, out, lse, w, vec,
):
    for d in range(DP):
        rows = pair_w[d, ROWS:, :].astype(f32)
        pieces = []
        for y in range(4):
            v = rows[3 * y : 3 * y + 1] + rows[3 * y + 1 : 3 * y + 2] + rows[3 * y + 2 : 3 * y + 3]
            pieces += [v[:, :40], v[:, HEAD : HEAD + 40]]
        vec[:, 320 * d : 320 * (d + 1)] = jnp.concatenate(pieces, 1)
    key_start = 2 * D + JC * KEY_AT + HEAD * lax.div(jnp.minimum(ids[2], KEY_AT - 1), 3)
    bias = jnp.concatenate(
        [
            vec[:, at(2 * D + JC * ids[2], JC, JC)],
            vec[:, at(key_start, HEAD, HEAD)],
            vec[:, at(key_start + JC, HEAD, HEAD)],
        ],
        1,
    )
    w[:, :JC] = query_w[:, :ROWS, :].reshape(D, JC)
    w[:, JC:] = pair_w[:, :ROWS, :].reshape(D, JC)

    gain = vec[:, :D]

    @pl.loop(0, T // 128)
    def _(i):
        rows = at(i * 128, 128, 128)
        x = tok[rows, :].astype(f32)
        s = lax.rsqrt(jnp.mean(x * x, -1, keepdims=True) + EPS_NORM)
        n = (x * s * gain).astype(bf16)
        normed[rows, :] = n
        j = nn(n, w[...]) + bias
        for h in range(4):
            cols = slice(HEAD * h, HEAD * (h + 1))
            u = j[:, cols]
            if h < 3:
                u = u * cosine[rows, :] + pltpu.roll(u, HEAD // 2, 1) * sine[rows, :]
            heads[rows, cols] = u.astype(bf16)

    for h in range(2):
        for i in range(4):
            n = 128 * (i + 1)
            q = heads[128 * i : n, HEAD * h : HEAD * (h + 1)]
            k, v = heads[:n, 2 * HEAD : 3 * HEAD], heads[:n, 3 * HEAD :]
            s = jnp.where(kept(i, n, ids[0]), nt(q, k) * SCALE, MASKED)
            m = jnp.max(s, -1, keepdims=True)
            e = jnp.exp(s - m)
            total = jnp.sum(e, -1, keepdims=True)
            o = nn((e / total).astype(bf16), v).astype(bf16)
            lse[128 * i : n, HEAD * h : HEAD * (h + 1)] = jnp.broadcast_to(
                m + jnp.log(total), (128, HEAD)
            )
            at_row = 128 * (i % 2)
            for y in range(4):
                out[2 * y + i // 2, at_row : at_row + 128, HEAD * h : HEAD * (h + 1)] = o


def assemble(ids, a0, a1, a2, a3, b0, b1, b2, b3, mixer, rows_w):
    y, c = ids[3], ids[4]
    for e, a, b in zip(RELATIVE, (a0, a1, a2, a3), (b0, b1, b2, b3)):
        first = 384 * lax.rem(y + e + 4, 4)
        left, right = at(first, JC, 128), at(first + JC, HEAD, 128)
        for d in range(DP):
            for half, v in ((c, a), (1 - c, b)):
                row = ROWS * d + 48 * half
                mixer[at(row, 48, 16), left] = v[d, :48, :]
                mixer[at(row, 32, 16), right] = v[d, 48:80, :HEAD]
                mixer[at(row + 32, 16, 16), right] = v[d, 48:64, HEAD:]
    rows_w[...] = mixer[at(JC * jnp.minimum(ids[2], KEY_AT - 1), JC, JC), :]


def mix(ids, att, mixer, tok, vec, hidden_part, normed, hidden, side):
    i = pl.program_id(0)

    @pl.when(i == 0)
    def _():
        for j in range(KEY_AT):
            side[:, JC * j : JC * (j + 1)] = att[j]

    cols = at(384 * i, 384, 384)
    hidden[:, cols] = nn(side[...], mixer[...]) + tok[...].astype(f32)

    @pl.when(i == 3)
    def _():
        hidden_part[...] = hidden[at(PART * ids[3], PART, PART), :]
        for r in range(0, HALF, 64):
            v = hidden[r : r + 64, :]
            s = lax.rsqrt(jnp.mean(v * v, -1, keepdims=True) + EPS_NORM)
            normed[r : r + 64, :] = (v * s * vec[:, D : 2 * D]).astype(bf16)


def gated(near, far, back, back_t, w, act, gate_grad, up_grad, grads, near_t):
    @pl.when(pl.program_id(0) == 0)
    def _():
        near_t[:, :HALF] = near[...].T
        near_t[:, HALF:] = far[...].T

    gate_w, up_w, down_w = [w[:, m].reshape(D, 256) for m in range(3)]
    for r, normed in ((0, near), (HALF, far)):
        rows = slice(r, r + HALF)
        g = nn(normed[...], gate_w)
        u = nn(normed[...], up_w)
        a = nn(back[rows, :], down_w)
        sigma = 1.0 / (1.0 + jnp.exp(-g))
        swished = g * sigma
        act[rows, :] = (swished * u).astype(bf16)
        gate_grad[rows, :] = (a * u * sigma * (1.0 + g * (1.0 - sigma))).astype(bf16)
        up_grad[rows, :] = (a * swished).astype(bf16)
    for m, (left, right) in enumerate(((near_t, gate_grad), (near_t, up_grad), (back_t, act))):
        for r in range(4):
            part = nn(left[384 * r : 384 * (r + 1), :], right[...]).astype(bf16)
            grads[4 * r : 4 * (r + 1), m] = part.reshape(4, ROWS, 256)


def spread(gate_grad, up_grad, w, near, far):
    gate_w, up_w = [w[:, m].reshape(768, FP) for m in range(2)]
    for b in range(3):
        cols = slice(256 * b, 256 * (b + 1))
        part = nt(gate_grad[...], gate_w[cols]) + nt(up_grad[...], up_w[cols])
        near[:, cols] = part[:HALF].astype(bf16)
        far[:, cols] = part[HALF:].astype(bf16)


def spread_out(act, w, near, far):
    down_w = w[:, 0].reshape(768, FP)
    for b in range(3):
        cols = slice(256 * b, 256 * (b + 1))
        part = nt(act[...], down_w[cols])
        near[:, cols] = part[:HALF].astype(bf16)
        far[:, cols] = part[HALF:].astype(bf16)


def halve(ids, near, other, own, p1, p2, p3):
    y = ids[3]
    for k, out in ((0, own), (1, p1), (3, p2), (2, p3)):
        rows = at(PART * lax.rem(y + k, 4), PART, PART)
        out[...] = (near[rows, :].astype(f32) + other[rows, :].astype(f32)).astype(out.dtype)


def summed(own, parts):
    total = own[...]
    for part in parts:
        total += part[...].astype(f32)
    return total


def hidden_back(ids, own, a1, a2, a3, hidden, back, gain, grad, low, gain_part):
    h = hidden[...]
    g = summed(own, (a1, a2, a3))
    scale = lax.rsqrt(jnp.mean(h * h, -1, keepdims=True) + EPS_NORM)
    gain_part[...] = jnp.sum(g * h * scale, 0, keepdims=True)
    v = back[...].astype(f32) + norm_back(h, scale, gain[...], g)
    grad[...] = v
    low[...] = v.astype(bf16)


def finish(ids, out_sum, own, a1, a2, a3, hidden, tok, grad, gain, done):
    length, y, c = ids[0], ids[3], ids[4]
    o, g = out_sum[...], summed(own, (a1, a2, a3))
    t = lax.broadcasted_iota(jnp.int32, (PART, 1), 0) + HALF * c + PART * y
    done[0] = jnp.where(t < length, o + hidden[...], 0.0).astype(bf16)
    x = tok[...].astype(f32)
    scale = lax.rsqrt(jnp.mean(x * x, -1, keepdims=True) + EPS_NORM)
    done[1] = (grad[...] + norm_back(x, scale, gain[...], g)).astype(bf16)


def attend_back(
    ids, near, far, rows_w, heads, lse, cosine, sine,
    grads, window, own_kind, other_kind, low, att_grad, key_grad, value_grad,
):
    length, y, c = ids[0], ids[3], ids[4]
    for k, e in enumerate(RELATIVE):
        place = PART * lax.rem(y + e + 4, 4)
        low[at(HALF * c + place, PART, PART), :] = near[k]
        low[at(HALF * (1 - c) + place, PART, PART), :] = far[k]
    window[...] = low[:, at(384 * y, 384, 384)]
    has_heads = (ids[2] < KEY_AT).astype(f32)
    att_grad[...] = (nt(low[...], rows_w[...]) * has_heads).astype(bf16)
    key_grad[...] = jnp.zeros_like(key_grad)
    value_grad[...] = jnp.zeros_like(value_grad)
    for h in range(2):
        cols = slice(HEAD * h, HEAD * (h + 1))
        for i in range(4):
            n = 128 * (i + 1)
            rows = slice(128 * i, n)
            q = heads[rows, cols]
            k, v = heads[:n, 2 * HEAD : 3 * HEAD], heads[:n, 3 * HEAD :]
            o = att_grad[rows, cols]
            s = nt(q, k) * SCALE
            p = jnp.where(kept(i, n, length), jnp.exp(s - lse[rows, HEAD * h : HEAD * h + 1]), 0.0)
            d = nt(o, v)
            g = (p * (d - jnp.sum(p * d, -1, keepdims=True))).astype(bf16)
            value_grad[:n, :] += tn(p.astype(bf16), o)
            key_grad[:n, :] += tn(g, q)
            dq = nn(g, k) * SCALE
            dq = dq * cosine[rows, :] - pltpu.roll(dq, HEAD // 2, 1) * sine[rows, :]
            grads[rows, cols] = dq.astype(bf16)
    dk = key_grad[...] * SCALE
    dk = dk * cosine[...] - pltpu.roll(dk, HEAD // 2, 1) * sine[...]
    grads[:, 2 * HEAD : 3 * HEAD] = dk.astype(bf16)
    grads[:, 3 * HEAD :] = value_grad[...].astype(bf16)
    k, v = grads[:, 2 * HEAD : 3 * HEAD], grads[:, 3 * HEAD :]

    @pl.when(c == 0)
    def _():
        own_kind[...] = k
        other_kind[...] = v

    @pl.when(c != 0)
    def _():
        own_kind[...] = v
        other_kind[...] = k


def joint_back(
    ids, grads, w, tok, second_part,
    near, far, chunks, gain_part, vec, blocks,
):
    g = grads[...]
    gain_part[...] = jnp.zeros_like(gain_part)
    for r in range(0, T, 128):
        rows = slice(r, r + 128)
        back = nt(g[rows], w[...])
        half, place = r // HALF, slice(r % HALF, r % HALF + 128)
        moves = back.astype(bf16)

        @pl.when(ids[4] == half)
        def _():
            near[place, :] = moves

        @pl.when(ids[4] != half)
        def _():
            far[place, :] = moves

        x = tok[rows, :].astype(f32)
        s = lax.rsqrt(jnp.mean(x * x, -1, keepdims=True) + EPS_NORM)
        gain_part[...] += jnp.sum(back * x * s, 0, keepdims=True)
    vec[...] = jnp.zeros_like(vec)
    vec[:, :D] = gain_part[...]
    vec[:, D : 2 * D] = second_part[...]
    bias = jnp.sum(g.astype(f32), 0, keepdims=True)
    head_at = jnp.minimum(ids[2], KEY_AT - 1)
    key_start = 2 * D + JC * KEY_AT + HEAD * lax.div(head_at, 3)
    vec[:, at(2 * D + JC * head_at, JC, JC)] = bias[:, :JC]
    vec[:, at(key_start, HEAD, HEAD)] = bias[:, JC : JC + HEAD]
    vec[:, at(key_start + JC, HEAD, HEAD)] = bias[:, JC + HEAD :]
    for d in range(DP):
        blocks[d : d + 1, :] = vec[:, 320 * d : 320 * (d + 1)]
    for m in range(MP):
        piece = blocks[:, 40 * m : 40 * (m + 1)]
        piece = jnp.concatenate([piece, jnp.zeros((DP, HEAD - 40), f32)], 1)
        high = piece.astype(bf16)
        chunks[m, :DP, :] = high
        chunks[m, DP:, :] = (piece - high.astype(f32)).astype(bf16)


def back_to_input(
    ids, near_low, far_low, rows_w, heads, lse, cosine, sine, w, tok, second_part,
    grads, window, own_kind, other_kind, near, far, chunks,
    low, att_grad, key_grad, value_grad, gain_part, vec, blocks, w_held, tok_held, sems,
):
    copies = [
        pltpu.make_async_copy(w, w_held, sems.at[0]),
        pltpu.make_async_copy(tok, tok_held, sems.at[1]),
    ]
    for copy in copies:
        copy.start()
    attend_back(
        ids, near_low, far_low, rows_w, heads, lse, cosine, sine,
        grads, window, own_kind, other_kind, low, att_grad, key_grad, value_grad,
    )
    for copy in copies:
        copy.wait()
    joint_back(ids, grads, w_held, tok_held, second_part, near, far, chunks, gain_part, vec, blocks)


def group_parts(ids, own, other, o0, o1, o2, o3, both, left, right, out_sum):
    out_sum[...] = summed(o0, (o1, o2, o3))
    own_group = lax.div(jnp.minimum(ids[2], KEY_AT - 1), 3)
    partner = ids[2] + 1 - 2 * ids[4]
    other_group = lax.div(jnp.minimum(partner, KEY_AT - 1), 3)
    a, b = own[...].astype(f32), other[...].astype(f32)
    for g, out in ((0, left), (1, right)):
        part = a * (own_group == g).astype(f32) + b * (other_group == g).astype(f32)
        out[...] = part.astype(bf16)
        both[:, HEAD * g : HEAD * (g + 1)] = part.astype(bf16)


def weigh_joint(ids, normed, grads, left, right, both, moved, mixer_parts, parts):
    pair = jnp.concatenate([left[...].astype(f32), right[...].astype(f32)], 1)
    pair = pair + both[...].astype(f32)
    own = grads[:, :JC].astype(f32)
    g = jnp.where(ids[2] < KEY_AT, own, pair).astype(bf16)
    for r in range(4):
        cols = slice(384 * r, 384 * (r + 1))
        part = tn(normed[:, cols], g).astype(bf16)
        parts[4 * r : 4 * (r + 1), :ROWS, :] = part.reshape(4, ROWS, JC)
    parts[:, ROWS : ROWS + 80, :] = mixer_parts[...]
    vec = moved[0].astype(f32)
    for j in range(1, MP):
        vec += moved[j].astype(f32)
    vec = vec[:DP] + vec[DP:]
    high = vec.astype(bf16).astype(f32)
    for d in range(DP):
        parts[d, ROWS + 80 :, :HEAD] = jnp.broadcast_to(high[d : d + 1], (8, HEAD)).astype(bf16)
        low = (vec - high)[d : d + 1]
        parts[d, ROWS + 80 :, HEAD:] = jnp.broadcast_to(low, (8, HEAD)).astype(bf16)


def weigh_mixer(ids, near, far, low, packed, parts):
    c = ids[4]

    def own_columns(half):
        v = low[at(HALF * half, HALF, HALF), :].astype(f32)
        return jnp.where(c == 0, v[:, :MC], v[:, MC:]).astype(bf16)

    mine, other = own_columns(c), own_columns(1 - c)
    for j in range(KEY_AT):
        part = tn(near[j], mine) + tn(far[j], other)
        start = JC * j
        while start < JC * (j + 1):
            stop = min((start // ROWS + 1) * ROWS, JC * (j + 1))
            first = start % ROWS
            parts[start // ROWS, first : first + stop - start, :] = part[
                start - JC * j : stop - JC * j
            ]
            start = stop
    for d in range(DP):
        left, right = parts[d, :, :HEAD], parts[d, :, HEAD:]
        packed[d, :48, :HEAD] = left[:48].astype(bf16)
        packed[d, :48, HEAD:] = left[48:].astype(bf16)
        packed[d, 48:, :HEAD] = jnp.concatenate([right[:32], right[32:64]], 1).astype(bf16)
        packed[d, 48:, HEAD:] = jnp.concatenate(
            [right[64:], jnp.zeros((32, JC - MC), f32)], 1
        ).astype(bf16)


def settle_grads(ids, moved, ff, joint, mixer, vector, squares):
    total = moved[0].astype(f32)
    for d in range(1, DP):
        total += moved[d].astype(f32)
    joint[...] = total[:ROWS]
    left, right = total[ROWS : ROWS + 48], total[ROWS + 48 : ROWS + 80]
    mixer[:48, :HEAD] = left[:, :HEAD]
    mixer[48:, :HEAD] = left[:, HEAD:]
    mixer[:32, HEAD:] = right[:, : MC - HEAD]
    mixer[32:64, HEAD:] = right[:, MC - HEAD : HEAD]
    mixer[64:, HEAD:] = right[:, HEAD:MC]
    vec = total[ROWS + 80 : ROWS + 81, :HEAD] + total[ROWS + 80 : ROWS + 81, HEAD:]
    vector[...] = vec
    total = total[: ROWS + 80]
    total = jnp.sum(total * total) + jnp.sum(vec * vec)
    for m in range(3):
        v = ff[m].astype(f32)
        total += jnp.sum(v * v)
    squares[...] = jnp.full(squares.shape, total, f32)


def update(
    squares, joint_grad, mixer_grad, ff_grad, vector_grad,
    joint_w, joint_m, joint_v, mixer_w, mixer_m, mixer_v, expand_w, expand_m, expand_v,
    shrink_w, shrink_m, shrink_v, vector_w, vector_m, vector_v,
    norm_out, joint_wn, joint_mn, joint_vn, mixer_wn, mixer_mn, mixer_vn,
    expand_wn, expand_mn, expand_vn, shrink_wn, shrink_mn, shrink_vn,
    vector_wn, vector_mn, vector_vn,
):
    norm = jnp.sqrt(jnp.sum(squares[:, 0, :], 0, keepdims=True))
    norm_out[...] = norm
    clip = jnp.minimum(1.0, MAX_NORM / (norm[:, :1] + 1e-06))

    def step(grad, before, after, rate, decay, part=Ellipsis):
        w, m, v = [ref[part] for ref in before]
        results = adam_step(w, clip * grad, m, v, rate, decay)
        for ref, new in zip(after, results):
            ref[part] = new

    step(
        joint_grad[...], (joint_w, joint_m, joint_v), (joint_wn, joint_mn, joint_vn),
        RATE_MATRIX, DECAY,
    )
    step(
        mixer_grad[...], (mixer_w, mixer_m, mixer_v), (mixer_wn, mixer_mn, mixer_vn),
        RATE_MATRIX, DECAY,
    )
    for m in range(2):
        step(
            ff_grad[m, :, :FF].astype(f32),
            (expand_w, expand_m, expand_v), (expand_wn, expand_mn, expand_vn),
            RATE_MATRIX, DECAY, m,
        )
    step(
        ff_grad[2, :, :FF].astype(f32),
        (shrink_w, shrink_m, shrink_v), (shrink_wn, shrink_mn, shrink_vn),
        RATE_MATRIX, DECAY,
    )
    step(
        vector_grad[:, :40], (vector_w, vector_m, vector_v), (vector_wn, vector_mn, vector_vn),
        RATE_VECTOR, 0.0,
    )


def write_half(ids, half, pieces, outs, rows, sems):
    for k, e in enumerate(RELATIVE):
        place = at(PART * lax.rem(ids[3] + e + 4, 4), PART, PART)
        for n in range(2):
            rows[n, place, :] = pieces[k][n].astype(f32)
    copies = [
        pltpu.make_async_copy(rows.at[n], out.at[0, at(HALF * half, HALF, HALF)], sems.at[n])
        for n, out in enumerate(outs)
    ]
    for copy in copies:
        copy.start()
    for copy in copies:
        copy.wait()


def settle_near(ids, p0, p1, p2, p3, output, input_grad, token, rows, sems):
    token[...] = jnp.zeros_like(token)
    write_half(ids, ids[4], (p0, p1, p2, p3), (output, input_grad), rows, sems)


def settle_far(ids, far, _a, _b, output, input_grad, rows, sems):
    pieces = [far.at[k] for k in range(4)]
    write_half(ids, 1 - ids[4], pieces, (output, input_grad), rows, sems)


def pile(ids, p0, p1, p2, p3, out):
    for k, p in enumerate((p0, p1, p2, p3)):
        out[k] = p[...]


def norm_back(v, scale, gain, grad):
    scaled = gain * grad
    return scale * scaled - v * scale * scale * scale * jnp.mean(scaled * v, -1, keepdims=True)


def adam_step(weight, grad, moment, square, rate, decay):
    moment_next = BETA_ONE * moment + (1.0 - BETA_ONE) * grad
    square_next = BETA_TWO * square + (1.0 - BETA_TWO) * grad * grad
    first_hat = moment_next * (1.0 / (1.0 - BETA_ONE**STEP))
    second_hat = square_next * (1.0 / (1.0 - BETA_TWO**STEP))
    weight_next = weight - rate * (first_hat / (jnp.sqrt(second_hat) + ADAM_EPS) + decay * weight)
    return (weight_next, moment_next, square_next)


def tables():
    freq = np.float32(ROPE_BASE) ** (-np.arange(0, HEAD, 2, dtype=np.float32) / np.float32(HEAD))
    angle = np.arange(T, dtype=np.float32)[:, None] * freq.astype(np.float32)[None, :]
    cosine, sine = np.cos(angle), np.sin(angle)
    return (
        np.concatenate([cosine, cosine], -1).astype(np.float32),
        np.concatenate([-sine, sine], -1).astype(np.float32),
    )


def split_low(v):
    high = lax.reduce_precision(v, 8, 7)
    middle = lax.reduce_precision(v - high, 8, 7)
    return [part.astype(bf16) for part in (high, middle, v - high - middle)]


def body(
    tokens, lengths, cotangent,
    joint_weight, joint_moment, joint_square,
    mixer_weight, mixer_moment, mixer_square,
    expand_weight, expand_moment, expand_square,
    shrink_weight, shrink_moment, shrink_square,
    vector_params, vector_moment, vector_square,
):
    dp, mp = lax.axis_index("dp"), lax.axis_index("mp")
    y, c = mp // 2, mp % 2
    tok, length = tokens[0], lengths[0]
    ids = jnp.stack([length, dp, mp, y, c]).astype(jnp.int32)

    stack = jnp.concatenate(
        [expand_weight.astype(bf16), shrink_weight.T.astype(bf16)[None]], 0
    )
    stack = jnp.pad(stack, ((0, 0), (0, 0), (0, FP - FF)))
    ff = lax.all_gather(stack, "dp", axis=0, tiled=False)

    low = jnp.concatenate([joint_weight.astype(bf16), mixer_weight.astype(bf16)], 1)
    vec = jnp.pad(jnp.stack(split_low(vector_params)), ((0, 13), (0, JC + MC - 40)))
    low = jnp.concatenate([low, vec], 0)
    other = swap_core(low)
    first, second = jnp.where(c == 0, low, other), jnp.where(c == 0, other, low)
    pairs = [
        jnp.concatenate([first[:ROWS, cols], second[:ROWS, cols]], 1)
        for cols in (slice(0, HEAD), slice(HEAD, JC))
    ]
    chip = jnp.concatenate([first[:ROWS, JC:], second[:ROWS, JC:]], 1)
    chip = lax.dynamic_slice_in_dim(chip, 48 * c, 48, 0)
    rest = jnp.concatenate([chip[:32, JC:], jnp.pad(chip[32:, JC:], ((0, 16), (0, 0)))], 1)
    sent = jnp.concatenate([low[:ROWS, :JC], chip[:, :JC], rest], 0)
    query_w = exchange(jnp.broadcast_to(sent, (DP,) + sent.shape), "dp")
    vec = jnp.concatenate([first[ROWS:, :HEAD], second[ROWS:, :HEAD]], 1)
    sends = [pairs[0], pairs[1], jnp.where(c == 0, pairs[0], pairs[1])]
    sends = [jnp.concatenate([v, vec], 0) for v in sends]
    a1, a2, a3 = [shift_y(v, k) for v, k in zip(sends, (1, -1, 2))]
    pair = jnp.where(y == 0, a1[:ROWS], jnp.where(y == 2, a2[:ROWS], a3[:ROWS]))
    vec = jnp.stack([vec, a2[ROWS:], a3[ROWS:], a1[ROWS:]])[:, :3]
    vec = lax.dynamic_slice_in_dim(jnp.concatenate([vec, vec]), (4 - y) % 4, 4, 0)
    sent = jnp.concatenate([pair, vec.reshape(12, JC), query_w[0, :4]], 0)
    pair_w = exchange(jnp.broadcast_to(sent, (DP,) + sent.shape), "dp")
    cosine, sine = tables()
    back, back_t, back_part, tok_part, tok_half = whole(
        prepare,
        [
            ((T, D), bf16), ((D, T), bf16),
            ((PART, D), bf16), ((PART, D), bf16), ((HALF, D), bf16),
        ],
        [ids, cotangent[0], tok],
    )
    normed, heads, att_sent, lse, joint_w, vec = whole(
        attend,
        [
            ((T, D), bf16), ((T, 2 * JC), bf16), ((MP, HALF, JC), bf16),
            ((T, JC), f32), ((D, 2 * JC), bf16), ((1, VEC), f32),
        ],
        [ids, tok, cosine, sine, query_w, pair_w],
        after=[back],
    )
    gain_first, gain_second = vec[:, :D], vec[:, D : 2 * D]
    att_near = exchange(att_sent, "mp")
    att_far = swap_core(att_near)
    mixer_near = gather(shift_y, query_w[:, ROWS:])
    mixer_far = [swap_core(v) for v in mixer_near]
    mixer, rows_w = whole(
        assemble, [((D, D), bf16), ((JC, D), bf16)], [ids] + mixer_near + mixer_far
    )

    def fixed(shape):
        return pl.BlockSpec(shape, lambda i: (0,) * len(shape))

    hidden_part, normed_near = pl.pallas_call(
        mix,
        grid=(4,),
        out_shape=[jax.ShapeDtypeStruct((PART, D), f32), jax.ShapeDtypeStruct((HALF, D), bf16)],
        in_specs=[
            SM,
            fixed((MP, HALF, JC)),
            pl.BlockSpec((D, 384), lambda i: (0, i)),
            pl.BlockSpec((HALF, 384), lambda i: (0, i)),
            fixed((1, VEC)),
        ],
        out_specs=[fixed((PART, D)), fixed((HALF, D))],
        scratch_shapes=[pltpu.VMEM((HALF, D), f32), pltpu.VMEM((HALF, D), bf16)],
        compiler_params=pltpu.CompilerParams(vmem_limit_bytes=60 * MiB),
        cost_estimate=SMALL,
    )(ids, att_near, mixer, tok_half, vec)
    normed_far = swap_core(normed_near)

    def columns(n):
        return pl.BlockSpec((n, 256), lambda i: (0, i))

    block = pl.BlockSpec((DP, 3, ROWS, 256), lambda i: (0, 0, 0, i))
    act, gate_grad, up_grad, ff_grads = pl.pallas_call(
        gated,
        grid=(pl.cdiv(FP, 256),),
        out_shape=[jax.ShapeDtypeStruct((T, FP), bf16)] * 3
        + [jax.ShapeDtypeStruct((DP, 3, ROWS, FP), bf16)],
        in_specs=[fixed((HALF, D)), fixed((HALF, D)), fixed((T, D)), fixed((D, T)), block],
        out_specs=[columns(T)] * 3 + [block],
        scratch_shapes=[pltpu.VMEM((D, T), bf16)],
        compiler_params=pltpu.CompilerParams(vmem_limit_bytes=60 * MiB),
        cost_estimate=SMALL,
    )(normed_near, normed_far, back, back_t, ff)
    ff_shard = lax.psum_scatter(ff_grads, "dp", scatter_dimension=0, tiled=False)

    near, far = pl.pallas_call(
        spread,
        grid=(2,),
        out_shape=[jax.ShapeDtypeStruct((HALF, D), bf16)] * 2,
        in_specs=[fixed((T, FP))] * 2
        + [pl.BlockSpec((DP // 2, 2, ROWS, FP), lambda i: (i, 0, 0, 0))],
        out_specs=[pl.BlockSpec((HALF, 768), lambda i: (0, i))] * 2,
        compiler_params=pltpu.CompilerParams(vmem_limit_bytes=60 * MiB),
        cost_estimate=SMALL,
    )(gate_grad, up_grad, ff)

    def half_sum(near, far, after=()):
        own, *parts = whole(
            halve,
            [((PART, D), f32)] + [((PART, D), bf16)] * 3,
            [ids, near, swap_core(far)],
            after=after,
            limit=8,
        )
        return [own, shift_y(parts[2], 2), shift_y(parts[0], 1), shift_y(parts[1], -1)]

    normed_second_parts = half_sum(near, far)
    out_near, out_far = pl.pallas_call(
        spread_out,
        grid=(2,),
        out_shape=[jax.ShapeDtypeStruct((HALF, D), bf16)] * 2,
        in_specs=[
            fixed((T, FP)),
            pl.BlockSpec((DP // 2, 1, ROWS, FP), lambda i: (i, 2, 0, 0)),
        ],
        out_specs=[pl.BlockSpec((HALF, 768), lambda i: (0, i))] * 2,
        compiler_params=pltpu.CompilerParams(vmem_limit_bytes=60 * MiB),
        cost_estimate=SMALL,
    )(act, ff)
    hidden_grad, low, gain_second_part = whole(
        hidden_back,
        [((PART, D), f32), ((PART, D), bf16), ((1, D), f32)],
        [ids] + normed_second_parts + [hidden_part, back_part, gain_second],
        after=[out_far],
        limit=8,
    )
    out_parts = half_sum(out_near, out_far)
    low_near = jnp.stack(gather(shift_y, low))
    low_far = swap_core(low_near)
    heads_grad, hidden_low, own_kind, other_kind, input_near, input_far, chunks = whole(
        back_to_input,
        [
            ((T, 2 * JC), bf16), ((T, 2 * MC), bf16), ((T, HEAD), bf16), ((T, HEAD), bf16),
            ((HALF, D), bf16), ((HALF, D), bf16), ((MP, 2 * DP, HEAD), bf16),
        ],
        [ids, low_near, low_far, rows_w, heads, lse, cosine, sine, joint_w, tok, gain_second_part],
        scratch=[
            pltpu.VMEM((T, D), bf16),
            pltpu.VMEM((T, JC), bf16),
            pltpu.VMEM((T, HEAD), f32),
            pltpu.VMEM((T, HEAD), f32),
            pltpu.VMEM((1, D), f32),
            pltpu.VMEM((1, DP * MP * 40), f32),
            pltpu.VMEM((DP, MP * 40), f32),
            pltpu.VMEM((D, 2 * JC), bf16),
            pltpu.VMEM((T, D), bf16),
            pltpu.SemaphoreType.DMA((2,)),
        ],
        after=[out_parts[0]],
        loose=(8, 9),
    )
    both, left, right, out_sum = whole(
        group_parts,
        [((T, JC), bf16), ((T, HEAD), bf16), ((T, HEAD), bf16), ((PART, D), f32)],
        [ids, own_kind, swap_core(other_kind)] + out_parts,
        limit=8,
    )
    left, right, both = to_last_chip(left, 0), to_last_chip(right, 2), to_last_chip(both, 1)
    moved = exchange(chunks, "mp")
    (mixer_parts,) = whole(
        weigh_mixer,
        [((DP, 80, JC), bf16)],
        [ids, att_near, att_far, hidden_low],
        scratch=[pltpu.VMEM((DP, ROWS, MC), f32)],
        after=[out_sum],
    )
    (joint_parts,) = whole(
        weigh_joint,
        [((DP, ROWS + 88, JC), bf16)],
        [ids, normed, heads_grad, left, right, both, moved, mixer_parts],
    )
    joint_shard, mixer_shard, vector_shard, squares = whole(
        settle_grads,
        [((ROWS, JC), f32), ((ROWS, MC), f32), ((1, HEAD), f32), ((DP * MP, 1, HEAD), f32)],
        [ids, exchange(joint_parts, "dp"), ff_shard],
    )

    squares = exchange(squares, ("dp", "mp"))

    parts = half_sum(input_near, input_far, after=[joint_parts])
    (done,) = whole(
        finish,
        [((2, PART, D), bf16)],
        [ids, out_sum] + parts + [hidden_part, tok_part, hidden_grad, gain_first],
        limit=8,
    )
    done_parts = gather(shift_y, done)
    anywhere = pl.BlockSpec(memory_space=pl.ANY)
    results = [jax.ShapeDtypeStruct((1, T, D), f32)] * 2
    held = [pltpu.VMEM((2, HALF, D), f32), pltpu.SemaphoreType.DMA((2,))]
    *halves, token = pl.pallas_call(
        settle_near,
        out_shape=results + [jax.ShapeDtypeStruct((8, HEAD), f32)],
        in_specs=[SM] + [VM] * 4,
        out_specs=[anywhere] * 2 + [VM],
        scratch_shapes=held,
        compiler_params=pltpu.CompilerParams(vmem_limit_bytes=16 * MiB),
        cost_estimate=SMALL,
    )(ids, *done_parts)
    (done_near,) = whole(
        pile, [((4, 2, PART, D), bf16)], [ids] + done_parts, after=[squares, token], limit=8
    )
    output, input_grad = pl.pallas_call(
        settle_far,
        out_shape=results,
        in_specs=[SM, VM] + [anywhere] * 2,
        out_specs=[anywhere] * 2,
        input_output_aliases={2: 0, 3: 1},
        scratch_shapes=held,
        compiler_params=pltpu.CompilerParams(vmem_limit_bytes=16 * MiB),
        cost_estimate=SMALL,
    )(ids, swap_core(done_near), *halves)

    matrices = [joint_weight, joint_moment, joint_square]
    matrices += [mixer_weight, mixer_moment, mixer_square]
    matrices += [expand_weight, expand_moment, expand_square]
    matrices += [v.T for v in (shrink_weight, shrink_moment, shrink_square)]
    matrices += [v[None] for v in (vector_params, vector_moment, vector_square)]
    def third(shape):
        n = len(shape)
        if shape[-2] != ROWS:
            return pl.BlockSpec(shape, lambda i: (0,) * n)
        return pl.BlockSpec(
            shape[:-2] + (ROWS // 3, shape[-1]), lambda i: (0,) * (n - 2) + (i, 0)
        )

    given = [squares, joint_shard, mixer_shard, ff_shard, vector_shard] + matrices
    made = [(1, HEAD)] + [v.shape for v in matrices]
    norm, *new = pl.pallas_call(
        update,
        grid=(3,),
        out_shape=[jax.ShapeDtypeStruct(shape, f32) for shape in made],
        in_specs=[third(v.shape) for v in given],
        out_specs=[third(shape) for shape in made],
        compiler_params=pltpu.CompilerParams(vmem_limit_bytes=60 * MiB),
        cost_estimate=SMALL,
    )(*given)
    new[9:12] = [v.T for v in new[9:12]]
    new[12:] = [v[0] for v in new[12:]]
    return (output, input_grad, norm[0, 0], *new)


def solution(mesh):
    row = P("dp", None, None)
    matrix = [P("dp", "mp")] * 6 + [P(None, "dp", "mp")] * 3 + [P("mp", "dp")] * 3
    vector = [P(("dp", "mp"))] * 3
    return jax.shard_map(
        body,
        mesh=mesh,
        in_specs=tuple([row, P("dp"), row] + matrix + vector),
        out_specs=tuple([row, row, P()] + matrix + vector),
        check_vma=False,
    )
```
